32 devices in a mesh: blk: 4 (over x, core), batch: 8 (over z, y).
Axes of the slice: x: 2, y: 2, z: 4, core: 2. Of those that a mesh axis runs over, the one named last changes fastest.
Arguments:
- incoming_activation: bfloat16 [16, 1024, 768], P('batch', 'blk'), may hold values from -6 to 6
- first_norm_scale_vector: float32 [768], replicated, may hold values from 0.25 to 1.75
- triple_lookup_factors: bfloat16 [768, 2304], replicated, may hold values from -0.21875 to 0.21875
- attend_exit_factors: bfloat16 [768, 768], replicated, may hold values from -1.25 to 1.25
- second_norm_scale_vector: float32 [768], replicated, may hold values from 0.25 to 1.75
- dispatcher_coefficients: bfloat16 [768, 4], replicated, may hold values from -0.15625 to 0.15625
- specialist_entry_factors: bfloat16 [8, 768, 1536], P('batch', None, 'blk'), may hold values from -0.21875 to 0.21875
- specialist_exit_factors: bfloat16 [8, 1536, 768], P('batch', 'blk'), may hold values from -0.21875 to 0.21875
- chosen_specialist: int32 [16, 1024], P('batch', 'blk'), may hold values from 0 to 3, as said below
- specialist_quota: int32 [4], replicated, may hold values from 6 to 12
- training_period: int32 [16], P('batch'), may hold values from 1 to 2, as said below
- loss_sensitivity: bfloat16 [16, 1024, 768], P('batch', 'blk'), may hold values from -6 to 6
Outputs:
- output: bfloat16 [16, 1024, 768], P('batch', 'blk')
- input_grad: bfloat16 [16, 1024, 768], P('batch', 'blk')
- attn_gain_grad: float32 [768], replicated
- qkv_weight_grad: float32 [768, 2304], replicated
- proj_weight_grad: float32 [768, 768], replicated
- moe_gain_grad: float32 [768], replicated
- router_weight_grad: float32 [768, 4], replicated
- expert_in_grad: float32 [8, 768, 1536], P('batch', None, 'blk')
- expert_out_grad: float32 [8, 1536, 768], P('batch', 'blk')
The draws below stay inside these ranges and needn't reach their ends.
Inputs may be any that keep to these rules, and one draw needn't show every extreme that they name: `chosen_specialist`: within the rows of every device some expert whose capacity is 12 is named 12 times or more. `training_period`: some sequence has section 1 and some has section 2.
All inputs are finite; a program needn't handle non-finite values.
Results may differ from the reference program's by a relative error of at most 0.02.
Values may be sent and summed in bfloat16 or wider, within the bound.
No kernel may reach another device: no remote copies, remote signals or barrier semaphores. Data moves between devices by JAX's collectives and lax.ppermute only.
A program may use at most 192 MiB of HBM per device.

```python
import jax
import jax.numpy as jnp
from jax import lax

D = 768
HEADS = 12
HEAD_DIM = 64
FF = 3072
SPAN = 256
SEQ_DEV = 2
CAP = 12
EXP_SPLIT = 2
LEN = 1024
SEQS = 16
EXPERTS = 4
N_BLK = 4
N_BATCH = 8


def hot_order(key):
    return jax.random.permutation(key, EXPERTS)


def draw_chosen_specialist(key, part):
    expert_order = hot_order(key)
    key = jax.random.fold_in(key, 11)
    first_key, second_key, third_key, fourth_key = jax.random.split(key, 4)
    block_shape = (N_BATCH, N_BLK, SEQ_DEV * SPAN)
    picks = jnp.minimum(jax.random.randint(first_key, block_shape, 0, EXPERTS), jax.random.randint(second_key, block_shape, 0, EXPERTS))
    picks = jnp.minimum(picks, jax.random.randint(third_key, block_shape, 0, EXPERTS))
    chosen = expert_order[picks]
    ordering = jax.random.randint(fourth_key, block_shape, 0, 1 << 20) * (SEQ_DEV * SPAN) + jnp.arange(SEQ_DEV * SPAN, dtype=jnp.int32)
    placing = jnp.argsort(jnp.argsort(ordering, axis=-1), axis=-1)
    chosen = jnp.where(placing < CAP, expert_order[0], chosen)
    chosen = jnp.swapaxes(chosen.reshape(N_BATCH, N_BLK, SEQ_DEV, SPAN), 1, 2).reshape(SEQS, LEN)
    return chosen.astype(jnp.int32)


def draw_specialist_quota(key, part):
    expert_order = hot_order(key)
    key = jax.random.fold_in(key, 23)
    drawn = jax.random.randint(key, (EXPERTS,), CAP - CAP // 2, CAP + 1)
    return jnp.where(jnp.arange(EXPERTS) == expert_order[0], CAP, drawn).astype(jnp.int32)


def draw_training_period(key, part):
    key = jax.random.fold_in(key, 37)
    first_key, second_key = jax.random.split(key)
    sections = jax.random.randint(first_key, (SEQS,), 1, 3)
    order = jax.random.permutation(second_key, SEQS)
    sections = sections.at[order[0]].set(1)
    sections = sections.at[order[1]].set(2)
    return sections.astype(jnp.int32)


def steps_of(stream_key, shape, pieces, least, top_value):
    gain, own = 1.0, jax.random.fold_in(stream_key, 6)
    for axis_at, blocks in pieces:
        heights = jnp.exp(jax.random.uniform(jax.random.fold_in(own, axis_at), (blocks,), jnp.float32, least / len(pieces), top_value / len(pieces)))
        gain = gain * jnp.repeat(heights, shape[axis_at] // blocks).reshape([-1 if axis == axis_at else 1 for axis in range(len(shape))])
    return gain


def scatter_about(stream_key, extent, width, most, cuts=(), kind=jnp.bfloat16):
    result = width * jax.random.normal(stream_key, extent, jnp.float32)
    if cuts:
        result = result * steps_of(stream_key, extent, cuts, -0.22, 0.18)
    return jnp.clip(result, -most, most).astype(kind)


def setup_inputs(seed: int = 0) -> dict:
    key_of = jax.random.split(jax.random.key(seed), 13)
    incoming_activation = scatter_about(key_of[0], (SEQS, LEN, D), 1.0, 6.0, ((0, 8), (1, 4)))
    first_norm_scale_vector = jnp.clip(1.0 + 0.15 * jax.random.normal(key_of[1], (D,), jnp.float32), 0.25, 1.75)
    triple_lookup_factors = scatter_about(key_of[2], (D, 3 * D), D ** -0.5, 0.21875)
    attend_exit_factors = scatter_about(key_of[3], (D, D), (D // 32) ** -0.5, 1.25)
    second_norm_scale_vector = jnp.clip(1.0 + 0.15 * jax.random.normal(key_of[4], (D,), jnp.float32), 0.25, 1.75)
    dispatcher_coefficients = scatter_about(key_of[5], (D, EXPERTS), (2 * D) ** -0.5, 0.15625)
    specialist_entry_factors = scatter_about(key_of[6], (EXPERTS * EXP_SPLIT, D, FF // EXP_SPLIT), D ** -0.5, 0.21875, ((0, 8), (2, 4)))
    specialist_exit_factors = scatter_about(key_of[7], (EXPERTS * EXP_SPLIT, FF // EXP_SPLIT, D), (FF // 4) ** -0.5, 0.21875, ((0, 8), (1, 4)))
    chosen_specialist = draw_chosen_specialist(jax.random.fold_in(key_of[12], 71), 0)
    specialist_quota = draw_specialist_quota(jax.random.fold_in(key_of[12], 71), 0)
    training_period = draw_training_period(jax.random.fold_in(key_of[12], 71), 0)
    loss_sensitivity = scatter_about(key_of[11], (SEQS, LEN, D), 1.0, 6.0, ((0, 8), (1, 4)))
    return {"incoming_activation": incoming_activation, "first_norm_scale_vector": first_norm_scale_vector, "triple_lookup_factors": triple_lookup_factors, "attend_exit_factors": attend_exit_factors, "second_norm_scale_vector": second_norm_scale_vector, "dispatcher_coefficients": dispatcher_coefficients, "specialist_entry_factors": specialist_entry_factors, "specialist_exit_factors": specialist_exit_factors, "chosen_specialist": chosen_specialist, "specialist_quota": specialist_quota, "training_period": training_period, "loss_sensitivity": loss_sensitivity}


@jax.custom_vjp
def low(v):
    return lax.optimization_barrier(v.astype(jnp.bfloat16)).astype(jnp.float32)

@jax.custom_vjp
def low_back(v):
    return v

def low_keep(v):
    return (low(v), None)

def low_pass(kept, grad):
    return (grad,)

def back_keep(v):
    return (v, None)

def back_low(kept, grad):
    return (low(grad),)
low.defvjp(low_keep, low_pass)
low_back.defvjp(back_keep, back_low)
epsilon = 1e-05
far_below = -1e+30

def product(left_side, right_side):
    return jnp.dot(left_side, right_side, precision=lax.Precision.HIGHEST, preferred_element_type=jnp.float32)

def layer_norm(token_rows, norm_gain):
    centred = token_rows - lax.optimization_barrier(jnp.mean(token_rows, axis=-1, keepdims=True))
    return centred * lax.rsqrt(lax.optimization_barrier(jnp.mean(centred * centred, axis=-1, keepdims=True)) + epsilon) * norm_gain

def attend_sequence(qkv_block):
    queries = qkv_block[:, :D].reshape(LEN, HEADS, HEAD_DIM)
    key_rows = qkv_block[:, D:2 * D].reshape(LEN, HEADS, HEAD_DIM)
    values = qkv_block[:, 2 * D:].reshape(LEN, HEADS, HEAD_DIM)
    scores = low_back(HEAD_DIM ** (-0.5) * jnp.einsum('qhd,khd->hqk', queries, key_rows, precision=lax.Precision.HIGHEST))
    allowed = jnp.arange(LEN)[None, :] <= jnp.arange(LEN)[:, None]
    masked = jnp.where(allowed, scores, far_below)
    row_max = lax.optimization_barrier(jnp.max(masked, axis=-1, keepdims=True))
    raised = jnp.where(allowed, jnp.exp(masked - row_max), 0.0)
    attention = raised / lax.optimization_barrier(jnp.sum(raised, axis=-1, keepdims=True))
    mixed = jnp.einsum('hqk,khd->qhd', low(attention), values, precision=lax.Precision.HIGHEST)
    return mixed.reshape(LEN, D)

def expert_block(expert_args):
    slot_rows, block_in, block_out = expert_args
    weight_in = jnp.transpose(block_in, (1, 0, 2)).reshape(D, FF)
    weight_out = block_out.reshape(FF, D)
    hidden = low_back(product(slot_rows, weight_in))
    active = low(jax.nn.gelu(hidden, approximate=False))
    return product(active, weight_out)

def to_devices(whole_array):
    array_shape = whole_array.shape
    unfolded = whole_array.reshape((N_BATCH, SEQ_DEV, N_BLK, SPAN) + array_shape[2:])
    moved = jnp.swapaxes(unfolded, 1, 2)
    return moved.reshape((N_BATCH, N_BLK, SEQ_DEV * SPAN) + array_shape[2:])

def from_devices(whole_array):
    array_shape = whole_array.shape
    unfolded = whole_array.reshape((N_BATCH, N_BLK, SEQ_DEV, SPAN) + array_shape[3:])
    return jnp.swapaxes(unfolded, 1, 2).reshape((SEQS, LEN) + array_shape[3:])

def seat_arrangement_map(chosen_specialist, specialist_quota):
    assignments_each_shard = to_devices(chosen_specialist)
    is_routed = (assignments_each_shard[..., None] == jnp.arange(EXPERTS, dtype=jnp.int32)).astype(jnp.int32)
    before = jnp.cumsum(is_routed, axis=2) - is_routed
    element_precedence = lax.optimization_barrier(jnp.sum(before * is_routed, axis=-1))
    surviving_entries = element_precedence < specialist_quota[assignments_each_shard]
    seat_ordinal_number = jnp.where(surviving_entries, assignments_each_shard * CAP + element_precedence, EXPERTS * CAP)
    return seat_ordinal_number.astype(jnp.int32)

def place_rows(device_rows, device_slot):
    empty = jnp.zeros((EXPERTS * CAP + 1, D), device_rows.dtype)
    return empty.at[device_slot].set(device_rows)[:EXPERTS * CAP]

def fetch_rows(slot_box, slot_of):
    return slot_box[slot_of]

def forward(incoming_activation, first_norm_scale_vector, triple_lookup_factors, attend_exit_factors, second_norm_scale_vector, dispatcher_coefficients, specialist_entry_factors, specialist_exit_factors, seat_ordinal_number, chosen_specialist, router_live, frozen):
    token_rows = incoming_activation.reshape(SEQS * LEN, D)
    attn_in = low(layer_norm(token_rows, first_norm_scale_vector))
    qkv_rows = low_back(low(product(attn_in, triple_lookup_factors)))
    mixed = lax.map(jax.checkpoint(attend_sequence), qkv_rows.reshape(SEQS, LEN, 3 * D))
    attn_vec = low_back(low(mixed.reshape(SEQS * LEN, D)))
    after_attn = token_rows + low_back(product(attn_vec, attend_exit_factors))
    moe_in = low(layer_norm(after_attn, second_norm_scale_vector))
    logits = low_back(product(moe_in, dispatcher_coefficients))
    is_routed = chosen_specialist.reshape(SEQS * LEN)[:, None] == jnp.arange(EXPERTS, dtype=jnp.int32)[None, :]
    chosen = lax.optimization_barrier(jnp.sum(jnp.where(is_routed, logits, 0.0), axis=-1))
    gate_value = jax.nn.sigmoid(router_live * chosen + (1.0 - router_live) * frozen)
    dispatched = to_devices(low_back(moe_in).reshape(SEQS, LEN, D))
    slot_boxes = jax.vmap(jax.vmap(place_rows))(dispatched, seat_ordinal_number)
    grouped = jnp.transpose(slot_boxes.reshape(N_BATCH, N_BLK, EXPERTS, CAP, D), (2, 0, 1, 3, 4)).reshape(EXPERTS, N_BATCH * N_BLK * CAP, D)
    blocks_in = specialist_entry_factors.reshape(EXPERTS, EXP_SPLIT, D, FF // EXP_SPLIT)
    blocks_out = specialist_exit_factors.reshape(EXPERTS, EXP_SPLIT, FF // EXP_SPLIT, D)
    results = low_back(low(lax.map(jax.checkpoint(expert_block), (grouped, blocks_in, blocks_out))))
    returned = jnp.transpose(results.reshape(EXPERTS, N_BATCH, N_BLK, CAP, D), (1, 2, 0, 3, 4)).reshape(N_BATCH, N_BLK, EXPERTS * CAP, D)
    padded = jnp.concatenate([returned, jnp.zeros((N_BATCH, N_BLK, 1, D), returned.dtype)], axis=2)
    fetched = jax.vmap(jax.vmap(fetch_rows))(padded, seat_ordinal_number)
    expert_val = from_devices(fetched).reshape(SEQS * LEN, D)
    output = after_attn + gate_value[:, None] * expert_val
    return (output.reshape(SEQS, LEN, D), chosen)

def reference(incoming_activation, first_norm_scale_vector, triple_lookup_factors, attend_exit_factors, second_norm_scale_vector, dispatcher_coefficients, specialist_entry_factors, specialist_exit_factors, chosen_specialist, specialist_quota, training_period, loss_sensitivity):
    seat_ordinal_number = seat_arrangement_map(chosen_specialist, specialist_quota)
    router_live = jnp.repeat((training_period == 1).astype(jnp.float32), LEN)
    as_floats = (incoming_activation.astype(jnp.float32), first_norm_scale_vector, triple_lookup_factors.astype(jnp.float32), attend_exit_factors.astype(jnp.float32), second_norm_scale_vector, dispatcher_coefficients.astype(jnp.float32), specialist_entry_factors.astype(jnp.float32), specialist_exit_factors.astype(jnp.float32))
    first_pass = forward(*as_floats, seat_ordinal_number, chosen_specialist, jnp.ones((SEQS * LEN,), jnp.float32), jnp.zeros((SEQS * LEN,), jnp.float32))
    frozen = first_pass[1]

    def whole_block(*params):
        return forward(*params, seat_ordinal_number, chosen_specialist, router_live, frozen)
    primal, pullback = jax.vjp(whole_block, *as_floats)
    gradients = pullback((loss_sensitivity.astype(jnp.float32), jnp.zeros_like(frozen)))
    return (primal[0].astype(jnp.bfloat16), gradients[0].astype(jnp.bfloat16), gradients[1], gradients[2], gradients[3], gradients[4], gradients[5], gradients[6], gradients[7])
```

```python
import functools

import jax
import jax.numpy as jnp
from jax import lax
from jax.experimental import pallas as pl
from jax.experimental.pallas import tpu as pltpu
from jax.sharding import PartitionSpec as P

HEAD_DIM = 64
CAP = 12
SEAT = 16
LANES = 128
EPSILON = 1e-05
FAR_BELOW = -1e30
BF = jnp.bfloat16
F32 = jnp.float32


def dot(left, right):
    return jnp.dot(left, right, preferred_element_type=F32)


def dot_rows(left, right):
    return lax.dot_general(left, right, (((0,), (0,)), ((), ())), preferred_element_type=F32)


def dot_cols(left, right):
    return lax.dot_general(left, right, (((1,), (1,)), ((), ())), preferred_element_type=F32)


def norm_parts(rows):
    centred = rows - jnp.mean(rows, axis=-1, keepdims=True)
    scaling = lax.rsqrt(jnp.mean(centred * centred, axis=-1, keepdims=True) + EPSILON)
    return centred * scaling, scaling


def norm_pull(scaled, unit, scaling):
    return scaling * (
        scaled
        - jnp.mean(scaled, axis=-1, keepdims=True)
        - unit * jnp.mean(scaled * unit, axis=-1, keepdims=True)
    )


def run_kernel(body, scalars, operands, outs, scratch=(), flops=0, name=None):
    specs, arrays = [], []
    for operand in operands:
        if isinstance(operand, tuple):
            array, block, index = operand
            specs.append(pl.BlockSpec(block, functools.partial(lambda i, s, fn: fn(s), fn=index)))
        else:
            array = operand
            specs.append(pl.BlockSpec(array.shape, functools.partial(lambda i, s, n: (0,) * n, n=array.ndim)))
        arrays.append(array)
    out_specs = [
        pl.BlockSpec(out.shape, functools.partial(lambda i, s, n: (0,) * n, n=len(out.shape))) for out in outs
    ]
    moved = sum(a.size * a.dtype.itemsize for a in arrays) + sum(
        o.size * jnp.dtype(o.dtype).itemsize for o in outs
    )
    return pl.pallas_call(
        body,
        grid_spec=pltpu.PrefetchScalarGridSpec(
            num_scalar_prefetch=1,
            grid=(1,),
            in_specs=specs,
            out_specs=out_specs,
            scratch_shapes=list(scratch),
        ),
        out_shape=list(outs),
        compiler_params=pltpu.CompilerParams(vmem_limit_bytes=56 * 1024 * 1024),
        cost_estimate=pl.CostEstimate(flops=int(flops), bytes_accessed=int(moved), transcendentals=0),
        name=name,
    )(scalars, *arrays)


def shape_of(dims, dtype):
    return jax.ShapeDtypeStruct(dims, dtype)


def half_masks(span, scale):
    lane = lax.broadcasted_iota(jnp.int32, (span, LANES), 1)
    low = lane < HEAD_DIM
    first = jnp.where(low, F32(scale), F32(0.0))
    second = jnp.where(low, F32(0.0), F32(scale))
    return lane, low, (first, second)


def forward_body(
    sc, m0, m1, m2, m3, gain, wq, wk, wv, attn_in, qkv, mixed, stats, o0, o1, o2, o3, pieces
):
    span, group = m0.shape[0], wq.shape[1]
    place = sc[0]
    for rel, block in enumerate((m0, m1, m2, m3)):
        start = pl.multiple_of(jnp.bitwise_xor(place, rel) * span, span)
        unit, _ = norm_parts(block[...].astype(F32))
        normed = (unit * gain[...]).astype(BF)
        attn_in[pl.ds(start, span), :] = normed
        for j, weight in enumerate((wq, wk, wv)):
            qkv[pl.ds(start, span), j * group : (j + 1) * group] = dot(normed, weight[...]).astype(BF)
    lane, low, masks = half_masks(span, HEAD_DIM**-0.5)
    masks = [m.astype(BF) for m in masks]
    row = lax.broadcasted_iota(jnp.int32, (span, span), 0)
    col = lax.broadcasted_iota(jnp.int32, (span, span), 1)
    causal = col <= row
    for i in range(4):
        past = i * span
        upto = past + span
        stat = jnp.zeros((span, LANES), F32)
        for g in range(group // LANES):
            at = g * LANES
            queries = qkv[past:upto, at : at + LANES]
            keys = qkv[0:upto, group + at : group + at + LANES]
            values = qkv[0:upto, 2 * group + at : 2 * group + at + LANES]
            halves = []
            for u in range(2):
                scores = dot_cols(queries * masks[u], keys)
                last = jnp.where(causal, scores[:, past:], FAR_BELOW)
                scores = last if i == 0 else jnp.concatenate([scores[:, :past], last], axis=1)
                top = jnp.max(scores, axis=-1, keepdims=True)
                raised = jnp.exp(scores - top)
                total = jnp.sum(raised, axis=-1, keepdims=True)
                halves.append(dot(raised.astype(BF), values) * (1.0 / total))
                stat = jnp.where(lane == 2 * g + u, top + jnp.log(total), stat)
            both = jnp.where(low, halves[0], halves[1])
            mixed[past:upto, at : at + LANES] = both
            pieces[jnp.bitwise_xor(place, i), :, at : at + LANES] = both.astype(BF)
        stats[past:upto, :] = stat
    for rel, out in enumerate((o0, o1, o2, o3)):
        out[...] = pieces[rel]


def backward_body(
    sc, d0, d1, d2, d3, attn_in, qkv, mixed, stats, gain, wq, wk, wv,
    n0, n1, n2, n3, w0, w1, w2, w3, gain_out, dmix, dq, dk, dv, weight,
):
    span, group = d0.shape
    place, quarter = sc[0], sc[3]
    for rel, block in enumerate((d0, d1, d2, d3)):
        start = pl.multiple_of(jnp.bitwise_xor(place, rel) * span, span)
        dmix[pl.ds(start, span), :] = block[...]
    scale = HEAD_DIM**-0.5
    lane, low, masks_f = half_masks(span, 1.0)
    masks = [m.astype(BF) for m in masks_f]
    masks_q = [(m * scale).astype(BF) for m in masks_f]
    row = lax.broadcasted_iota(jnp.int32, (span, span), 0)
    col = lax.broadcasted_iota(jnp.int32, (span, span), 1)
    causal = col <= row
    dk[...] = jnp.zeros_like(dk)
    dv[...] = jnp.zeros_like(dv)
    for i in range(4):
        past = i * span
        upto = past + span
        for g in range(group // LANES):
            at = g * LANES
            queries = qkv[past:upto, at : at + LANES]
            keys = qkv[0:upto, group + at : group + at + LANES]
            values = qkv[0:upto, 2 * group + at : 2 * group + at + LANES]
            grads = dmix[past:upto, at : at + LANES]
            product = grads.astype(F32) * mixed[past:upto, at : at + LANES]
            dq_halves, dk_sum, dv_sum = [], None, None
            for u in range(2):
                head = 2 * g + u
                query = queries * masks_q[u]
                grad = grads * masks[u]
                weights = jnp.exp(dot_cols(query, keys) - stats[past:upto, head : head + 1])
                last = jnp.where(causal, weights[:, past:], 0.0)
                weights = last if i == 0 else jnp.concatenate([weights[:, :past], last], axis=1)
                delta = jnp.sum(product * masks_f[u], axis=-1, keepdims=True)
                score_grad = (weights * (dot_cols(grad, values) - delta)).astype(BF)
                dq_halves.append(dot(score_grad, keys))
                dk_part = dot_rows(score_grad, query)
                dv_part = dot_rows(weights.astype(BF), grad)
                dk_sum = dk_part if u == 0 else dk_sum + dk_part
                dv_sum = dv_part if u == 0 else dv_sum + dv_part
            dq[past:upto, at : at + LANES] = (jnp.where(low, dq_halves[0], dq_halves[1]) * scale).astype(BF)
            dk[0:upto, at : at + LANES] += dk_sum
            dv[0:upto, at : at + LANES] += dv_sum
    for j in range(4):
        start = pl.multiple_of(jnp.bitwise_xor(place, j) * span, span)
        rows = pl.ds(start, span)
        grad = (
            dot_cols(dq[rows, :], wq[...])
            + dot_cols(dk[rows, :].astype(BF), wk[...])
            + dot_cols(dv[rows, :].astype(BF), wv[...])
        )
        (n0, n1, n2, n3)[j][...] = grad.astype(BF)
        part = jnp.sum(grad * attn_in[rows, :].astype(F32), axis=0, keepdims=True)
        gain_sum = part if j == 0 else gain_sum + part
    gain_out[...] = gain_sum / gain[...]
    for j, source in enumerate((dq, dk, dv)):
        weight[:, j * group : (j + 1) * group] = dot_rows(attn_in[...], source[...].astype(BF)).astype(BF)
    size = weight.shape[0] // 4
    for rel, out in enumerate((w0, w1, w2, w3)):
        start = pl.multiple_of(jnp.bitwise_xor(quarter, rel) * size, 16)
        out[...] = weight[pl.ds(start, size), :]


def project_body(sc, a00, a01, a10, a11, x, w_own, w_peer, gain, seats, after, *rest):
    boxes, moe_in = rest[:-1], rest[-1]
    span = a00.shape[0]
    seq = sc[1]
    for rel, (own, peer) in enumerate(((a00, a01), (a10, a11))):
        rows = x[jnp.bitwise_xor(seq, rel)].astype(F32)
        rows = rows + (dot(own[...], w_own[...]) + dot(peer[...], w_peer[...]))
        after[rel] = rows
        unit, _ = norm_parts(rows)
        moe_in[rel * span : (rel + 1) * span, :] = (unit * gain[...]).astype(BF)
    packed = dot(seats[...], moe_in[...]).astype(BF)
    for j, box in enumerate(boxes):
        box[...] = packed[j * SEAT : (j + 1) * SEAT, :]


def pack_body(sc, grads, live, seats, *rest):
    boxes, rows = rest[:-1], rest[-1]
    span, width = grads.shape[1:]
    seq = sc[1]
    for rel in range(2):
        rows[rel * span : (rel + 1) * span, :] = grads[jnp.bitwise_xor(seq, rel)]
    packed = dot(seats[...], rows[...]).astype(BF)
    flags = dot(seats[...], live[...]).astype(BF)
    for j, box in enumerate(boxes):
        box[:, :width] = packed[j * SEAT : (j + 1) * SEAT, :]
        box[:, width:] = flags[j * SEAT : (j + 1) * SEAT, :]


def expert_body(sc, *refs):
    row_refs, grad_refs = refs[:8], refs[8:16]
    router, w_in, w_out = refs[16:19]
    back_own, back_peer, val_own, val_peer, rows, active, hidden_grad, val_grad, logit_grad = refs[19:]
    piece, width = row_refs[0].shape
    expert = sc[4]
    for k, ref in enumerate(row_refs):
        rows[k * piece : (k + 1) * piece, :] = ref[...]
    column = router[pl.ds(expert, 1), :]
    per = max(1, 512 // piece)
    for first in range(0, 8, per):
        here = slice(first * piece, (first + per) * piece)
        moe_in = rows[here, :]
        grads = jnp.concatenate([grad_refs[k][...] for k in range(first, first + per)], axis=0)
        live = grads[:, width : width + 1].astype(F32)
        grads = grads[:, :width].astype(F32)
        logit = jnp.sum(moe_in.astype(F32) * column, axis=-1, keepdims=True)
        gate = 1.0 / (1.0 + jnp.exp(-logit))
        value_grad = (gate * grads).astype(BF)
        hidden = dot(moe_in, w_in[...])
        bent = 0.5 * (1.0 + lax.erf(hidden * (0.5**0.5)))
        act = (hidden * bent).astype(BF)
        slope = bent + hidden * jnp.exp(-0.5 * hidden * hidden) * ((2.0 * jnp.pi) ** -0.5)
        pulled = (slope * dot_cols(value_grad, w_out[...])).astype(BF)
        part = dot(act, w_out[...])
        logit_part = jnp.sum(part * grads, axis=-1, keepdims=True) * (gate * (1.0 - gate) * live)
        back = (dot_cols(pulled, w_in[...]) + logit_part * column).astype(BF)
        value = (gate * part).astype(BF)
        active[here, :] = act
        hidden_grad[here, :] = pulled
        val_grad[here, :] = value_grad
        lane = lax.broadcasted_iota(jnp.int32, (logit_part.shape[0], LANES), 1)
        logit_grad[here, :] = jnp.where(lane == expert, logit_part, 0.0).astype(BF)
        for k in range(first, first + per):
            at = slice((k - first) * piece, (k - first + 1) * piece)
            to = slice((k % 4) * piece, (k % 4 + 1) * piece)
            (back_own if k < 4 else back_peer)[to, :] = back[at, :]
            (val_own if k < 4 else val_peer)[to, :] = value[at, :]


def expert_grad_body(sc, rows, active, hidden_grad, val_grad, logit_grad, in_grad, out_grad, router_grad):
    in_grad[...] = dot_rows(rows[...], hidden_grad[...])
    out_grad[...] = dot_rows(active[...], val_grad[...])
    router_grad[...] = dot_rows(logit_grad[...], rows[...])[: router_grad.shape[0], :]


def add_body(sc, own, peer, *outs):
    total = own[...].astype(F32) + peer[...].astype(F32)
    size = outs[0].shape[0]
    for j, out in enumerate(outs):
        out[...] = total[j * size : (j + 1) * size, :].astype(BF)


def add_seats_body(sc, *refs):
    parts, outs = refs[:4], refs[4:]
    total = parts[0][...].astype(F32)
    for part in parts[1:]:
        total = total + part[...].astype(F32)
    size = outs[0].shape[0]
    for j, out in enumerate(outs):
        out[...] = total[j * size : (j + 1) * size, :].astype(BF)


def return_body(
    sc, back, seats_t, after, grads, gain, w_own, w_peer, mid, branch, gain_out, d00, d01, d10, d11
):
    span = d00.shape[0]
    seq = sc[1]
    for rel, (own, peer) in enumerate(((d00, d01), (d10, d11))):
        at = slice(rel * span, (rel + 1) * span)
        upstream = dot(seats_t[at, :], back[...])
        unit, scaling = norm_parts(after[rel])
        part = jnp.sum(upstream * unit, axis=0, keepdims=True)
        gain_sum = part if rel == 0 else gain_sum + part
        total = grads[jnp.bitwise_xor(seq, rel)].astype(F32) + norm_pull(upstream * gain[...], unit, scaling)
        mid[rel] = total
        low = total.astype(BF)
        branch[rel] = low
        own[...] = dot_cols(low, w_own[...]).astype(BF)
        peer[...] = dot_cols(low, w_peer[...]).astype(BF)
    gain_out[...] = gain_sum


def projection_grad_body(sc, a00, a01, a10, a11, branch, own, peer):
    group = a00.shape[1]
    core = sc[2]
    for half, out in enumerate((own, peer)):
        to = pl.multiple_of(jnp.bitwise_xor(core, half) * group, LANES)
        cut0, cut1 = branch[0, :, pl.ds(to, group)], branch[1, :, pl.ds(to, group)]
        for kind, (first, second) in enumerate(((a00, a10), (a01, a11))):
            at = pl.multiple_of(jnp.bitwise_xor(core, kind) * group, 16)
            out[pl.ds(at, group), :] = (dot_rows(first[...], cut0) + dot_rows(second[...], cut1)).astype(BF)


def quarters_body(sc, own, peer, *outs):
    size = outs[0].shape[0]
    for rel, out in enumerate(outs):
        at = pl.ds(pl.multiple_of(jnp.bitwise_xor(sc[3], rel) * size, 16), size)
        out[...] = (own[at, :].astype(F32) + peer[at, :].astype(F32)).astype(BF)


def cut_body(sc, *refs):
    parts, outs, held = refs[:4], refs[4:-1], refs[-1]
    total = parts[0][...].astype(F32)
    for part in parts[1:]:
        total = total + part[...].astype(F32)
    size = outs[0].shape[0]
    rows = total.shape[0]
    if held.shape[0] > rows:
        held[...] = jnp.zeros_like(held)
    held[:rows, :] = total
    for rel, out in enumerate(outs):
        at = pl.multiple_of(jnp.bitwise_xor(sc[4], rel) * size, 16)
        out[...] = held[pl.ds(at, size), :].astype(BF)


def sum_body(sc, *refs):
    total = refs[0][...].astype(F32)
    for part in refs[1:-1]:
        total = total + part[...].astype(F32)
    refs[-1][...] = total.astype(BF)


def spread_body(count, step, sc, *refs):
    own, peer, out, held = refs[:4], refs[4:8], refs[8], refs[9]
    core, quarter, expert = sc[2], sc[3], sc[4]
    size = out.shape[0] // 4
    cut = own[0].shape[0] // count
    columns = own[0].shape[1]
    for half, refs_of in enumerate((own, peer)):
        side = jnp.bitwise_xor(core, half)
        for rel, ref in enumerate(refs_of):
            for j in range(count):
                at = pl.multiple_of(jnp.bitwise_xor(expert, j) * cut, 16)
                held[pl.ds(at, cut), :] = ref[j * cut : (j + 1) * cut, :].astype(F32)
            rows = pl.ds(pl.multiple_of(jnp.bitwise_xor(quarter, rel) * size, 8), size)
            for j in range(columns // step):
                to = pl.multiple_of(side * step, LANES) + 2 * j * step
                out[rows, pl.ds(pl.multiple_of(to, LANES), step)] = held[:size, j * step : (j + 1) * step]


def input_body(sc, x, mid, first_own, first_peer, second, gain, out):
    seq = sc[1]
    for rel in range(2):
        if rel == 0:
            upstream = first_own[...].astype(F32) + first_peer[...].astype(F32)
        else:
            upstream = second[...].astype(F32)
        at = jnp.bitwise_xor(seq, rel)
        unit, scaling = norm_parts(x[at].astype(F32))
        out[at] = (mid[rel] + norm_pull(upstream * gain[...], unit, scaling)).astype(BF)


def output_body(sc, after, seats_t, values, out):
    span = after.shape[1]
    for rel in range(2):
        value = dot(seats_t[rel * span : (rel + 1) * span, :], values[...])
        out[jnp.bitwise_xor(sc[1], rel)] = (after[rel] + value).astype(BF)


def local(
    blk_count,
    batch_count,
    x,
    gain_one,
    w_qkv,
    w_proj,
    gain_two,
    router,
    w_in,
    w_out,
    routes,
    quota,
    period,
    g,
):
    seq_count, span, width = x.shape
    group = width // 2
    experts = quota.shape[0]
    share = batch_count // experts
    assert blk_count == 4 and seq_count == 2 and share == 2
    blk, batch = lax.axis_index("blk"), lax.axis_index("batch")
    chip, core = blk // 2, blk % 2
    expert, half = batch // share, batch % share
    quarter = chip * 2 + half
    sc = jnp.stack([blk, chip, core, quarter, expert]).astype(jnp.int32)

    def to_blk(value, bits):
        return lax.ppermute(value, "blk", [(i, i ^ bits) for i in range(4)])

    def to_batch(value, bits):
        return lax.ppermute(value, "batch", [(i, i ^ bits) for i in range(batch_count)])

    def to_expert(value, bits):
        return to_batch(value, bits * share)

    def to_plane(value, rel):
        if rel == 1:
            return to_batch(value, 1)
        if rel == 2:
            return to_blk(value, 2)
        pairs = [
            (i * batch_count + j, (i ^ 2) * batch_count + (j ^ 1)) for i in range(4) for j in range(batch_count)
        ]
        return lax.ppermute(value, ("blk", "batch"), pairs)

    route = routes.reshape(1, seq_count * span)
    is_routed = route == jnp.arange(experts, dtype=jnp.int32)[:, None]
    token = jnp.arange(seq_count * span, dtype=jnp.int32)
    earlier = (token[:, None] < token[None, :]).astype(BF)
    before = dot(is_routed.astype(BF), earlier)
    rank = jnp.sum(jnp.where(is_routed, before, 0.0), axis=0).astype(jnp.int32)
    limit = jnp.sum(jnp.where(is_routed, quota[:, None], 0), axis=0)
    seat = jnp.where(rank < limit, jnp.bitwise_xor(route[0], expert) * SEAT + rank, -1)
    seat = seat.reshape(seq_count, span)
    live = (period == 1).astype(BF)
    seat = jnp.where(chip == 0, seat, seat[::-1]).reshape(seq_count * span)
    live = jnp.where(chip == 0, live, live[::-1])
    live = jnp.broadcast_to(jnp.repeat(live, span)[:, None], (seq_count * span, LANES))
    seat_ids = jnp.arange(experts * SEAT, dtype=jnp.int32)
    seats = (seat_ids[:, None] == seat[None, :]).astype(BF)
    seats_t = (seat[:, None] == seat_ids[None, :]).astype(BF)
    gain_one_row, gain_two_row = gain_one.reshape(1, width), gain_two.reshape(1, width)

    mine = lax.dynamic_index_in_dim(x, chip, 0, keepdims=False)
    other = lax.dynamic_index_in_dim(x, 1 - chip, 0, keepdims=False)
    block_x = to_blk(other, 2)
    block_c = to_blk(mine, 1)
    block_xc = to_blk(block_x, 1)

    def dispatch(boxes):
        rows = jnp.concatenate([boxes[0]] + [to_expert(boxes[j], j) for j in range(1, experts)], axis=0)
        own = [rows] + [to_plane(rows, rel) for rel in (1, 2, 3)]
        return own + [to_blk(part, 1) for part in own]

    grad_boxes = run_kernel(
        pack_body,
        sc,
        [g, live, seats],
        [shape_of((SEAT, width + LANES), BF)] * experts,
        [pltpu.VMEM((seq_count * span, width), BF)],
        name="pack_grads",
    )
    grad_rows = dispatch(grad_boxes)

    def third(j):
        return (w_qkv, (width, group), lambda s: (0, 2 * j + s[2]))

    def proj_half(flip):
        return (w_proj, (group, width), lambda s: (jnp.bitwise_xor(s[2], flip), 0))

    length = 4 * span
    attn_flops = 2 * length * length * group
    piece = shape_of((span, group), BF)
    attn_in, qkv, mixed, stats, own0, own1, own2, own3 = run_kernel(
        forward_body,
        sc,
        [mine, block_c, block_x, block_xc, gain_one_row, third(0), third(1), third(2)],
        [
            shape_of((length, width), BF),
            shape_of((length, 3 * group), BF),
            shape_of((length, group), F32),
            shape_of((length, LANES), F32),
            piece,
            piece,
            piece,
            piece,
        ],
        [pltpu.VMEM((4, span, group), BF)],
        flops=4 * attn_flops,
        name="attention_forward",
    )
    a00, a01, a10, a11 = own0, to_blk(own1, 1), to_blk(own2, 2), to_blk(own3, 3)
    row_box = shape_of((SEAT, width), BF)
    rows_f32 = shape_of((seq_count, span, width), F32)
    after, *boxes = run_kernel(
        project_body,
        sc,
        [a00, a01, a10, a11, x, proj_half(0), proj_half(1), gain_two_row, seats],
        [rows_f32] + [row_box] * experts,
        [pltpu.VMEM((seq_count * span, width), BF)],
        name="project",
    )
    expert_rows = dispatch(boxes)
    seat_rows = experts * SEAT
    total_rows = 8 * seat_rows
    hidden_units = w_in.shape[2]
    quad = shape_of((4 * seat_rows, width), BF)
    back_own, back_peer, val_own, val_peer, rows, active, hidden_grad, val_grad, logit_grad = run_kernel(
        expert_body,
        sc,
        [*expert_rows, *grad_rows, router.T.astype(F32), w_in[0], w_out[0]],
        [
            quad,
            quad,
            quad,
            quad,
            shape_of((total_rows, width), BF),
            shape_of((total_rows, hidden_units), BF),
            shape_of((total_rows, hidden_units), BF),
            shape_of((total_rows, width), BF),
            shape_of((total_rows, LANES), BF),
        ],
        name="expert",
    )

    def collect(own, peer):
        parts = run_kernel(
            add_body, sc, [own, to_blk(peer, 1)], [shape_of((seat_rows, width), BF)] * 4, name="add_cores"
        )
        parts = [parts[0]] + [to_plane(parts[rel], rel) for rel in (1, 2, 3)]
        cuts = run_kernel(add_seats_body, sc, parts, [row_box] * experts, name="add_plane")
        return jnp.concatenate([cuts[0]] + [to_expert(cuts[j], j) for j in range(1, experts)], axis=0)

    back = collect(back_own, back_peer)
    row = shape_of((1, width), F32)
    mid, branch, moe_gain_part, d00, d01, d10, d11 = run_kernel(
        return_body,
        sc,
        [back, seats_t, after, g, gain_two_row, proj_half(0), proj_half(1)],
        [rows_f32, shape_of((seq_count, span, width), BF), row, piece, piece, piece, piece],
        name="return_rows",
    )
    d1, d2, d3 = to_blk(d01, 1), to_blk(d10, 2), to_blk(d11, 3)
    router_rows = max(8, experts)
    in_grad, out_grad, router_part = run_kernel(
        expert_grad_body,
        sc,
        [rows, active, hidden_grad, val_grad, logit_grad],
        [
            shape_of((width, hidden_units), F32),
            shape_of((hidden_units, width), F32),
            shape_of((router_rows, width), F32),
        ],
        name="expert_grads",
    )
    proj_own, proj_peer = run_kernel(
        projection_grad_body,
        sc,
        [a00, a01, a10, a11, branch],
        [shape_of((width, group), BF)] * 2,
        name="projection_grad",
    )
    values = collect(val_own, val_peer)
    output = run_kernel(
        output_body, sc, [after, seats_t, values], [shape_of(x.shape, BF)], name="output"
    )[0]

    size = width // 4
    cut = -(-size // (experts * 16)) * 16

    def sum_everywhere(quarters, columns):
        parts = [quarters[0]] + [to_plane(quarters[rel], rel) for rel in (1, 2, 3)]
        cuts = run_kernel(
            cut_body,
            sc,
            parts,
            [shape_of((cut, columns), BF)] * experts,
            [pltpu.VMEM((experts * cut, columns), F32)],
            name="sum_plane",
        )
        parts = [cuts[0]] + [to_expert(cuts[j], j) for j in range(1, experts)]
        whole = run_kernel(sum_body, sc, parts, [shape_of((cut, columns), BF)], name="sum_experts")[0]
        column = jnp.concatenate([whole] + [to_expert(whole, j) for j in range(1, experts)], axis=0)
        plane = [column] + [to_plane(column, rel) for rel in (1, 2, 3)]
        peer = [to_blk(part, 1) for part in plane]
        return run_kernel(
            functools.partial(spread_body, experts, group),
            sc,
            plane + peer,
            [shape_of((width, 2 * columns), F32)],
            [pltpu.VMEM((experts * cut, columns), F32)],
            name="spread",
        )[0]

    proj_quarters = run_kernel(
        quarters_body, sc, [proj_own, to_blk(proj_peer, 1)], [shape_of((size, group), BF)] * 4, name="add_halves"
    )
    proj_grad = sum_everywhere(proj_quarters, group)

    part = shape_of((span, width), BF)
    quarter_out = shape_of((size, 3 * group), BF)
    n0, n1, n2, n3, q0, q1, q2, q3, attn_gain_part = run_kernel(
        backward_body,
        sc,
        [d00, d1, d2, d3, attn_in, qkv, mixed, stats, gain_one_row, third(0), third(1), third(2)],
        [part, part, part, part, quarter_out, quarter_out, quarter_out, quarter_out, row],
        [
            pltpu.VMEM((length, group), BF),
            pltpu.VMEM((length, group), BF),
            pltpu.VMEM((length, group), F32),
            pltpu.VMEM((length, group), F32),
            pltpu.VMEM((width, 3 * group), BF),
        ],
        flops=8 * attn_flops,
        name="attention_backward",
    )
    qkv_grad = sum_everywhere([q0, q1, q2, q3], 3 * group)
    first_peer = to_blk(n1, 1)
    second = run_kernel(sum_body, sc, [n2, to_blk(n3, 1)], [part], name="add_second")[0]
    second = to_blk(second, 2)
    input_grad = run_kernel(
        input_body,
        sc,
        [x, mid, n0, first_peer, second, gain_one_row],
        [shape_of(x.shape, BF)],
        name="input_grad",
    )[0]

    small = jnp.concatenate([attn_gain_part, moe_gain_part, router_part[:experts]], axis=0)
    small = small + to_blk(small, 1)
    small = small + to_blk(small, 2)
    bits = 1
    while bits < batch_count:
        small = small + to_batch(small, bits)
        bits *= 2
    return (
        output,
        input_grad,
        small[0],
        qkv_grad,
        proj_grad,
        small[1],
        small[2:].T,
        in_grad[None],
        out_grad[None],
    )


def solution(mesh):
    rows, kept = P("batch", "blk", None), P()
    w_in, w_out = P("batch", None, "blk"), P("batch", "blk", None)
    return jax.shard_map(
        functools.partial(local, mesh.shape["blk"], mesh.shape["batch"]),
        mesh=mesh,
        in_specs=(rows, kept, kept, kept, kept, kept, w_in, w_out, P("batch", "blk"), kept, P("batch"), rows),
        out_specs=(rows, rows, kept, kept, kept, kept, kept, w_in, w_out),
        check_vma=False,
    )
```

```python
import functools

import jax
import jax.numpy as jnp
from jax import lax
from jax.experimental import pallas as pl
from jax.experimental.pallas import tpu as pltpu
from jax.sharding import PartitionSpec as P

HEAD_DIM = 64
CAP = 12
SEAT = 16
LANES = 128
EPSILON = 1e-05
FAR_BELOW = -1e30
BF = jnp.bfloat16
F32 = jnp.float32


def dot(left, right):
    return jnp.dot(left, right, preferred_element_type=F32)


def dot_rows(left, right):
    return lax.dot_general(left, right, (((0,), (0,)), ((), ())), preferred_element_type=F32)


def dot_cols(left, right):
    return lax.dot_general(left, right, (((1,), (1,)), ((), ())), preferred_element_type=F32)


def norm_parts(rows):
    centred = rows - jnp.mean(rows, axis=-1, keepdims=True)
    scaling = lax.rsqrt(jnp.mean(centred * centred, axis=-1, keepdims=True) + EPSILON)
    return centred * scaling, scaling


def norm_pull(scaled, unit, scaling):
    return scaling * (
        scaled
        - jnp.mean(scaled, axis=-1, keepdims=True)
        - unit * jnp.mean(scaled * unit, axis=-1, keepdims=True)
    )


def run_kernel(body, scalars, operands, outs, scratch=(), flops=0, name=None, after=()):
    specs, arrays = [], []
    after, given, run = list(after), len(operands), body
    if after:

        def run(sc, *refs):
            body(sc, *refs[:given], *refs[given + len(after) :])

    for operand in operands:
        if isinstance(operand, tuple):
            array, block, index = operand
            specs.append(pl.BlockSpec(block, functools.partial(lambda i, s, fn: fn(s), fn=index)))
        else:
            array = operand
            specs.append(pl.BlockSpec(array.shape, functools.partial(lambda i, s, n: (0,) * n, n=array.ndim)))
        arrays.append(array)
    specs += [pl.BlockSpec(memory_space=pl.ANY)] * len(after)
    out_specs = [
        pl.BlockSpec(out.shape, functools.partial(lambda i, s, n: (0,) * n, n=len(out.shape))) for out in outs
    ]
    moved = sum(a.size * a.dtype.itemsize for a in arrays) + sum(
        o.size * jnp.dtype(o.dtype).itemsize for o in outs
    )
    return pl.pallas_call(
        run,
        grid_spec=pltpu.PrefetchScalarGridSpec(
            num_scalar_prefetch=1,
            grid=(1,),
            in_specs=specs,
            out_specs=out_specs,
            scratch_shapes=list(scratch),
        ),
        out_shape=list(outs),
        compiler_params=pltpu.CompilerParams(vmem_limit_bytes=56 * 1024 * 1024),
        cost_estimate=pl.CostEstimate(flops=int(flops), bytes_accessed=int(moved), transcendentals=0),
        name=name,
    )(scalars, *arrays, *after)


def together(values):
    return list(lax.optimization_barrier(tuple(values)))


def shape_of(dims, dtype):
    return jax.ShapeDtypeStruct(dims, dtype)


def half_masks(span, scale):
    lane = lax.broadcasted_iota(jnp.int32, (span, LANES), 1)
    low = lane < HEAD_DIM
    first = jnp.where(low, F32(scale), F32(0.0))
    second = jnp.where(low, F32(0.0), F32(scale))
    return lane, low, (first, second)


def forward_body(
    sc, m0, m1, m2, m3, gain, wq, wk, wv, attn_in, qkv, mixed, stats, o0, o1, o2, o3, pieces
):
    span, group = m0.shape[0], wq.shape[1]
    place = sc[0]
    for rel, block in enumerate((m0, m1, m2, m3)):
        start = pl.multiple_of(jnp.bitwise_xor(place, rel) * span, span)
        unit, _ = norm_parts(block[...].astype(F32))
        normed = (unit * gain[...]).astype(BF)
        attn_in[pl.ds(start, span), :] = normed
        for j, weight in enumerate((wq, wk, wv)):
            qkv[pl.ds(start, span), j * group : (j + 1) * group] = dot(normed, weight[...]).astype(BF)
    lane, low, masks = half_masks(span, HEAD_DIM**-0.5)
    masks = [m.astype(BF) for m in masks]
    row = lax.broadcasted_iota(jnp.int32, (span, span), 0)
    col = lax.broadcasted_iota(jnp.int32, (span, span), 1)
    causal = col <= row
    for i in range(4):
        past = i * span
        upto = past + span
        stat = jnp.zeros((span, LANES), F32)
        for g in range(group // LANES):
            at = g * LANES
            queries = qkv[past:upto, at : at + LANES]
            keys = qkv[0:upto, group + at : group + at + LANES]
            values = qkv[0:upto, 2 * group + at : 2 * group + at + LANES]
            halves = []
            for u in range(2):
                scores = dot_cols(queries * masks[u], keys)
                last = jnp.where(causal, scores[:, past:], FAR_BELOW)
                scores = last if i == 0 else jnp.concatenate([scores[:, :past], last], axis=1)
                top = jnp.max(scores, axis=-1, keepdims=True)
                raised = jnp.exp(scores - top)
                total = jnp.sum(raised, axis=-1, keepdims=True)
                halves.append(dot(raised.astype(BF), values) * (1.0 / total))
                stat = jnp.where(lane == 2 * g + u, top + jnp.log(total), stat)
            both = jnp.where(low, halves[0], halves[1])
            mixed[past:upto, at : at + LANES] = both
            pieces[jnp.bitwise_xor(place, i), :, at : at + LANES] = both.astype(BF)
        stats[past:upto, :] = stat
    for rel, out in enumerate((o0, o1, o2, o3)):
        out[...] = pieces[rel]


def pair_backward(stats, head, queries_of, keys_of, values_of, mixed, dmix, dq, dk, dv, dk_sum, dv_sum):
    span = queries_of.shape[0] // 4
    scale = HEAD_DIM**-0.5
    _, low, masks_f = half_masks(span, 1.0)
    masks = [m.astype(BF) for m in masks_f]
    masks_q = [(m * scale).astype(BF) for m in masks_f]
    row = lax.broadcasted_iota(jnp.int32, (span, span), 0)
    col = lax.broadcasted_iota(jnp.int32, (span, span), 1)
    causal = col <= row
    for i in reversed(range(4)):
        past = i * span
        upto = past + span
        queries = queries_of[past:upto, :]
        keys = keys_of[0:upto, :]
        values = values_of[0:upto, :]
        grads = dmix[past:upto, :]
        product = grads.astype(F32) * mixed[past:upto, :]
        dq_halves = []
        for u in range(2):
            query = queries * masks_q[u]
            grad = grads * masks[u]
            weights = jnp.exp(dot_cols(query, keys) - stats[past:upto, head + u : head + u + 1])
            last = jnp.where(causal, weights[:, past:], 0.0)
            weights = last if i == 0 else jnp.concatenate([weights[:, :past], last], axis=1)
            delta = jnp.sum(product * masks_f[u], axis=-1, keepdims=True)
            score_grad = (weights * (dot_cols(grad, values) - delta)).astype(BF)
            dq_halves.append(dot(score_grad, keys))
            dk_part = dot_rows(score_grad, query)
            dv_part = dot_rows(weights.astype(BF), grad)
            if i == 3 and u == 0:
                dk_sum[...] = dk_part
                dv_sum[...] = dv_part
            else:
                dk_sum[0:upto, :] += dk_part
                dv_sum[0:upto, :] += dv_part
        dq[past:upto, :] = (jnp.where(low, dq_halves[0], dq_halves[1]) * scale).astype(BF)
    dk[...] = dk_sum[...].astype(BF)
    dv[...] = dv_sum[...].astype(BF)


def stage_rows(held, columns, value, stride):
    size = value.shape[0] // 4
    for k in range(4):
        held[k * stride : k * stride + size, columns] = value[k * size : (k + 1) * size, :]
        if stride > size:
            held[k * stride + size : (k + 1) * stride, columns] = jnp.zeros((stride - size, value.shape[1]), BF)


def place_cuts(cut, quarter, expert, held, sent, kept, first_bit):
    stride = sent.shape[0] // 2
    other = 3 ^ first_bit
    for out, rels in ((kept, (0, other)), (sent, (first_bit, 3))):
        for n, rel in enumerate(rels):
            first = jnp.bitwise_xor(quarter, rel) * stride
            for j in range(stride // cut):
                at = pl.multiple_of(first + jnp.bitwise_xor(expert, j) * cut, 16)
                out[n * stride + j * cut : n * stride + (j + 1) * cut, :] = held[pl.ds(at, cut), :]


def load_grads(place, blocks, dmix):
    span = blocks[0].shape[0]
    for rel, block in enumerate(blocks):
        start = pl.multiple_of(jnp.bitwise_xor(place, rel) * span, span)
        dmix[pl.ds(start, span), :] = block[...]


def weight_columns(attn_in, sources, weights, held, first, stride):
    total = None
    for j, source in enumerate(sources):
        grad = dot_rows(attn_in[...], source[...])
        stage_rows(held, slice(first + j * LANES, first + (j + 1) * LANES), grad.astype(BF), stride)
        part = grad * weights[j][...].astype(F32)
        total = part if total is None else total + part
    return jnp.sum(total, axis=-1, keepdims=True)


def first_backward_body(cut, bit, sc, *refs):
    cols, (attn_in, stats, proj_own, proj_peer) = refs[:11], refs[11:15]
    dq, dk, dv, sent, kept, gain_sum, dmix, dk_sum, dv_sum, held = refs[15:]
    stride = sent.shape[0] // 2
    group = proj_own.shape[1]
    load_grads(sc[0], cols[:4], dmix)
    pair_backward(stats, 0, *cols[4:8], dmix, dq, dk, dv, dk_sum, dv_sum)
    both = (proj_own[...].astype(F32) + proj_peer[...].astype(F32)).astype(BF)
    stage_rows(held, slice(0, group), both, stride)
    sums = weight_columns(attn_in, (dq, dk, dv), cols[8:11], held, group, stride)
    gain_sum[...] = jnp.broadcast_to(sums, gain_sum.shape)
    place_cuts(cut, sc[3], sc[4], held, sent, kept, bit)


def second_backward_body(pairs, cut, bit, sc, *refs):
    count = 11 * (pairs - 1)
    cols, (attn_in, stats, gain_sum, gain, moe_cols, router_cols) = refs[:count], refs[count : count + 6]
    rest = refs[count + 6 :]
    grads, rest = rest[: 3 * (pairs - 1)], rest[3 * (pairs - 1) :]
    sent, kept, dmix, dk_sum, dv_sum, held = rest
    stride = sent.shape[0] // 2
    sums = gain_sum[:, :1]
    for n in range(pairs - 1):
        own = cols[11 * n : 11 * (n + 1)]
        load_grads(sc[0], own[:4], dmix)
        pair_backward(stats, 2 * (n + 1), *own[4:8], dmix, *grads[3 * n : 3 * n + 3], dk_sum, dv_sum)
        sums = sums + weight_columns(
            attn_in, grads[3 * n : 3 * n + 3], own[8:11], held, 3 * LANES * n, stride
        )
    small = moe_cols[...] + router_cols[...]
    lane = lax.broadcasted_iota(jnp.int32, small.shape, 1)
    small = jnp.where(lane == 0, sums / gain[...], small)
    stage_rows(held, slice(3 * LANES * (pairs - 1), 3 * LANES * (pairs - 1) + LANES), small.astype(BF), stride)
    place_cuts(cut, sc[3], sc[4], held, sent, kept, bit)


def norm_grad_body(sc, *refs):
    grads, (wq, wk, wv, own, sent, kept) = refs[:-6], refs[-6:]
    span = own.shape[0]
    for j in range(4):
        rows = pl.ds(pl.multiple_of(jnp.bitwise_xor(sc[0], j) * span, span), span)
        grad = None
        for part, weight in enumerate((wq, wk, wv)):
            cols = jnp.concatenate([grads[n][rows, :] for n in range(part, len(grads), 3)], axis=1)
            term = dot_cols(cols, weight[...])
            grad = term if part == 0 else grad + term
        if j % 2:
            sent[j // 2] = grad.astype(BF)
        else:
            (own if j == 0 else kept)[...] = grad.astype(BF)


def project_body(sc, a00, a01, a10, a11, x, w_own, w_peer, gain, seats, grads, live, after, *rest):
    boxes, (moe_in, grad_rows) = rest[:-2], rest[-2:]
    span, width = a00.shape[0], moe_in.shape[1]
    seq = sc[1]
    for rel, (own, peer) in enumerate(((a00, a01), (a10, a11))):
        at = jnp.bitwise_xor(seq, rel)
        rows = x[at].astype(F32)
        rows = rows + (dot(own[...], w_own[...]) + dot(peer[...], w_peer[...]))
        after[rel] = rows
        unit, _ = norm_parts(rows)
        moe_in[rel * span : (rel + 1) * span, :] = (unit * gain[...]).astype(BF)
        grad_rows[rel * span : (rel + 1) * span, :] = grads[at]
    packed = dot(seats[...], moe_in[...]).astype(BF)
    packed_grads = dot(seats[...], grad_rows[...]).astype(BF)
    flags = dot(seats[...], live[...]).astype(BF)
    for j, box in enumerate(boxes):
        at = slice(j * SEAT, (j + 1) * SEAT)
        box[:, :width] = packed[at, :]
        box[:, width : 2 * width] = packed_grads[at, :]
        box[:, 2 * width :] = flags[at, :]


def expert_body(sc, *refs):
    row_refs = refs[:8]
    router, w_in, w_out = refs[8:11]
    back_own, back_peer, rows, active, hidden_grad, val_grad, logit_grad = refs[11:]
    piece, width = row_refs[0].shape[0], rows.shape[1]
    expert = sc[4]
    for k, ref in enumerate(row_refs):
        rows[k * piece : (k + 1) * piece, :] = ref[:, :width]
    column = router[pl.ds(expert, 1), :]
    per = max(1, 512 // piece)
    for first in range(0, 8, per):
        here = slice(first * piece, (first + per) * piece)
        moe_in = rows[here, :]
        grads = jnp.concatenate([row_refs[k][:, width:] for k in range(first, first + per)], axis=0)
        live = grads[:, width : width + 1].astype(F32)
        grads = grads[:, :width].astype(F32)
        logit = jnp.sum(moe_in.astype(F32) * column, axis=-1, keepdims=True)
        gate = 1.0 / (1.0 + jnp.exp(-logit))
        value_grad = (gate * grads).astype(BF)
        hidden = dot(moe_in, w_in[...])
        bent = 0.5 * (1.0 + lax.erf(hidden * (0.5**0.5)))
        act = (hidden * bent).astype(BF)
        slope = bent + hidden * jnp.exp(-0.5 * hidden * hidden) * ((2.0 * jnp.pi) ** -0.5)
        pulled = (slope * dot_cols(value_grad, w_out[...])).astype(BF)
        part = dot(act, w_out[...])
        logit_part = jnp.sum(part * grads, axis=-1, keepdims=True) * (gate * (1.0 - gate) * live)
        back = (dot_cols(pulled, w_in[...]) + logit_part * column).astype(BF)
        value = (gate * part).astype(BF)
        active[here, :] = act
        hidden_grad[here, :] = pulled
        val_grad[here, :] = value_grad
        lane = lax.broadcasted_iota(jnp.int32, (logit_part.shape[0], LANES), 1)
        logit_grad[here, :] = jnp.where(lane == expert + 2, logit_part, 0.0).astype(BF)
        for k in range(first, first + per):
            at = slice((k - first) * piece, (k - first + 1) * piece)
            to = slice((k % 4) * piece, (k % 4 + 1) * piece)
            out = back_own if k < 4 else back_peer
            out[to, :width] = back[at, :]
            out[to, width:] = value[at, :]


def expert_grad_body(sc, rows, active, hidden_grad, val_grad, logit_grad, in_grad, out_grad, router_cols):
    in_grad[...] = dot_rows(rows[...], hidden_grad[...])
    out_grad[...] = dot_rows(active[...], val_grad[...])
    router_cols[...] = dot_rows(rows[...], logit_grad[...])


def return_body(
    sc, back, seats_t, after, grads, gain, w_own, w_peer, mid, branch, gain_cols, d00, d01, d10, d11
):
    span = d00.shape[0]
    seq = sc[1]
    lane = lax.broadcasted_iota(jnp.int32, (span, LANES), 1)
    pick = jnp.where(lane == 1, 1.0, 0.0).astype(BF)
    for rel, (own, peer) in enumerate(((d00, d01), (d10, d11))):
        at = slice(rel * span, (rel + 1) * span)
        upstream = dot(seats_t[at, :], back[...])
        unit, scaling = norm_parts(after[rel])
        part = dot_rows((upstream * unit).astype(BF), pick)
        gain_sum = part if rel == 0 else gain_sum + part
        total = grads[jnp.bitwise_xor(seq, rel)].astype(F32) + norm_pull(upstream * gain[...], unit, scaling)
        mid[rel] = total
        low = total.astype(BF)
        branch[rel] = low
        own[...] = dot_cols(low, w_own[...]).astype(BF)
        peer[...] = dot_cols(low, w_peer[...]).astype(BF)
    gain_cols[...] = gain_sum


def projection_grad_body(sc, a00, a01, a10, a11, branch, own, peer):
    group = a00.shape[1]
    core = sc[2]
    for half, out in enumerate((own, peer)):
        to = pl.multiple_of(jnp.bitwise_xor(core, half) * group, LANES)
        cut0, cut1 = branch[0, :, pl.ds(to, group)], branch[1, :, pl.ds(to, group)]
        for kind, (first, second) in enumerate(((a00, a10), (a01, a11))):
            at = pl.multiple_of(jnp.bitwise_xor(core, kind) * group, 16)
            out[pl.ds(at, group), :] = (dot_rows(first[...], cut0) + dot_rows(second[...], cut1)).astype(BF)


def spread_body(cut, group, pairs, sc, *refs):
    first, second = refs[:8], refs[8:16]
    qkv_out, proj_out, small_out, held = refs[16:]
    core, expert = sc[2], sc[4]
    size = qkv_out.shape[0]
    stride = first[0].shape[0]

    def place(ref):
        columns = ref.shape[1]
        for j in range(stride // cut):
            at = pl.multiple_of(jnp.bitwise_xor(expert, j) * cut, 16)
            held[pl.ds(at, cut), :columns] = ref[j * cut : (j + 1) * cut, :].astype(F32)

    def write_pair(pair, side, base):
        for j in range(3):
            to = pl.multiple_of(side * group + pair * LANES + 2 * j * group, LANES)
            qkv_out[:, pl.ds(to, LANES)] = held[:size, base + j * LANES : base + (j + 1) * LANES]

    def write(rel):
        for half in range(2):
            side = jnp.bitwise_xor(core, half)
            place(first[half * 4 + rel])
            proj_out[:, pl.ds(pl.multiple_of(side * group, LANES), group)] = held[:size, :group]
            write_pair(0, side, group)
            place(second[half * 4 + rel])
            for pair in range(1, pairs):
                write_pair(pair, side, 3 * LANES * (pair - 1))
            small = held[:size, 3 * LANES * (pairs - 1) : 3 * LANES * (pairs - 1) + LANES]
            small_out[...] = small if half == 0 else small_out[...] + small

    for rel in range(4):
        pl.when(pl.program_id(0) == rel)(functools.partial(write, rel))


def input_body(sc, x, mid, first_own, arrived, second, gain, out):
    seq = sc[1]
    for rel in range(2):
        if rel == 0:
            upstream = first_own[...].astype(F32) + arrived[0].astype(F32)
        else:
            upstream = second[...].astype(F32)
        at = jnp.bitwise_xor(seq, rel)
        unit, scaling = norm_parts(x[at].astype(F32))
        out[at] = (mid[rel] + norm_pull(upstream * gain[...], unit, scaling)).astype(BF)


def output_body(sc, after, seats_t, values, out):
    span = after.shape[1]
    for rel in range(2):
        value = dot(seats_t[rel * span : (rel + 1) * span, :], values[...])
        out[jnp.bitwise_xor(sc[1], rel)] = (after[rel] + value).astype(BF)


def local(
    blk_count,
    batch_count,
    x,
    gain_one,
    w_qkv,
    w_proj,
    gain_two,
    router,
    w_in,
    w_out,
    routes,
    quota,
    period,
    g,
):
    seq_count, span, width = x.shape
    group = width // 2
    experts = quota.shape[0]
    share = batch_count // experts
    assert blk_count == 4 and seq_count == 2 and share == 2
    blk, batch = lax.axis_index("blk"), lax.axis_index("batch")
    chip, core = blk // 2, blk % 2
    expert, half = batch // share, batch % share
    quarter = chip * 2 + half
    sc = jnp.stack([blk, chip, core, quarter, expert]).astype(jnp.int32)

    def to_blk(value, bits):
        return lax.ppermute(value, "blk", [(i, i ^ bits) for i in range(4)])

    def to_batch(value, bits):
        return lax.ppermute(value, "batch", [(i, i ^ bits) for i in range(batch_count)])

    def to_expert(value, bits):
        return to_batch(value, bits * share)

    def to_plane(value, rel):
        if rel == 1:
            return to_batch(value, 1)
        if rel == 2:
            return to_blk(value, 2)
        pairs = [
            (i * batch_count + j, (i ^ 2) * batch_count + (j ^ 1)) for i in range(4) for j in range(batch_count)
        ]
        return lax.ppermute(value, ("blk", "batch"), pairs)

    route = routes.reshape(1, seq_count * span)
    is_routed = route == jnp.arange(experts, dtype=jnp.int32)[:, None]
    token = jnp.arange(seq_count * span, dtype=jnp.int32)
    earlier = (token[:, None] < token[None, :]).astype(BF)
    before = dot(is_routed.astype(BF), earlier)
    rank = jnp.sum(jnp.where(is_routed, before, 0.0), axis=0).astype(jnp.int32)
    limit = jnp.sum(jnp.where(is_routed, quota[:, None], 0), axis=0)
    seat = jnp.where(rank < limit, jnp.bitwise_xor(route[0], expert) * SEAT + rank, -1)
    seat = seat.reshape(seq_count, span)
    live = (period == 1).astype(BF)
    seat = jnp.where(chip == 0, seat, seat[::-1]).reshape(seq_count * span)
    live = jnp.where(chip == 0, live, live[::-1])
    live = jnp.broadcast_to(jnp.repeat(live, span)[:, None], (seq_count * span, LANES))
    seat_ids = jnp.arange(experts * SEAT, dtype=jnp.int32)
    seats = (seat_ids[:, None] == seat[None, :]).astype(BF)
    seats_t = (seat[:, None] == seat_ids[None, :]).astype(BF)
    gain_one_row, gain_two_row = gain_one.reshape(1, width), gain_two.reshape(1, width)

    mine = lax.dynamic_index_in_dim(x, chip, 0, keepdims=False)
    other = lax.dynamic_index_in_dim(x, 1 - chip, 0, keepdims=False)
    block_x = to_blk(other, 2)
    block_c = to_blk(mine, 1)
    block_xc = to_blk(block_x, 1)

    def dispatch(boxes):
        rows = jnp.concatenate(
            together([boxes[0]] + [to_expert(boxes[j], j) for j in range(1, experts)]), axis=0
        )
        own = [rows] + [to_plane(rows, rel) for rel in (1, 2, 3)]
        return own + [to_blk(part, 1) for part in own]

    def third(j):
        return (w_qkv, (width, group), lambda s: (0, 2 * j + s[2]))

    def proj_half(flip):
        return (w_proj, (group, width), lambda s: (jnp.bitwise_xor(s[2], flip), 0))

    length = 4 * span
    attn_flops = 2 * length * length * group
    piece = shape_of((span, group), BF)
    attn_in, qkv, mixed, stats, own0, own1, own2, own3 = run_kernel(
        forward_body,
        sc,
        [mine, block_c, block_x, block_xc, gain_one_row, third(0), third(1), third(2)],
        [
            shape_of((length, width), BF),
            shape_of((length, 3 * group), BF),
            shape_of((length, group), F32),
            shape_of((length, LANES), F32),
            piece,
            piece,
            piece,
            piece,
        ],
        [pltpu.VMEM((4, span, group), BF)],
        flops=4 * attn_flops,
        name="attention_forward",
    )
    a00, a01, a10, a11 = own0, to_blk(own1, 1), to_blk(own2, 2), to_blk(own3, 3)
    row_box = shape_of((SEAT, 2 * width + LANES), BF)
    rows_f32 = shape_of((seq_count, span, width), F32)
    after, *boxes = run_kernel(
        project_body,
        sc,
        [a00, a01, a10, a11, x, proj_half(0), proj_half(1), gain_two_row, seats, g, live],
        [rows_f32] + [row_box] * experts,
        [pltpu.VMEM((seq_count * span, width), BF)] * 2,
        name="project",
    )
    expert_rows = dispatch(boxes)
    seat_rows = experts * SEAT
    total_rows = 8 * seat_rows
    hidden_units = w_in.shape[2]
    quad = shape_of((4 * seat_rows, 2 * width), BF)
    back_own, back_peer, rows, active, hidden_grad, val_grad, logit_grad = run_kernel(
        expert_body,
        sc,
        [*expert_rows, router.T.astype(F32), w_in[0], w_out[0]],
        [
            quad,
            quad,
            shape_of((total_rows, width), BF),
            shape_of((total_rows, hidden_units), BF),
            shape_of((total_rows, hidden_units), BF),
            shape_of((total_rows, width), BF),
            shape_of((total_rows, LANES), BF),
        ],
        name="expert",
    )
    in_grad, out_grad, router_cols = run_kernel(
        expert_grad_body,
        sc,
        [rows, active, hidden_grad, val_grad, logit_grad],
        [
            shape_of((width, hidden_units), F32),
            shape_of((hidden_units, width), F32),
            shape_of((width, LANES), F32),
        ],
        name="expert_grads",
    )

    def total_of(parts):
        total = parts[0].astype(F32)
        for part in parts[1:]:
            total = total + part.astype(F32)
        return total.astype(BF)

    arrived = to_blk(back_peer, 1)
    parts = []
    for rel in range(4):
        at = slice(rel * seat_rows, (rel + 1) * seat_rows)
        part = total_of([back_own[at], arrived[at]])
        parts.append(part if rel == 0 else to_plane(part, rel))
    parts = together(parts)
    cuts = [total_of([part[j * SEAT : (j + 1) * SEAT] for part in parts]) for j in range(experts)]
    back = jnp.concatenate(together([cuts[0]] + [to_expert(cuts[j], j) for j in range(1, experts)]), axis=0)

    wide_cols = shape_of((width, LANES), F32)
    mid, branch, moe_gain_cols, d00, d01, d10, d11 = run_kernel(
        return_body,
        sc,
        [
            (back, (seat_rows, width), lambda s: (0, 0)),
            seats_t,
            after,
            g,
            gain_two_row,
            proj_half(0),
            proj_half(1),
        ],
        [rows_f32, shape_of((seq_count, span, width), BF), wide_cols, piece, piece, piece, piece],
        name="return_rows",
        after=[router_cols],
    )
    d1, d2, d3 = to_blk(d01, 1), to_blk(d10, 2), to_blk(d11, 3)

    size = width // 4
    cut = -(-size // (experts * 16)) * 16
    stride = experts * cut

    def scatter_second(sent, kept, bit):
        arrived = to_plane(sent, bit)
        far = total_of([kept[stride:], arrived[stride:]])
        return arrived, to_plane(far, 3 ^ bit)

    def sum_cuts(kept, arrived, second):
        parts = [kept, arrived, second]
        return [total_of([part[j * cut : (j + 1) * cut] for part in parts]) for j in range(experts)]

    def sum_experts(cuts):
        return total_of(together([cuts[0]] + [to_expert(cuts[j], j) for j in range(1, experts)]))

    def gather_experts(whole):
        parts = together([whole] + [to_expert(whole, j) for j in range(1, experts)])
        return jnp.concatenate(parts, axis=0)

    def gather_plane(column):
        plane = [column, to_plane(column, 1), to_plane(column, 2)]
        plane.append(to_plane(plane[1], 2))
        return plane + [to_blk(part, 1) for part in plane]

    proj_own, proj_peer = run_kernel(
        projection_grad_body,
        sc,
        [a00, a01, a10, a11, branch],
        [shape_of((width, group), BF)] * 2,
        name="projection_grad",
    )
    proj_arrived = to_blk(proj_peer, 1)

    def columns_of(array, at):
        return (array, (array.shape[0], LANES), lambda s: (0, at))

    pairs = group // LANES

    def pair_operands(pair):
        def weight_part(j):
            return (w_qkv, (width, LANES), lambda s: (0, (2 * j + s[2]) * pairs + pair))

        return (
            [columns_of(array, pair) for array in (d00, d1, d2, d3)]
            + [columns_of(qkv, pair + j * pairs) for j in range(3)]
            + [columns_of(mixed, pair)]
            + [weight_part(j) for j in range(3)]
        )

    tall = shape_of((length, LANES), BF)
    working = [
        pltpu.VMEM((length, LANES), BF),
        pltpu.VMEM((length, LANES), F32),
        pltpu.VMEM((length, LANES), F32),
    ]
    wide_one = group + 3 * LANES
    wide_two = 3 * LANES * (pairs - 1) + LANES
    first_bit, second_bit = 1, 1
    dq, dk, dv, sent_one, kept_one, gain_sum = run_kernel(
        functools.partial(first_backward_body, cut, first_bit),
        sc,
        [*pair_operands(0), attn_in, stats, proj_own, proj_arrived],
        [tall, tall, tall] + [shape_of((2 * stride, wide_one), BF)] * 2 + [wide_cols],
        working + [pltpu.VMEM((4 * stride, wide_one), BF)],
        flops=3 * attn_flops,
        name="attention_backward_one",
    )
    arrived_one, second_one = scatter_second(sent_one, kept_one, first_bit)
    *grads, sent_two, kept_two = run_kernel(
        functools.partial(second_backward_body, pairs, cut, second_bit),
        sc,
        [operand for pair in range(1, pairs) for operand in pair_operands(pair)]
        + [attn_in, stats, gain_sum, gain_one.reshape(width, 1), moe_gain_cols, router_cols],
        [tall] * (3 * (pairs - 1)) + [shape_of((2 * stride, wide_two), BF)] * 2,
        working + [pltpu.VMEM((4 * stride, wide_two), BF)],
        flops=6 * attn_flops,
        name="attention_backward_two",
    )
    arrived_two, second_two = scatter_second(sent_two, kept_two, second_bit)
    part = shape_of((span, width), BF)
    first_own, sent, kept_rows = run_kernel(
        norm_grad_body,
        sc,
        [dq, dk, dv, *grads, third(0), third(1), third(2)],
        [part, shape_of((2, span, width), BF), part],
        name="norm_one_grad",
        after=[arrived_one],
    )
    one = gather_plane(gather_experts(sum_experts(sum_cuts(kept_one, arrived_one, second_one))))
    two = gather_plane(gather_experts(sum_experts(sum_cuts(kept_two, arrived_two, second_two))))
    arrived = to_blk(sent, 1)
    second = to_blk(total_of([kept_rows, arrived[1]]), 2)
    input_grad = run_kernel(
        input_body,
        sc,
        [x, mid, first_own, arrived, second, gain_one_row],
        [shape_of(x.shape, BF)],
        name="input_grad",
    )[0]
    output = run_kernel(
        output_body,
        sc,
        [after, seats_t, (back, (seat_rows, width), lambda s: (0, 1))],
        [shape_of(x.shape, BF)],
        name="output",
    )[0]

    def quarter_spec(columns):
        return pl.BlockSpec((size, columns), lambda i, s: (jnp.bitwise_xor(s[3], i), 0))

    out_widths = (3 * width, width, LANES)
    qkv_grad, proj_grad, small = pl.pallas_call(
        functools.partial(spread_body, cut, group, pairs),
        grid_spec=pltpu.PrefetchScalarGridSpec(
            num_scalar_prefetch=1,
            grid=(4,),
            in_specs=[pl.BlockSpec(array.shape, lambda i, s: (0, 0)) for array in one + two],
            out_specs=[quarter_spec(columns) for columns in out_widths],
            scratch_shapes=[pltpu.VMEM((stride, max(wide_one, wide_two)), F32)],
        ),
        out_shape=[shape_of((width, columns), F32) for columns in out_widths],
        compiler_params=pltpu.CompilerParams(vmem_limit_bytes=56 * 1024 * 1024),
        name="spread",
    )(sc, *one, *two)
    return (
        output,
        input_grad,
        small[:, 0],
        qkv_grad,
        proj_grad,
        small[:, 1],
        small[:, 2 : 2 + experts],
        in_grad[None],
        out_grad[None],
    )


def solution(mesh):
    rows, kept = P("batch", "blk", None), P()
    w_in, w_out = P("batch", None, "blk"), P("batch", "blk", None)
    return jax.shard_map(
        functools.partial(local, mesh.shape["blk"], mesh.shape["batch"]),
        mesh=mesh,
        in_specs=(rows, kept, kept, kept, kept, kept, w_in, w_out, P("batch", "blk"), kept, P("batch"), rows),
        out_specs=(rows, rows, kept, kept, kept, kept, kept, w_in, w_out),
        check_vma=False,
    )
```

```python
import functools

import jax
import jax.numpy as jnp
from jax import lax
from jax.experimental import pallas as pl
from jax.experimental.pallas import tpu as pltpu
from jax.sharding import PartitionSpec as P

HEAD_DIM = 64
CAP = 12
SEAT = 16
LANES = 128
EPSILON = 1e-05
FAR_BELOW = -1e30
BF = jnp.bfloat16
F32 = jnp.float32


def dot(left, right):
    return jnp.dot(left, right, preferred_element_type=F32)


def dot_rows(left, right):
    return lax.dot_general(left, right, (((0,), (0,)), ((), ())), preferred_element_type=F32)


def dot_cols(left, right):
    return lax.dot_general(left, right, (((1,), (1,)), ((), ())), preferred_element_type=F32)


def norm_parts(rows):
    centred = rows - jnp.mean(rows, axis=-1, keepdims=True)
    scaling = lax.rsqrt(jnp.mean(centred * centred, axis=-1, keepdims=True) + EPSILON)
    return centred * scaling, scaling


def norm_pull(scaled, unit, scaling):
    return scaling * (
        scaled
        - jnp.mean(scaled, axis=-1, keepdims=True)
        - unit * jnp.mean(scaled * unit, axis=-1, keepdims=True)
    )


def run_kernel(body, scalars, operands, outs, scratch=(), flops=0, name=None, after=()):
    specs, arrays = [], []
    after, given, run = list(after), len(operands), body
    if after:

        def run(sc, *refs):
            body(sc, *refs[:given], *refs[given + len(after) :])

    for operand in operands:
        if isinstance(operand, tuple):
            array, block, index = operand
            specs.append(pl.BlockSpec(block, functools.partial(lambda i, s, fn: fn(s), fn=index)))
        else:
            array = operand
            specs.append(pl.BlockSpec(memory_space=pltpu.VMEM))
        arrays.append(array)
    specs += [pl.BlockSpec(memory_space=pl.ANY)] * len(after)
    held = sum(array.size * array.dtype.itemsize for array in arrays + list(outs))
    out_specs = [pl.BlockSpec(memory_space=pltpu.VMEM) for _ in outs]
    return pl.pallas_call(
        run,
        grid_spec=pltpu.PrefetchScalarGridSpec(
            num_scalar_prefetch=1,
            grid=(1,),
            in_specs=specs,
            out_specs=out_specs,
            scratch_shapes=list(scratch),
        ),
        out_shape=list(outs),
        compiler_params=pltpu.CompilerParams(vmem_limit_bytes=(28 if held < 20e6 else 60) * 1024 * 1024),
        cost_estimate=pl.CostEstimate(flops=int(flops), bytes_accessed=0, transcendentals=0),
        name=name,
    )(scalars, *arrays, *after)


def together(values):
    return list(lax.optimization_barrier(tuple(values)))


def shape_of(dims, dtype):
    return jax.ShapeDtypeStruct(dims, dtype)


def half_masks(span, scale):
    lane = lax.broadcasted_iota(jnp.int32, (span, LANES), 1)
    low = lane < HEAD_DIM
    first = jnp.where(low, F32(scale), F32(0.0))
    second = jnp.where(low, F32(0.0), F32(scale))
    return lane, low, (first, second)


def one_hot(seat, count):
    slot = lax.broadcasted_iota(jnp.int32, (count, seat.shape[1]), 0)
    return jnp.where(slot == seat, 1.0, 0.0).astype(BF)


def forward_body(
    sc, m0, m1, m2, m3, s0, s1, s2, s3, gain, wq, wk, wv,
    attn_in, qkv, mixed, stats, o0, o1, o2, o3, k0, k2, k3, pieces,
):
    span, group = m2.shape[0], wq.shape[1]
    place = sc[0]
    for rel, block in enumerate((m0, m1, m2, m3)):
        start = pl.multiple_of(jnp.bitwise_xor(place, rel) * span, span)
        unit, _ = norm_parts(block[...].astype(F32))
        normed = (unit * gain[...]).astype(BF)
        attn_in[pl.ds(start, span), :] = normed
        for j, weight in enumerate((wq, wk, wv)):
            qkv[pl.ds(start, span), j * group : (j + 1) * group] = dot(normed, weight[...]).astype(BF)
    lane, low, masks = half_masks(span, HEAD_DIM**-0.5)
    masks = [m.astype(BF) for m in masks]
    row = lax.broadcasted_iota(jnp.int32, (span, span), 0)
    col = lax.broadcasted_iota(jnp.int32, (span, span), 1)
    causal = col <= row
    for i in range(4):
        past = i * span
        upto = past + span
        stat = jnp.zeros((span, LANES), F32)
        for g in range(group // LANES):
            at = g * LANES
            queries = qkv[past:upto, at : at + LANES]
            keys = qkv[0:upto, group + at : group + at + LANES]
            values = qkv[0:upto, 2 * group + at : 2 * group + at + LANES]
            halves = []
            for u in range(2):
                scores = dot_cols(queries * masks[u], keys)
                last = jnp.where(causal, scores[:, past:], FAR_BELOW)
                scores = last if i == 0 else jnp.concatenate([scores[:, :past], last], axis=1)
                top = jnp.max(scores, axis=-1, keepdims=True)
                raised = jnp.exp(scores - top)
                total = jnp.sum(raised, axis=-1, keepdims=True)
                halves.append(dot(raised.astype(BF), values) * (1.0 / total))
                stat = jnp.where(lane == 2 * g + u, top + jnp.log(total), stat)
            both = jnp.where(low, halves[0], halves[1])
            mixed[past:upto, at : at + LANES] = both
            pieces[jnp.bitwise_xor(place, i), :, at : at + LANES] = both.astype(BF)
        stats[past:upto, :] = stat
    for rel, (out, kept, seat) in enumerate(zip((o0, o1, o2, o3), (k0, o1, k2, k3), (s0, s1, s2, s3))):
        out[:span, :] = pieces[rel]
        rows = dot(one_hot(seat[...], k0.shape[0]), pieces[rel]).astype(BF)
        if rel == 1:
            out[span:, :] = rows
        else:
            kept[...] = rows


def pair_backward(stats, head, queries_of, keys_of, values_of, mixed, dmix, dq, dk, dv, dk_sum, dv_sum):
    span = queries_of.shape[0] // 4
    scale = HEAD_DIM**-0.5
    _, low, masks_f = half_masks(span, 1.0)
    masks = [m.astype(BF) for m in masks_f]
    masks_q = [(m * scale).astype(BF) for m in masks_f]
    row = lax.broadcasted_iota(jnp.int32, (span, span), 0)
    col = lax.broadcasted_iota(jnp.int32, (span, span), 1)
    causal = col <= row
    for i in reversed(range(4)):
        past = i * span
        upto = past + span
        queries = queries_of[past:upto, :]
        keys = keys_of[0:upto, :]
        values = values_of[0:upto, :]
        grads = dmix[past:upto, :]
        product = grads.astype(F32) * mixed[past:upto, :]
        dq_halves = []
        for u in range(2):
            query = queries * masks_q[u]
            grad = grads * masks[u]
            weights = jnp.exp(dot_cols(query, keys) - stats[past:upto, head + u : head + u + 1])
            last = jnp.where(causal, weights[:, past:], 0.0)
            weights = last if i == 0 else jnp.concatenate([weights[:, :past], last], axis=1)
            delta = jnp.sum(product * masks_f[u], axis=-1, keepdims=True)
            score_grad = (weights * (dot_cols(grad, values) - delta)).astype(BF)
            dq_halves.append(dot(score_grad, keys))
            dk_part = dot_rows(score_grad, query)
            dv_part = dot_rows(weights.astype(BF), grad)
            if i == 3 and u == 0:
                dk_sum[...] = dk_part
                dv_sum[...] = dv_part
            else:
                dk_sum[0:upto, :] += dk_part
                dv_sum[0:upto, :] += dv_part
        dq[past:upto, :] = (jnp.where(low, dq_halves[0], dq_halves[1]) * scale).astype(BF)
    dk[...] = dk_sum[...].astype(BF)
    dv[...] = dv_sum[...].astype(BF)


def stage_rows(held, columns, value, stride):
    size = value.shape[0] // 4
    for k in range(4):
        held[k * stride : k * stride + size, columns] = value[k * size : (k + 1) * size, :]
        if stride > size:
            held[k * stride + size : (k + 1) * stride, columns] = jnp.zeros((stride - size, value.shape[1]), BF)


def place_cuts(cut, quarter, expert, held, sent, kept, first_bit):
    stride = sent.shape[0] // 2
    other = 3 ^ first_bit
    for out, rels in ((kept, (0, other)), (sent, (first_bit, 3))):
        for n, rel in enumerate(rels):
            first = jnp.bitwise_xor(quarter, rel) * stride
            for j in range(stride // cut):
                at = pl.multiple_of(first + jnp.bitwise_xor(expert, j) * cut, 16)
                out[n * stride + j * cut : n * stride + (j + 1) * cut, :] = held[pl.ds(at, cut), :]


def load_grads(place, blocks, kept, seats, dmix):
    span = blocks[0].shape[0]
    for rel, block in enumerate(blocks):
        start = pl.multiple_of(jnp.bitwise_xor(place, rel) * span, span)
        late = dot_rows(one_hot(seats[rel][...], kept[rel].shape[0]), kept[rel][...])
        dmix[pl.ds(start, span), :] = (block[...].astype(F32) + late).astype(BF)


def weight_columns(attn_in, sources, weights, held, first, stride):
    total = None
    for j, source in enumerate(sources):
        grad = dot_rows(attn_in[...], source[...])
        stage_rows(held, slice(first + j * LANES, first + (j + 1) * LANES), grad.astype(BF), stride)
        part = grad * weights[j][...].astype(F32)
        total = part if total is None else total + part
    return jnp.sum(total, axis=-1, keepdims=True)


PAIR_REFS = 15


def first_backward_body(cut, bit, sc, *refs):
    cols, seats, rest = refs[:PAIR_REFS], refs[PAIR_REFS : PAIR_REFS + 4], refs[PAIR_REFS + 4 :]
    attn_in, stats, proj_own, proj_peer, attn_own, attn_peer, branch, core_late = rest[:8]
    dq, dk, dv, sent, kept, gain_sum, dmix, dk_sum, dv_sum, held = rest[8:]
    stride = sent.shape[0] // 2
    group = proj_own.shape[1]
    load_grads(sc[0], cols[:4], cols[4:8], seats, dmix)
    pair_backward(stats, 0, *cols[8:12], dmix, dq, dk, dv, dk_sum, dv_sum)
    core = sc[2]
    to = pl.multiple_of(core * group, LANES)
    late = branch[:, pl.ds(to, group)]
    late_peer = core_late[:, pl.ds(pl.multiple_of(3 * group + to, LANES), group)]
    mine = dot_rows(attn_own[...], late) + dot_rows(core_late[:, 2 * group : 3 * group], late_peer)
    others = dot_rows(attn_peer[...], late) + dot_rows(core_late[:, group : 2 * group], late_peer)
    both = jnp.concatenate(
        [jnp.where(core == 0, mine, others), jnp.where(core == 0, others, mine)], axis=0
    )
    both = (proj_own[...].astype(F32) + proj_peer[...].astype(F32) + both).astype(BF)
    stage_rows(held, slice(0, group), both, stride)
    sums = weight_columns(attn_in, (dq, dk, dv), cols[12:], held, group, stride)
    gain_sum[...] = jnp.broadcast_to(sums, gain_sum.shape)
    place_cuts(cut, sc[3], sc[4], held, sent, kept, bit)


def second_backward_body(pairs, cut, bit, sc, *refs):
    count = PAIR_REFS * (pairs - 1)
    cols, seats, rest = refs[:count], refs[count : count + 4], refs[count + 4 :]
    attn_in, stats, gain_sum, gain, moe_cols, router_cols = rest[:6]
    grads, rest = rest[6 : 6 + 3 * (pairs - 1)], rest[6 + 3 * (pairs - 1) :]
    sent, kept, dmix, dk_sum, dv_sum, held = rest
    stride = sent.shape[0] // 2
    sums = gain_sum[:, :1]
    for n in range(pairs - 1):
        own = cols[PAIR_REFS * n : PAIR_REFS * (n + 1)]
        load_grads(sc[0], own[:4], own[4:8], seats, dmix)
        pair_backward(stats, 2 * (n + 1), *own[8:12], dmix, *grads[3 * n : 3 * n + 3], dk_sum, dv_sum)
        sums = sums + weight_columns(attn_in, grads[3 * n : 3 * n + 3], own[12:], held, 3 * LANES * n, stride)
    small = moe_cols[...] + router_cols[...]
    lane = lax.broadcasted_iota(jnp.int32, small.shape, 1)
    small = jnp.where(lane == 0, sums / gain[...], small)
    stage_rows(held, slice(3 * LANES * (pairs - 1), 3 * LANES * (pairs - 1) + LANES), small.astype(BF), stride)
    place_cuts(cut, sc[3], sc[4], held, sent, kept, bit)


def norm_grad_body(sc, *refs):
    grads, (wq, wk, wv, own, sent, kept) = refs[:-6], refs[-6:]
    span = own.shape[0]
    for j in range(4):
        rows = pl.ds(pl.multiple_of(jnp.bitwise_xor(sc[0], j) * span, span), span)
        grad = None
        for part, weight in enumerate((wq, wk, wv)):
            cols = jnp.concatenate([grads[n][rows, :] for n in range(part, len(grads), 3)], axis=1)
            term = dot_cols(cols, weight[...])
            grad = term if part == 0 else grad + term
        if j % 2:
            sent[j // 2] = grad.astype(BF)
        else:
            (own if j == 0 else kept)[...] = grad.astype(BF)


def prepare_body(sc, x, grads, seats, free, live, w_own, w_peer, x_kept, tail, b00, b01, b10, b11):
    seqs, span, width = x.shape
    picks = [seats[:, n * span : (n + 1) * span] for n in range(seqs)]
    x_kept[...] = sum(dot(pick, x[n]) for n, pick in enumerate(picks)).astype(BF)
    tail[:, :width] = sum(dot(pick, grads[n]) for n, pick in enumerate(picks)).astype(BF)
    tail[:, width:] = dot(seats[...], live[...]).astype(BF)
    for rel, (own, peer) in enumerate(((b00, b01), (b10, b11))):
        at = jnp.bitwise_xor(sc[1], rel)
        rows = grads[at] * free[at]
        own[...] = dot_cols(rows, w_own[...]).astype(BF)
        peer[...] = dot_cols(rows, w_peer[...]).astype(BF)


def project_body(sc, k00, k01, k10, k11, x_kept, tail, w_own, w_peer, gain, after, own, peer, *boxes):
    own[...] = k00[...] + k10[...]
    peer[...] = k01[...] + k11[...]
    rows = x_kept[...].astype(F32) + (dot(own[...], w_own[...]) + dot(peer[...], w_peer[...]))
    after[...] = rows
    unit, _ = norm_parts(rows)
    moe_in = (unit * gain[...]).astype(BF)
    width = moe_in.shape[1]
    for j, box in enumerate(boxes):
        at = slice(j * SEAT, (j + 1) * SEAT)
        box[:, :width] = moe_in[at, :]
        box[:, width:] = tail[at, :]


def expert_body(sc, *refs):
    row_refs = refs[:8]
    router, w_in, w_out = refs[8:11]
    back_own, back_peer, rows, active, hidden_grad, val_grad, logit_grad = refs[11:]
    piece, width = row_refs[0].shape[0], rows.shape[1]
    expert = sc[4]
    for k, ref in enumerate(row_refs):
        rows[k * piece : (k + 1) * piece, :] = ref[:, :width]
    column = router[pl.ds(expert, 1), :]
    per = max(1, 512 // piece)
    for first in range(0, 8, per):
        here = slice(first * piece, (first + per) * piece)
        moe_in = rows[here, :]
        grads = jnp.concatenate([row_refs[k][:, width:] for k in range(first, first + per)], axis=0)
        live = grads[:, width : width + 1].astype(F32)
        grads = grads[:, :width].astype(F32)
        logit = jnp.sum(moe_in.astype(F32) * column, axis=-1, keepdims=True)
        gate = 1.0 / (1.0 + jnp.exp(-logit))
        value_grad = (gate * grads).astype(BF)
        hidden = dot(moe_in, w_in[...])
        bent = 0.5 * (1.0 + lax.erf(hidden * (0.5**0.5)))
        act = (hidden * bent).astype(BF)
        slope = bent + hidden * jnp.exp(-0.5 * hidden * hidden) * ((2.0 * jnp.pi) ** -0.5)
        pulled = (slope * dot_cols(value_grad, w_out[...])).astype(BF)
        part = dot(act, w_out[...])
        logit_part = jnp.sum(part * grads, axis=-1, keepdims=True) * (gate * (1.0 - gate) * live)
        back = (dot_cols(pulled, w_in[...]) + logit_part * column).astype(BF)
        value = (gate * part).astype(BF)
        active[here, :] = act
        hidden_grad[here, :] = pulled
        val_grad[here, :] = value_grad
        lane = lax.broadcasted_iota(jnp.int32, (logit_part.shape[0], LANES), 1)
        logit_grad[here, :] = jnp.where(lane == expert + 2, logit_part, 0.0).astype(BF)
        for k in range(first, first + per):
            at = slice((k - first) * piece, (k - first + 1) * piece)
            to = slice((k % 4) * piece, (k % 4 + 1) * piece)
            out = back_own if k < 4 else back_peer
            out[to, :width] = back[at, :]
            out[to, width:] = value[at, :]


def expert_grad_body(sc, rows, active, hidden_grad, val_grad, logit_grad, in_grad, out_grad, router_cols):
    in_grad[...] = dot_rows(rows[...], hidden_grad[...])
    out_grad[...] = dot_rows(active[...], val_grad[...])
    router_cols[...] = dot_rows(rows[...], logit_grad[...])


def return_body(sc, back, after, tail, attn_own, attn_peer, gain, w_own, w_peer, mid, branch, gain_cols, own, core):
    upstream = back[...].astype(F32)
    unit, scaling = norm_parts(after[...])
    lane = lax.broadcasted_iota(jnp.int32, (upstream.shape[0], LANES), 1)
    pick = jnp.where(lane == 1, 1.0, 0.0).astype(BF)
    gain_cols[...] = dot_rows((upstream * unit).astype(BF), pick)
    total = tail[...].astype(F32) + norm_pull(upstream * gain[...], unit, scaling)
    mid[...] = total
    low = total.astype(BF)
    branch[...] = low
    group = own.shape[1]
    own[...] = dot_cols(low, w_own[...]).astype(BF)
    core[:, :group] = dot_cols(low, w_peer[...]).astype(BF)
    core[:, group : 2 * group] = attn_own[...]
    core[:, 2 * group : 3 * group] = attn_peer[...]
    core[:, 3 * group :] = low


def projection_grad_body(sc, a00, a01, a10, a11, grads, free, own, peer, rows):
    span, group = a00.shape
    core = sc[2]
    for rel in range(2):
        at = jnp.bitwise_xor(sc[1], rel)
        rows[rel] = grads[at] * free[at]
    for half, out in enumerate((own, peer)):
        to = pl.ds(pl.multiple_of(jnp.bitwise_xor(core, half) * group, LANES), group)
        cut0, cut1 = rows[0, :, to], rows[1, :, to]
        for kind, (first, second) in enumerate(((a00, a10), (a01, a11))):
            at = pl.multiple_of(jnp.bitwise_xor(core, kind) * group, 16)
            total = dot_rows(first[:span, :], cut0) + dot_rows(second[...], cut1)
            out[pl.ds(at, group), :] = total.astype(BF)


def place_column(sc, cut, parts, column, out):
    size = out.shape[0] // 4
    stride = parts[0].shape[0]
    for rel, part in enumerate(parts):
        first = jnp.bitwise_xor(sc[3], rel) * size
        for j in range(stride // cut):
            place = jnp.bitwise_xor(sc[4], j) * cut
            value = part[j * cut : (j + 1) * cut, pl.ds(column, LANES)].astype(F32)

            def store(place=place, value=value, first=first):
                out[pl.ds(pl.multiple_of(first + place, 16), cut), :] = value

            if stride > size:
                pl.when(place < size)(store)
            else:
                store()


def spread_proj_body(cut, sc, *refs):
    parts, out = refs[:8], refs[8]
    step = pl.program_id(0)

    def write(side):
        place_column(sc, cut, parts[4 * side : 4 * side + 4], pl.multiple_of(step % 3 * LANES, LANES), out)

    for side in range(2):
        pl.when(step // 3 == side)(functools.partial(write, side))


def spread_body(cut, group, pairs, experts, sc, *refs):
    first, second, rest = refs[:8], refs[8:16], refs[17:]
    out, attn_gain, moe_gain, router, held = rest
    core, expert = sc[2], sc[4]
    size = out.shape[0]
    stride = first[0].shape[0]

    def write(rel):
        for half in range(2):
            side = jnp.bitwise_xor(core, half) * group
            for j in range(stride // cut):
                place = jnp.bitwise_xor(expert, j) * cut
                here = slice(j * cut, (j + 1) * cut)

                def store(place=place, here=here, half=half, side=side):
                    rows = pl.ds(pl.multiple_of(place, 16), cut)
                    for pair in range(pairs):
                        ref = (first if pair == 0 else second)[half * 4 + rel]
                        base = 0 if pair == 0 else 3 * LANES * (pair - 1)
                        for part in range(3):
                            at = base + part * LANES
                            to = pl.multiple_of(side + pair * LANES + 2 * part * group, LANES)
                            out[rows, pl.ds(to, LANES)] = ref[here, at : at + LANES].astype(F32)

                if stride > size:
                    pl.when(place < size)(store)
                else:
                    store()

    for rel in range(4):
        pl.when(pl.program_id(0) == rel)(functools.partial(write, rel))

    @pl.when(pl.program_id(0) == 0)
    def _():
        column = 3 * LANES * (pairs - 1)
        place_column(sc, cut, second[:4], column, held)
        total = held[...]
        place_column(sc, cut, second[4:], column, held)
        rows = jnp.transpose(total + held[...])
        attn_gain[...] = rows[0]
        moe_gain[...] = rows[1]
        router[...] = rows[2 : 2 + experts, :]


def input_body(sc, x, grads, free, seats_t, mid, first_own, arrived, second, gain, out):
    span = x.shape[1]
    high = mid[...].astype(BF)
    rest = (mid[...] - high.astype(F32)).astype(BF)
    for rel in range(2):
        if rel == 0:
            upstream = first_own[...].astype(F32) + arrived[0].astype(F32)
        else:
            upstream = second[...].astype(F32)
        at = jnp.bitwise_xor(sc[1], rel)
        pick = seats_t[pl.ds(pl.multiple_of(at * span, span), span), :]
        total = (grads[at] * free[at]).astype(F32) + (dot(pick, high) + dot(pick, rest))
        unit, scaling = norm_parts(x[at].astype(F32))
        out[at] = (total + norm_pull(upstream * gain[...], unit, scaling)).astype(BF)


def output_body(sc, a00, a01, a10, a11, x, w_own, w_peer, seats_t, values, out):
    span = x.shape[1]
    for rel, (own, peer) in enumerate(((a00, a01), (a10, a11))):
        at = jnp.bitwise_xor(sc[1], rel)
        rows = x[at].astype(F32) + (dot(own[:span, :], w_own[...]) + dot(peer[:span, :], w_peer[...]))
        pick = seats_t[pl.ds(pl.multiple_of(at * span, span), span), :]
        out[at] = (rows + dot(pick, values[...])).astype(BF)


def local(
    blk_count,
    batch_count,
    x,
    gain_one,
    w_qkv,
    w_proj,
    gain_two,
    router,
    w_in,
    w_out,
    routes,
    quota,
    period,
    g,
):
    seq_count, span, width = x.shape
    group = width // 2
    experts = quota.shape[0]
    share = batch_count // experts
    assert blk_count == 4 and seq_count == 2 and share == 2
    blk, batch = lax.axis_index("blk"), lax.axis_index("batch")
    chip, core = blk // 2, blk % 2
    expert, half = batch // share, batch % share
    quarter = chip * 2 + half
    sc = jnp.stack([blk, chip, core, quarter, expert]).astype(jnp.int32)

    def to_blk(value, bits):
        return lax.ppermute(value, "blk", [(i, i ^ bits) for i in range(4)])

    def to_batch(value, bits):
        return lax.ppermute(value, "batch", [(i, i ^ bits) for i in range(batch_count)])

    def to_expert(value, bits):
        return to_batch(value, bits * share)

    def to_plane(value, rel):
        if rel == 1:
            return to_batch(value, 1)
        if rel == 2:
            return to_blk(value, 2)
        pairs = [
            (i * batch_count + j, (i ^ 2) * batch_count + (j ^ 1)) for i in range(4) for j in range(batch_count)
        ]
        return lax.ppermute(value, ("blk", "batch"), pairs)

    def third(j):
        return (w_qkv, (width, group), lambda s: (0, 2 * j + s[2]))

    def proj_half(flip):
        return (w_proj, (group, width), lambda s: (jnp.bitwise_xor(s[2], flip), 0))

    mine = lax.dynamic_index_in_dim(x, chip, 0, keepdims=False)
    other = lax.dynamic_index_in_dim(x, 1 - chip, 0, keepdims=False)
    block_x = to_blk(other, 2)
    block_c = to_blk(mine, 1)

    tokens = seq_count * span
    route = routes.reshape(1, tokens)
    is_routed = route == jnp.arange(experts, dtype=jnp.int32)[:, None]
    token = jnp.arange(tokens, dtype=jnp.int32)
    earlier = (token[:, None] < token[None, :]).astype(BF)
    before = dot(is_routed.astype(BF), earlier)
    rank = jnp.sum(jnp.where(is_routed, before, 0.0), axis=0).astype(jnp.int32)
    limit = jnp.sum(jnp.where(is_routed, quota[:, None], 0), axis=0)
    seat = jnp.where(rank < limit, jnp.bitwise_xor(route[0], expert) * SEAT + rank, -1)
    seat_ids = jnp.arange(experts * SEAT, dtype=jnp.int32)
    seats = (seat_ids[:, None] == seat[None, :]).astype(BF)
    seats_t = (seat[:, None] == seat_ids[None, :]).astype(BF)
    free = (seat < 0).astype(BF).reshape(seq_count, span, 1)
    live = jnp.broadcast_to(jnp.repeat((period == 1).astype(BF), span)[:, None], (tokens, LANES))
    seat_of = seat.reshape(seq_count, 1, span)
    seat_mine = jnp.where(chip == 0, seat_of[0], seat_of[1])
    seat_other = jnp.where(chip == 0, seat_of[1], seat_of[0])
    seat_rels = [seat_mine, to_blk(seat_mine, 1), to_blk(seat_other, 2), to_blk(seat_other, 3)]
    gain_one_row, gain_two_row = gain_one.reshape(1, width), gain_two.reshape(1, width)

    seat_rows = experts * SEAT
    length = 4 * span
    piece = shape_of((span, group), BF)
    kept_piece = shape_of((seat_rows, group), BF)
    kept_rows = shape_of((seat_rows, width), BF)
    x_kept, tail, b00, b01, b10, b11 = run_kernel(
        prepare_body,
        sc,
        [x, g, seats, free, live, proj_half(0), proj_half(1)],
        [kept_rows, shape_of((seat_rows, width + LANES), BF), piece, piece, piece, piece],
        name="prepare",
    )
    base = [b00, to_blk(b01, 1), to_blk(b10, 2), to_blk(b11, 3)]
    block_x, _ = together([block_x, x_kept])
    block_xc = to_blk(block_x, 1)
    attn_in, qkv, mixed, stats, own0, own1, own2, own3, kept0, kept2, kept3 = run_kernel(
        forward_body,
        sc,
        [mine, block_c, block_x, block_xc, *seat_rels, gain_one_row, third(0), third(1), third(2)],
        [
            shape_of((length, width), BF),
            shape_of((length, 3 * group), BF),
            shape_of((length, group), F32),
            shape_of((length, LANES), F32),
            piece,
            shape_of((span + seat_rows, group), BF),
            piece,
            piece,
            kept_piece,
            kept_piece,
            kept_piece,
        ],
        [pltpu.VMEM((4, span, group), BF)],
        name="attention_forward",
    )
    own1, kept2, kept3, *base = together([own1, kept2, kept3, *base])
    core_rows = to_blk(own1, 1)
    late = [kept0, core_rows, to_blk(kept2, 2), to_blk(kept3, 3)]
    own2, own3, *late = together([own2, own3, *late])
    core_rows = late[1]
    a10, a11 = to_blk(own2, 2), to_blk(own3, 3)
    row_box = shape_of((SEAT, 2 * width + LANES), BF)
    after_kept, attn_own, attn_peer, *boxes = run_kernel(
        project_body,
        sc,
        [
            kept0,
            core_rows[span:],
            *late[2:],
            x_kept,
            tail,
            proj_half(0),
            proj_half(1),
            gain_two_row,
        ],
        [shape_of((seat_rows, width), F32), kept_piece, kept_piece] + [row_box] * experts,
        name="project",
    )

    def dispatch(boxes, before):
        parts = [boxes[0]] + [to_expert(boxes[j], j) for j in range(1, experts)]
        rows = jnp.concatenate(together([*parts, *before])[:experts], axis=0)
        own = [rows] + [to_plane(rows, rel) for rel in (1, 2, 3)]
        return own + [to_blk(part, 1) for part in own]

    expert_rows = dispatch(boxes, [a10, a11])
    total_rows = 8 * seat_rows
    hidden_units = w_in.shape[2]
    quad = shape_of((4 * seat_rows, 2 * width), BF)
    back_own, back_peer, rows, active, hidden_grad, val_grad, logit_grad = run_kernel(
        expert_body,
        sc,
        [*expert_rows, router.T.astype(F32), w_in[0], w_out[0]],
        [
            quad,
            quad,
            shape_of((total_rows, width), BF),
            shape_of((total_rows, hidden_units), BF),
            shape_of((total_rows, hidden_units), BF),
            shape_of((total_rows, width), BF),
            shape_of((total_rows, LANES), BF),
        ],
        name="expert",
    )
    in_grad, out_grad, router_cols = run_kernel(
        expert_grad_body,
        sc,
        [rows, active, hidden_grad, val_grad, logit_grad],
        [
            shape_of((width, hidden_units), F32),
            shape_of((hidden_units, width), F32),
            shape_of((width, LANES), F32),
        ],
        name="expert_grads",
    )

    def total_of(parts):
        total = parts[0].astype(F32)
        for part in parts[1:]:
            total = total + part.astype(F32)
        return total.astype(BF)

    arrived = to_blk(back_peer, 1)
    parts = []
    for rel in range(4):
        at = slice(rel * seat_rows, (rel + 1) * seat_rows)
        part = total_of([back_own[at], arrived[at]])
        parts.append(part if rel == 0 else to_plane(part, rel))
    parts = together(parts)
    cuts = [total_of([part[j * SEAT : (j + 1) * SEAT] for part in parts]) for j in range(experts)]
    back = jnp.concatenate(together([cuts[0]] + [to_expert(cuts[j], j) for j in range(1, experts)]), axis=0)

    proj_own, proj_peer = run_kernel(
        projection_grad_body,
        sc,
        [own0, core_rows, a10, a11, g, free],
        [shape_of((width, group), BF)] * 2,
        [pltpu.VMEM((seq_count, span, width), BF)],
        name="projection_grad",
        after=[back_own],
    )
    proj_arrived = to_blk(proj_peer, 1)
    wide_cols = shape_of((width, LANES), F32)
    mid, branch, moe_gain_cols, m_own, m_core = run_kernel(
        return_body,
        sc,
        [
            (back, (seat_rows, width), lambda s: (0, 0)),
            after_kept,
            (tail, (seat_rows, width), lambda s: (0, 0)),
            attn_own,
            attn_peer,
            gain_two_row,
            proj_half(0),
            proj_half(1),
        ],
        [
            shape_of((seat_rows, width), F32),
            kept_rows,
            wide_cols,
            kept_piece,
            shape_of((seat_rows, 3 * group + width), BF),
        ],
        name="return_rows",
        after=[router_cols, proj_arrived],
    )
    core_late = to_blk(m_core, 1)
    mix_late = [m_own, core_late, to_blk(m_own, 2), to_blk(m_core[:, :group], 3)]

    size = width // 4
    cut = -(-size // (experts * 16)) * 16
    stride = experts * cut

    def sum_cuts(kept, arrived, second):
        parts = [kept, arrived, second]
        return [total_of([part[j * cut : (j + 1) * cut] for part in parts]) for j in range(experts)]

    def sum_experts(cuts):
        return total_of(together([cuts[0]] + [to_expert(cuts[j], j) for j in range(1, experts)]))

    def gather_experts(whole):
        parts = together([whole] + [to_expert(whole, j) for j in range(1, experts)])
        return jnp.concatenate(parts, axis=0)

    def gather_plane(column):
        plane = [column] + [to_plane(column, rel) for rel in (1, 2, 3)]
        return plane + [to_blk(part, 1) for part in plane]


    def columns_of(array, at):
        return (array, (array.shape[0], LANES), lambda s: (0, at))

    pairs = group // LANES

    def pair_operands(pair):
        def weight_part(j):
            return (w_qkv, (width, LANES), lambda s: (0, (2 * j + s[2]) * pairs + pair))

        return (
            [columns_of(array, pair) for array in base + mix_late]
            + [columns_of(qkv, pair + j * pairs) for j in range(3)]
            + [columns_of(mixed, pair)]
            + [weight_part(j) for j in range(3)]
        )

    tall = shape_of((length, LANES), BF)
    working = [
        pltpu.VMEM((length, LANES), BF),
        pltpu.VMEM((length, LANES), F32),
        pltpu.VMEM((length, LANES), F32),
    ]
    wide_one = group + 3 * LANES
    wide_two = 3 * LANES * (pairs - 1) + LANES
    first_bit, second_bit = 1, 1
    dq, dk, dv, sent_one, kept_one, gain_sum = run_kernel(
        functools.partial(first_backward_body, cut, first_bit),
        sc,
        [
            *pair_operands(0),
            *seat_rels,
            attn_in,
            stats,
            proj_own,
            proj_arrived,
            attn_own,
            attn_peer,
            branch,
            core_late,
        ],
        [tall, tall, tall] + [shape_of((2 * stride, wide_one), BF)] * 2 + [wide_cols],
        working + [pltpu.VMEM((4 * stride, wide_one), BF)],
        name="attention_backward_one",
    )
    arrived_one = to_plane(sent_one, first_bit)
    *grads, sent_two, kept_two = run_kernel(
        functools.partial(second_backward_body, pairs, cut, second_bit),
        sc,
        [operand for pair in range(1, pairs) for operand in pair_operands(pair)]
        + [*seat_rels, attn_in, stats, gain_sum, gain_one.reshape(width, 1), moe_gain_cols, router_cols],
        [tall] * (3 * (pairs - 1)) + [shape_of((2 * stride, wide_two), BF)] * 2,
        working + [pltpu.VMEM((4 * stride, wide_two), BF)],
        name="attention_backward_two",
    )
    arrived_two = to_plane(sent_two, second_bit)
    part = shape_of((span, width), BF)

    first_own, sent, near = run_kernel(
        norm_grad_body,
        sc,
        [dq, dk, dv, *grads, third(0), third(1), third(2)],
        [part, shape_of((2, span, width), BF), part],
        name="norm_one_grad",
    )
    far_one, sent = together([total_of([kept_one[stride:], arrived_one[stride:]]), sent])
    second_one = to_plane(far_one, 3 ^ first_bit)
    arrived = to_blk(sent, 1)
    second = to_blk(total_of([near, arrived[1]]), 2)
    arrived_two, second_one = together([arrived_two, second_one])
    far_two = total_of([kept_two[stride:], arrived_two[stride:]])
    second_two = to_plane(far_two, 3 ^ second_bit)
    second_one, _ = together([second_one, arrived])
    whole_one = sum_experts(sum_cuts(kept_one, arrived_one, second_one))
    whole_one, second, _ = together([whole_one, second, far_two])
    input_grad = run_kernel(
        input_body,
        sc,
        [x, g, free, seats_t, mid, first_own, arrived, second, gain_one_row],
        [shape_of(x.shape, BF)],
        name="input_grad",
    )[0]
    output = run_kernel(
        output_body,
        sc,
        [own0, core_rows, a10, a11, x, proj_half(0), proj_half(1), seats_t, (back, (seat_rows, width), lambda s: (0, 1))],
        [shape_of(x.shape, BF)],
        name="output",
    )[0]
    column_one = gather_experts(whole_one)
    whole_two = sum_experts(sum_cuts(kept_two, arrived_two, second_two))
    whole_two, input_grad, column_one = together([whole_two, input_grad, column_one])
    one = gather_plane(column_one)
    column_two, output = together([gather_experts(whole_two), output])
    two = gather_plane(column_two)

    def whole_specs(arrays):
        return [pl.BlockSpec(array.shape, lambda i, s: (0, 0)) for array in arrays]

    params = pltpu.CompilerParams(vmem_limit_bytes=28 * 1024 * 1024)
    proj_grad = pl.pallas_call(
        functools.partial(spread_proj_body, cut),
        grid_spec=pltpu.PrefetchScalarGridSpec(
            num_scalar_prefetch=1,
            grid=(6,),
            in_specs=[pl.BlockSpec((stride, group), lambda i, s: (0, 0)) for _ in one],
            out_specs=pl.BlockSpec((width, LANES), lambda i, s: (0, jnp.bitwise_xor(s[2], i // 3) * pairs + i % 3)),
        ),
        out_shape=shape_of((width, width), F32),
        compiler_params=params,
        name="spread_proj",
    )(sc, *one)
    qkv_grad, attn_gain, moe_gain, router_grad = pl.pallas_call(
        functools.partial(spread_body, cut, group, pairs, experts),
        grid_spec=pltpu.PrefetchScalarGridSpec(
            num_scalar_prefetch=1,
            grid=(4,),
            in_specs=[pl.BlockSpec((stride, 3 * LANES), lambda i, s: (0, 1)) for _ in one]
            + whole_specs(two)
            + [pl.BlockSpec(memory_space=pl.ANY)],
            out_specs=[
                pl.BlockSpec((size, 3 * width), lambda i, s: (jnp.bitwise_xor(s[3], i), 0)),
                pl.BlockSpec((width,), lambda i, s: (0,)),
                pl.BlockSpec((width,), lambda i, s: (0,)),
                pl.BlockSpec((experts, width), lambda i, s: (0, 0)),
            ],
            scratch_shapes=[pltpu.VMEM((width, LANES), F32)],
        ),
        out_shape=[
            shape_of((width, 3 * width), F32),
            shape_of((width,), F32),
            shape_of((width,), F32),
            shape_of((experts, width), F32),
        ],
        compiler_params=params,
        name="spread",
    )(sc, *one, *two, proj_grad)
    return (
        output,
        input_grad,
        attn_gain,
        qkv_grad,
        proj_grad,
        moe_gain,
        router_grad.T,
        in_grad[None],
        out_grad[None],
    )


def solution(mesh):
    rows, kept = P("batch", "blk", None), P()
    w_in, w_out = P("batch", None, "blk"), P("batch", "blk", None)
    return jax.shard_map(
        functools.partial(local, mesh.shape["blk"], mesh.shape["batch"]),
        mesh=mesh,
        in_specs=(rows, kept, kept, kept, kept, kept, w_in, w_out, P("batch", "blk"), kept, P("batch"), rows),
        out_specs=(rows, rows, kept, kept, kept, kept, kept, w_in, w_out),
        check_vma=False,
    )
```

```python
import functools
import math

import jax
import jax.numpy as jnp
from jax import lax
from jax.experimental import pallas as pl
from jax.experimental.pallas import tpu as pltpu
from jax.sharding import PartitionSpec as P

HEAD_DIM = 64
CAP = 12
SEAT = 16
LANES = 128
EPSILON = 1e-05
FAR_BELOW = -1e30
BF = jnp.bfloat16
F32 = jnp.float32


def dot(left, right):
    return jnp.dot(left, right, preferred_element_type=F32)


def dot_rows(left, right):
    return lax.dot_general(left, right, (((0,), (0,)), ((), ())), preferred_element_type=F32)


def dot_cols(left, right):
    return lax.dot_general(left, right, (((1,), (1,)), ((), ())), preferred_element_type=F32)


def norm_parts(rows):
    centred = rows - jnp.mean(rows, axis=-1, keepdims=True)
    scaling = lax.rsqrt(jnp.mean(centred * centred, axis=-1, keepdims=True) + EPSILON)
    return centred * scaling, scaling


def norm_pull(scaled, unit, scaling):
    return scaling * (
        scaled
        - jnp.mean(scaled, axis=-1, keepdims=True)
        - unit * jnp.mean(scaled * unit, axis=-1, keepdims=True)
    )


def run_kernel(body, scalars, operands, outs, scratch=(), flops=0, name=None, after=()):
    specs, arrays, held = [], [], 0
    after, given, run = list(after), len(operands), body
    if after:

        def run(sc, *refs):
            body(sc, *refs[:given], *refs[given + len(after) :])

    for operand in operands:
        if isinstance(operand, tuple):
            array, block, index = operand
            held += 2 * math.prod(block) * array.dtype.itemsize
            specs.append(pl.BlockSpec(block, functools.partial(lambda i, s, fn: fn(s), fn=index)))
        else:
            array = operand
            held += array.size * array.dtype.itemsize
            specs.append(pl.BlockSpec(memory_space=pltpu.VMEM))
        arrays.append(array)
    specs += [pl.BlockSpec(memory_space=pl.ANY)] * len(after)
    held += sum(out.size * out.dtype.itemsize for out in outs)
    out_specs = [pl.BlockSpec(memory_space=pltpu.VMEM) for _ in outs]
    return pl.pallas_call(
        run,
        grid_spec=pltpu.PrefetchScalarGridSpec(
            num_scalar_prefetch=1,
            grid=(1,),
            in_specs=specs,
            out_specs=out_specs,
            scratch_shapes=list(scratch),
        ),
        out_shape=list(outs),
        compiler_params=pltpu.CompilerParams(vmem_limit_bytes=(28 if held < 20e6 else 60) * 1024 * 1024),
        cost_estimate=pl.CostEstimate(flops=int(flops), bytes_accessed=0, transcendentals=0),
        name=name,
    )(scalars, *arrays, *after)


def together(values):
    return list(lax.optimization_barrier(tuple(values)))


def shape_of(dims, dtype):
    return jax.ShapeDtypeStruct(dims, dtype)


def half_masks(span, scale):
    lane = lax.broadcasted_iota(jnp.int32, (span, LANES), 1)
    low = lane < HEAD_DIM
    first = jnp.where(low, F32(scale), F32(0.0))
    second = jnp.where(low, F32(0.0), F32(scale))
    return lane, low, (first, second)


def one_hot(cols, count):
    seat = cols[:, :1].astype(F32) * SEAT + cols[:, 1:2].astype(F32)
    slot = lax.broadcasted_iota(jnp.int32, (cols.shape[0], count), 1).astype(F32)
    return jnp.where(slot == seat, 1.0, 0.0).astype(BF)


def forward_body(
    sc, m0, m1, m2, m3, gain, weights, attn_in, qkv, mixed, stats, o0, o1, o2, o3, pieces
):
    span, group = m2.shape[0], weights.shape[1] // 3
    place = sc[0]
    for rel, block in enumerate((m0, m1, m2, m3)):
        start = pl.multiple_of(jnp.bitwise_xor(place, rel) * span, span)
        unit, _ = norm_parts(block[...].astype(F32))
        normed = (unit * gain[...]).astype(BF)
        attn_in[pl.ds(start, span), :] = normed
        qkv[pl.ds(start, span), :] = dot(normed, weights[...]).astype(BF)
    lane, low, masks = half_masks(span, HEAD_DIM**-0.5)
    masks = [m.astype(BF) for m in masks]
    row = lax.broadcasted_iota(jnp.int32, (span, span), 0)
    col = lax.broadcasted_iota(jnp.int32, (span, span), 1)
    causal = col <= row
    for i in range(4):
        past = i * span
        upto = past + span
        stat = jnp.zeros((span, LANES), F32)
        for g in range(group // LANES):
            at = g * LANES
            queries = qkv[past:upto, at : at + LANES]
            keys = qkv[0:upto, group + at : group + at + LANES]
            values = qkv[0:upto, 2 * group + at : 2 * group + at + LANES]
            halves = []
            for u in range(2):
                scores = dot_cols(queries * masks[u], keys)
                last = jnp.where(causal, scores[:, past:], FAR_BELOW)
                scores = last if i == 0 else jnp.concatenate([scores[:, :past], last], axis=1)
                top = jnp.max(scores, axis=-1, keepdims=True)
                raised = jnp.exp(scores - top)
                total = jnp.sum(raised, axis=-1, keepdims=True)
                halves.append(dot(raised.astype(BF), values) * (1.0 / total))
                stat = jnp.where(lane == 2 * g + u, top + jnp.log(total), stat)
            both = jnp.where(low, halves[0], halves[1])
            mixed[past:upto, at : at + LANES] = both
            pieces[jnp.bitwise_xor(place, i), :, at : at + LANES] = both.astype(BF)
        stats[past:upto, :] = stat
    for rel, out in enumerate((o0, o1, o2, o3)):
        out[...] = pieces[rel]


def pick_body(sc, o0, o1, o2, o3, b0, b1, b2, b3, k0, core, k2, k3):
    span, group = o0.shape
    for out, rows, base in ((k0, o0, b0), (core, o1, b1), (k2, o2, b2), (k3, o3, b3)):
        kept = dot_rows(one_hot(base[:, group:], k0.shape[0]), rows[...]).astype(BF)
        if out is core:
            core[:span, :] = rows[...]
            core[span:, :] = kept
        else:
            out[...] = kept


def pair_backward(stats, pair, qkv, mixed, dmix, dq, dk, dv, dk_sum, dv_sum):
    span, group, head = qkv.shape[0] // 4, qkv.shape[1] // 3, 2 * pair
    at = [slice(j * group + pair * LANES, j * group + (pair + 1) * LANES) for j in range(3)]
    scale = HEAD_DIM**-0.5
    _, low, masks_f = half_masks(span, 1.0)
    masks = [m.astype(BF) for m in masks_f]
    masks_q = [(m * scale).astype(BF) for m in masks_f]
    row = lax.broadcasted_iota(jnp.int32, (span, span), 0)
    col = lax.broadcasted_iota(jnp.int32, (span, span), 1)
    causal = col <= row
    for i in reversed(range(4)):
        past = i * span
        upto = past + span
        queries = qkv[past:upto, at[0]]
        keys = qkv[0:upto, at[1]]
        values = qkv[0:upto, at[2]]
        grads = dmix[past:upto, :]
        product = grads.astype(F32) * mixed[past:upto, at[0]]
        dq_halves = []
        for u in range(2):
            query = queries * masks_q[u]
            grad = grads * masks[u]
            weights = jnp.exp(dot_cols(query, keys) - stats[past:upto, head + u : head + u + 1])
            last = jnp.where(causal, weights[:, past:], 0.0)
            weights = last if i == 0 else jnp.concatenate([weights[:, :past], last], axis=1)
            delta = jnp.sum(product * masks_f[u], axis=-1, keepdims=True)
            score_grad = (weights * (dot_cols(grad, values) - delta)).astype(BF)
            dq_halves.append(dot(score_grad, keys))
            dk_part = dot_rows(score_grad, query)
            dv_part = dot_rows(weights.astype(BF), grad)
            if i == 3 and u == 0:
                dk_sum[...] = dk_part
                dv_sum[...] = dv_part
            else:
                dk_sum[0:upto, :] += dk_part
                dv_sum[0:upto, :] += dv_part
        dq[past:upto, :] = (jnp.where(low, dq_halves[0], dq_halves[1]) * scale).astype(BF)
    dk[...] = dk_sum[...].astype(BF)
    dv[...] = dv_sum[...].astype(BF)


def stage_rows(held, columns, value, stride):
    size = value.shape[0] // 4
    for k in range(4):
        held[k * stride : k * stride + size, columns] = value[k * size : (k + 1) * size, :]
        if stride > size:
            held[k * stride + size : (k + 1) * stride, columns] = jnp.zeros((stride - size, value.shape[1]), BF)


def place_cuts(cut, quarter, expert, held, outs):
    stride = outs[0].shape[0]
    for rel, out in enumerate(outs):
        first = jnp.bitwise_xor(quarter, rel) * stride
        for j in range(stride // cut):
            at = pl.multiple_of(first + jnp.bitwise_xor(expert, j) * cut, 16)
            out[j * cut : (j + 1) * cut, :] = held[pl.ds(at, cut), :]


def load_grads(place, pair, blocks, kept, dmix):
    span, group = blocks[0].shape[0], blocks[0].shape[1] - LANES
    at = slice(pair * LANES, (pair + 1) * LANES)
    for rel, block in enumerate(blocks):
        start = pl.multiple_of(jnp.bitwise_xor(place, rel) * span, span)
        late = dot(one_hot(block[:, group:], kept[rel].shape[0]), kept[rel][:, at])
        dmix[pl.ds(start, span), :] = (block[:, at].astype(F32) + late).astype(BF)


def weight_columns(attn_in, sources, weights, pair, held, first, stride):
    total, group = None, weights.shape[1] // 3
    for j, source in enumerate(sources):
        grad = dot_rows(attn_in[...], source[...])
        stage_rows(held, slice(first + j * LANES, first + (j + 1) * LANES), grad.astype(BF), stride)
        at = j * group + pair * LANES
        part = grad * weights[:, at : at + LANES].astype(F32)
        total = part if total is None else total + part
    return jnp.sum(total, axis=-1, keepdims=True)


def first_backward_body(cut, sc, *refs):
    base, late, rest = refs[:4], refs[4:8], refs[8:]
    qkv, mixed, attn_in, stats, weights, proj_own, proj_peer, attn_own, attn_peer, branch = rest[:10]
    dq, dk, dv, w0, w1, w2, w3, gain_sum, dmix, dk_sum, dv_sum, held = rest[10:]
    stride, group, core_late = w0.shape[0], proj_own.shape[1], late[1]
    load_grads(sc[0], 0, base, late, dmix)
    pair_backward(stats, 0, qkv, mixed, dmix, dq, dk, dv, dk_sum, dv_sum)
    core = sc[2]
    to = pl.multiple_of(core * group, LANES)
    rows = branch[:, pl.ds(to, group)]
    rows_peer = core_late[:, pl.ds(pl.multiple_of(3 * group + to, LANES), group)]
    mine = dot_rows(attn_own[...], rows) + dot_rows(core_late[:, 2 * group : 3 * group], rows_peer)
    others = dot_rows(attn_peer[...], rows) + dot_rows(core_late[:, group : 2 * group], rows_peer)
    both = jnp.concatenate([jnp.where(core == 0, mine, others), jnp.where(core == 0, others, mine)], axis=0)
    both = (proj_own[...].astype(F32) + proj_peer[...].astype(F32) + both).astype(BF)
    stage_rows(held, slice(0, group), both, stride)
    sums = weight_columns(attn_in, (dq, dk, dv), weights, 0, held, group, stride)
    gain_sum[...] = jnp.broadcast_to(sums, gain_sum.shape)
    place_cuts(cut, sc[3], sc[4], held, (w0, w1, w2, w3))


def second_backward_body(pairs, cut, sc, *refs):
    base, late, rest = refs[:4], refs[4:8], refs[8:]
    qkv, mixed, attn_in, stats, weights, gain_sum, moe_cols, router_cols = rest[:8]
    grads, rest = rest[8 : 8 + 3 * (pairs - 1)], rest[8 + 3 * (pairs - 1) :]
    outs, (dmix, dk_sum, dv_sum, held) = rest[:4], rest[4:]
    stride = outs[0].shape[0]
    sums = gain_sum[:, :1]
    for n in range(pairs - 1):
        own = grads[3 * n : 3 * n + 3]
        load_grads(sc[0], n + 1, base, late, dmix)
        pair_backward(stats, n + 1, qkv, mixed, dmix, *own, dk_sum, dv_sum)
        sums = sums + weight_columns(attn_in, own, weights, n + 1, held, 3 * LANES * n, stride)
    small = moe_cols[...] + router_cols[...]
    lane = lax.broadcasted_iota(jnp.int32, small.shape, 1)
    small = jnp.where(lane == 0, sums, small)
    stage_rows(held, slice(3 * LANES * (pairs - 1), 3 * LANES * (pairs - 1) + LANES), small.astype(BF), stride)
    place_cuts(cut, sc[3], sc[4], held, outs)


def norm_grad_body(sc, *refs):
    grads, (weights, rows_in, active, hidden_grad, val_grad, *outs) = refs[:-12], refs[-12:]
    own, sent, upper, lower, kept, in_grad, out_grad = outs
    span = own.shape[0]
    in_grad[...] = dot_rows(rows_in[...], hidden_grad[...])
    out_grad[...] = dot_rows(active[...], val_grad[...])
    for j in range(4):
        rows = pl.ds(pl.multiple_of(jnp.bitwise_xor(sc[0], j) * span, span), span)
        cols = [grads[n][rows, :] for part in range(3) for n in range(part, len(grads), 3)]
        grad = dot_cols(jnp.concatenate(cols, axis=1), weights[...]).astype(BF)
        if j == 3:
            upper[...] = grad[: span // 2]
            lower[...] = grad[span // 2 :]
        else:
            (own, sent, kept)[j][...] = grad


def proj_rows(sc, w_proj, group):
    return [
        w_proj[pl.ds(pl.multiple_of(jnp.bitwise_xor(sc[2], flip) * group, 16), group), :] for flip in range(2)
    ]


def prepare_body(
    sc, x, grads, routes, w_proj, wq, wk, wv, x_kept, tail, b00, b01, b10, b11, w_own, cols
):
    seqs, span, width = x.shape
    group, count = wq.shape[1], x_kept.shape[0]
    experts = count // SEAT
    for j, weight in enumerate((wq, wk, wv)):
        w_own[:, j * group : (j + 1) * group] = weight[...]
    proj_own, proj_peer = proj_rows(sc, w_proj, group)
    earlier = lax.broadcasted_iota(jnp.int32, (span, span), 0) < lax.broadcasted_iota(jnp.int32, (span, span), 1)
    earlier = jnp.where(earlier, 1.0, 0.0).astype(BF)
    ids = lax.broadcasted_iota(jnp.int32, (max(8, experts), span), 0)
    slots = lax.broadcasted_iota(jnp.int32, (count, span), 0)
    rows_of = lax.broadcasted_iota(jnp.int32, (LANES, span), 0)
    seen = jnp.zeros((max(8, experts), 1), F32)
    x_sum, tail_sum, flag_sum = None, None, None
    for n in range(seqs):
        route = routes[n : n + 1, :]
        mine = jnp.where(ids == route, 1.0, 0.0)
        before = dot(mine.astype(BF), earlier) + seen
        rank = jnp.sum(mine * before, axis=0, keepdims=True)
        seen = seen + jnp.sum(mine, axis=1, keepdims=True)
        limit = jnp.zeros((1, span), jnp.int32)
        for e in range(experts):
            limit = jnp.where(route == e, sc[7 + e], limit)
        kept = rank < limit.astype(F32)
        place = jnp.bitwise_xor(route, sc[4])
        seat = jnp.where(kept, place * SEAT + rank.astype(jnp.int32), -1)
        pick = jnp.where(slots == seat, 1.0, 0.0).astype(BF)
        live = jnp.where(sc[5 + n] == 1, F32(1.0), F32(0.0))
        table = jnp.where(rows_of == 0, jnp.where(kept, place.astype(F32), -1.0), 0.0)
        table = jnp.where(rows_of == 1, jnp.where(kept, rank, 0.0), table)
        table = jnp.where(rows_of == 2, live, table)
        table = jnp.where(rows_of == 3, jnp.where(kept, 0.0, 1.0), table)
        columns = jnp.transpose(table).astype(BF)
        cols[n] = columns
        parts = dot(pick, x[n]), dot(pick, grads[n]), dot(pick, columns)
        x_sum = parts[0] if n == 0 else x_sum + parts[0]
        tail_sum = parts[1] if n == 0 else tail_sum + parts[1]
        flag_sum = parts[2] if n == 0 else flag_sum + parts[2]
    x_kept[...] = x_sum.astype(BF)
    tail[:, :width] = tail_sum.astype(BF)
    tail[:, width:] = flag_sum.astype(BF)
    for rel, (own, peer) in enumerate(((b00, b01), (b10, b11))):
        at = jnp.bitwise_xor(sc[1], rel)
        own_cols = cols[at]
        rows = grads[at] * own_cols[:, 3:4]
        for out, weight in ((own, proj_own), (peer, proj_peer)):
            out[:, :group] = dot_cols(rows, weight).astype(BF)
            out[:, group:] = own_cols


def project_body(sc, k00, k01, k10, k11, x_kept, tail, w_proj, gain, after, own, peer, *boxes):
    own[...] = k00[...] + k10[...]
    peer[...] = k01[...] + k11[...]
    w_own, w_peer = proj_rows(sc, w_proj, own.shape[1])
    rows = x_kept[...].astype(F32) + (dot(own[...], w_own) + dot(peer[...], w_peer))
    after[...] = rows
    unit, _ = norm_parts(rows)
    moe_in = (unit * gain[...]).astype(BF)
    width = moe_in.shape[1]
    for j, box in enumerate(boxes):
        at = slice(j * SEAT, (j + 1) * SEAT)
        box[:, :width] = moe_in[at, :]
        box[:, width:] = tail[at, :]


def expert_body(sc, *refs):
    row_refs = refs[:8]
    router, w_in, w_out = refs[8:11]
    back_own, back_peer, rows, active, hidden_grad, val_grad, logit_grad = refs[11:]
    piece, width = row_refs[0].shape[0], rows.shape[1]
    expert = sc[4]
    for k, ref in enumerate(row_refs):
        rows[k * piece : (k + 1) * piece, :] = ref[:, :width]
    column = router[pl.ds(expert, 1), :]
    per = max(1, 512 // piece)
    for first in range(0, 8, per):
        here = slice(first * piece, (first + per) * piece)
        moe_in = rows[here, :]
        grads = jnp.concatenate([row_refs[k][:, width:] for k in range(first, first + per)], axis=0)
        live = grads[:, width + 2 : width + 3].astype(F32)
        grads = grads[:, :width].astype(F32)
        logit = jnp.sum(moe_in.astype(F32) * column, axis=-1, keepdims=True)
        gate = 1.0 / (1.0 + jnp.exp(-logit))
        value_grad = (gate * grads).astype(BF)
        hidden = dot(moe_in, w_in[...])
        bent = 0.5 * (1.0 + lax.erf(hidden * (0.5**0.5)))
        act = (hidden * bent).astype(BF)
        slope = bent + hidden * jnp.exp(-0.5 * hidden * hidden) * ((2.0 * jnp.pi) ** -0.5)
        pulled = (slope * dot_cols(value_grad, w_out[...])).astype(BF)
        part = dot(act, w_out[...])
        logit_part = jnp.sum(part * grads, axis=-1, keepdims=True) * (gate * (1.0 - gate) * live)
        back = (dot_cols(pulled, w_in[...]) + logit_part * column).astype(BF)
        value = (gate * part).astype(BF)
        active[here, :] = act
        hidden_grad[here, :] = pulled
        val_grad[here, :] = value_grad
        lane = lax.broadcasted_iota(jnp.int32, (logit_part.shape[0], LANES), 1)
        logit_grad[here, :] = jnp.where(lane == expert + 2, logit_part, 0.0).astype(BF)
        for k in range(first, first + per):
            at = slice((k - first) * piece, (k - first + 1) * piece)
            to = slice((k % 4) * piece, (k % 4 + 1) * piece)
            out = back_own if k < 4 else back_peer
            out[to, :width] = back[at, :]
            out[to, width:] = value[at, :]


def return_body(sc, back, after, tail, attn_own, attn_peer, gain, w_proj, mid, branch, gain_cols, own, far, core):
    width = after.shape[1]
    upstream = back[:, :width].astype(F32)
    unit, scaling = norm_parts(after[...])
    lane = lax.broadcasted_iota(jnp.int32, (upstream.shape[0], LANES), 1)
    pick = jnp.where(lane == 1, 1.0, 0.0).astype(BF)
    gain_cols[...] = dot_rows((upstream * unit).astype(BF), pick)
    total = tail[:, :width].astype(F32) + norm_pull(upstream * gain[...], unit, scaling)
    mid[...] = total
    low = total.astype(BF)
    branch[...] = low
    group = own.shape[1]
    w_own, w_peer = proj_rows(sc, w_proj, group)
    own[...] = dot_cols(low, w_own).astype(BF)
    pulled = dot_cols(low, w_peer).astype(BF)
    far[...] = pulled
    core[:, :group] = pulled
    core[:, group : 2 * group] = attn_own[...]
    core[:, 2 * group : 3 * group] = attn_peer[...]
    core[:, 3 * group :] = low


def projection_grad_body(sc, a00, a01, a10, a11, grads, cols, expert_rows, logit_grad, own, peer, router_cols, rows):
    router_cols[...] = dot_rows(expert_rows[...], logit_grad[...])
    span, group = a00.shape
    core = sc[2]
    for rel in range(2):
        at = jnp.bitwise_xor(sc[1], rel)
        rows[rel] = grads[at] * cols[at][:, 3:4]
    for half, out in enumerate((own, peer)):
        to = pl.ds(pl.multiple_of(jnp.bitwise_xor(core, half) * group, LANES), group)
        cut0, cut1 = rows[0, :, to], rows[1, :, to]
        for kind, (first, second) in enumerate(((a00, a10), (a01, a11))):
            at = pl.multiple_of(jnp.bitwise_xor(core, kind) * group, 16)
            total = dot_rows(first[:span, :], cut0) + dot_rows(second[...], cut1)
            out[pl.ds(at, group), :] = total.astype(BF)


def place_column(sc, cut, parts, column, out):
    size = out.shape[0] // 4
    stride = parts[0].shape[0]
    for rel, part in enumerate(parts):
        first = jnp.bitwise_xor(sc[3], rel) * size
        for j in range(stride // cut):
            place = jnp.bitwise_xor(sc[4], j) * cut
            value = part[j * cut : (j + 1) * cut, pl.ds(column, LANES)].astype(F32)

            def store(place=place, value=value, first=first):
                out[pl.ds(pl.multiple_of(first + place, 16), cut), :] = value

            if stride > size:
                pl.when(place < size)(store)
            else:
                store()


def spread_proj_body(cut, sc, *refs):
    parts, out = refs[:8], refs[8]
    step = pl.program_id(0)

    def write(side):
        place_column(sc, cut, parts[4 * side : 4 * side + 4], pl.multiple_of(step % 3 * LANES, LANES), out)

    for side in range(2):
        pl.when(step // 3 == side)(functools.partial(write, side))


def spread_body(cut, group, pairs, experts, sc, *refs):
    first, second, gain, rest = refs[:8], refs[8:16], refs[16], refs[17:]
    out, attn_gain, moe_gain, router, held = rest
    core, expert = sc[2], sc[4]
    size = out.shape[0]
    stride = first[0].shape[0]

    def write(rel):
        for half in range(2):
            side = jnp.bitwise_xor(core, half) * group
            for j in range(stride // cut):
                place = jnp.bitwise_xor(expert, j) * cut
                here = slice(j * cut, (j + 1) * cut)

                def store(place=place, here=here, half=half, side=side):
                    rows = pl.ds(pl.multiple_of(place, 16), cut)
                    for pair in range(pairs):
                        ref = (first if pair == 0 else second)[half * 4 + rel]
                        base = 0 if pair == 0 else 3 * LANES * (pair - 1)
                        for part in range(3):
                            at = base + part * LANES
                            to = pl.multiple_of(side + pair * LANES + 2 * part * group, LANES)
                            out[rows, pl.ds(to, LANES)] = ref[here, at : at + LANES].astype(F32)

                if stride > size:
                    pl.when(place < size)(store)
                else:
                    store()

    for rel in range(4):
        pl.when(pl.program_id(0) == rel)(functools.partial(write, rel))

    @pl.when(pl.program_id(0) == 0)
    def _():
        column = 3 * LANES * (pairs - 1)
        place_column(sc, cut, second[:4], column, held)
        total = held[...]
        place_column(sc, cut, second[4:], column, held)
        rows = jnp.transpose(total + held[...])
        attn_gain[...] = (rows[:1, :] / gain[...])[0]
        moe_gain[...] = rows[1]
        router[...] = rows[2 : 2 + experts, :]


def input_body(sc, x, grads, cols, mid, first_own, arrived, second, gain, out):
    high = mid[...].astype(BF)
    rest = (mid[...] - high.astype(F32)).astype(BF)
    for rel in range(2):
        if rel == 0:
            upstream = first_own[...].astype(F32) + arrived[...].astype(F32)
        else:
            upstream = second[...].astype(F32)
        at = jnp.bitwise_xor(sc[1], rel)
        own_cols = cols[at]
        pick = one_hot(own_cols, mid.shape[0])
        total = (grads[at] * own_cols[:, 3:4]).astype(F32) + (dot(pick, high) + dot(pick, rest))
        unit, scaling = norm_parts(x[at].astype(F32))
        out[at] = (total + norm_pull(upstream * gain[...], unit, scaling)).astype(BF)


def output_body(sc, a00, a01, a10, a11, x, w_proj, cols, values, out):
    span, width = x.shape[1:]
    w_own, w_peer = proj_rows(sc, w_proj, a00.shape[1])
    for rel, (own, peer) in enumerate(((a00, a01), (a10, a11))):
        at = jnp.bitwise_xor(sc[1], rel)
        rows = x[at].astype(F32) + (dot(own[:span, :], w_own) + dot(peer[:span, :], w_peer))
        pick = one_hot(cols[at], values.shape[0])
        out[at] = (rows + dot(pick, values[:, width:])).astype(BF)


def local(
    blk_count,
    batch_count,
    x,
    gain_one,
    w_qkv,
    w_proj,
    gain_two,
    router,
    w_in,
    w_out,
    routes,
    quota,
    period,
    g,
):
    seq_count, span, width = x.shape
    group = width // 2
    experts = quota.shape[0]
    share = batch_count // experts
    assert blk_count == 4 and seq_count == 2 and share == 2
    blk, batch = lax.axis_index("blk"), lax.axis_index("batch")
    chip, core = blk // 2, blk % 2
    expert, half = batch // share, batch % share
    quarter = chip * 2 + half
    sc = jnp.concatenate([jnp.stack([blk, chip, core, quarter, expert]).astype(jnp.int32), period, quota])

    def to_blk(value, bits):
        return lax.ppermute(value, "blk", [(i, i ^ bits) for i in range(4)])

    def to_batch(value, bits):
        return lax.ppermute(value, "batch", [(i, i ^ bits) for i in range(batch_count)])

    def to_expert(value, bits):
        return to_batch(value, bits * share)

    def to_plane(value, rel):
        if rel == 1:
            return to_batch(value, 1)
        if rel == 2:
            return to_blk(value, 2)
        pairs = [
            (i * batch_count + j, (i ^ 2) * batch_count + (j ^ 1)) for i in range(4) for j in range(batch_count)
        ]
        return lax.ppermute(value, ("blk", "batch"), pairs)

    def third(j):
        return (w_qkv, (width, group), lambda s: (0, 2 * j + s[2]))

    mine = lax.dynamic_index_in_dim(x, chip, 0, keepdims=False)
    other = lax.dynamic_index_in_dim(x, 1 - chip, 0, keepdims=False)
    block_x = to_blk(other, 2)
    block_c = to_blk(mine, 1)

    gain_one_row, gain_two_row = gain_one.reshape(1, width), gain_two.reshape(1, width)

    seat_rows = experts * SEAT
    length = 4 * span
    piece = shape_of((span, group), BF)
    base_piece = shape_of((span, group + LANES), BF)
    kept_piece = shape_of((seat_rows, group), BF)
    kept_rows = shape_of((seat_rows, width), BF)
    x_kept, tail, b00, b01, b10, b11, w_own, cols = run_kernel(
        prepare_body,
        sc,
        [x, g, routes, w_proj, third(0), third(1), third(2)],
        [
            kept_rows,
            shape_of((seat_rows, width + LANES), BF),
            base_piece,
            base_piece,
            base_piece,
            base_piece,
            shape_of((width, 3 * group), BF),
            shape_of((seq_count, span, LANES), BF),
        ],
        name="prepare",
    )
    block_x, b01, b10, b11 = together([block_x, b01, b10, b11])
    base = [b00, to_blk(b01, 1), to_blk(b10, 2), to_blk(b11, 3)]
    block_xc = to_blk(block_x, 1)
    attn_in, qkv, mixed, stats, own0, own1, own2, own3 = run_kernel(
        forward_body,
        sc,
        [mine, block_c, block_x, block_xc, gain_one_row, w_own],
        [
            shape_of((length, width), BF),
            shape_of((length, 3 * group), BF),
            shape_of((length, group), F32),
            shape_of((length, LANES), F32),
            piece,
            piece,
            piece,
            piece,
        ],
        [pltpu.VMEM((4, span, group), BF)],
        name="attention_forward",
    )
    kept0, core_rows, kept2, kept3 = run_kernel(
        pick_body,
        sc,
        [own0, own1, own2, own3, *base],
        [kept_piece, shape_of((span + seat_rows, group), BF), kept_piece, kept_piece],
        name="pick_kept",
    )
    core_rows = to_blk(core_rows, 1)
    late = [kept0, core_rows, to_blk(kept2, 2), to_blk(kept3, 3)]
    own2, own3, *late = together([own2, own3, *late])
    core_rows = late[1]
    a10, a11 = to_blk(own2, 2), to_blk(own3, 3)
    row_box = shape_of((SEAT, 2 * width + LANES), BF)
    after_kept, attn_own, attn_peer, *boxes = run_kernel(
        project_body,
        sc,
        [
            kept0,
            (core_rows, (seat_rows, group), lambda s: (span // seat_rows, 0)) if span % seat_rows == 0 else core_rows[span:],
            *late[2:],
            x_kept,
            tail,
            w_proj,
            gain_two_row,
        ],
        [shape_of((seat_rows, width), F32), kept_piece, kept_piece] + [row_box] * experts,
        name="project",
    )

    def dispatch(boxes, before):
        parts = [boxes[0]] + [to_expert(boxes[j], j) for j in range(1, experts)]
        rows = jnp.concatenate(together([*parts, *before])[:experts], axis=0)
        own = [rows] + [to_plane(rows, rel) for rel in (1, 2, 3)]
        return own + [to_blk(part, 1) for part in own]

    expert_rows = dispatch(boxes, [a10, a11])
    total_rows = 8 * seat_rows
    hidden_units = w_in.shape[2]
    quad = shape_of((4 * seat_rows, 2 * width), BF)
    back_own, back_peer, rows, active, hidden_grad, val_grad, logit_grad = run_kernel(
        expert_body,
        sc,
        [*expert_rows, router.T.astype(F32), w_in[0], w_out[0]],
        [
            quad,
            quad,
            shape_of((total_rows, width), BF),
            shape_of((total_rows, hidden_units), BF),
            shape_of((total_rows, hidden_units), BF),
            shape_of((total_rows, width), BF),
            shape_of((total_rows, LANES), BF),
        ],
        name="expert",
    )
    def total_of(parts):
        total = parts[0].astype(F32)
        for part in parts[1:]:
            total = total + part.astype(F32)
        return total.astype(BF)

    arrived = to_blk(back_peer, 1)
    parts = []
    for rel in range(4):
        at = slice(rel * seat_rows, (rel + 1) * seat_rows)
        part = total_of([back_own[at], arrived[at]])
        parts.append(part if rel == 0 else to_plane(part, rel))
    parts = together(parts)
    cuts = [total_of([part[j * SEAT : (j + 1) * SEAT] for part in parts]) for j in range(experts)]
    back = jnp.concatenate(together([cuts[0]] + [to_expert(cuts[j], j) for j in range(1, experts)]), axis=0)

    proj_own, proj_peer, router_cols = run_kernel(
        projection_grad_body,
        sc,
        [own0, core_rows, a10, a11, g, cols, rows, logit_grad],
        [shape_of((width, group), BF)] * 2 + [shape_of((width, LANES), F32)],
        [pltpu.VMEM((seq_count, span, width), BF)],
        name="projection_grad",
        after=[back_own],
    )
    proj_arrived = to_blk(proj_peer, 1)
    wide_cols = shape_of((width, LANES), F32)
    mid, branch, moe_gain_cols, m_own, m_far, m_core = run_kernel(
        return_body,
        sc,
        [back, after_kept, tail, attn_own, attn_peer, gain_two_row, w_proj],
        [
            shape_of((seat_rows, width), F32),
            kept_rows,
            wide_cols,
            kept_piece,
            kept_piece,
            shape_of((seat_rows, 3 * group + width), BF),
        ],
        name="return_rows",
        after=[router_cols, proj_arrived],
    )
    mix_late = [m_own, to_blk(m_core, 1), to_blk(m_own, 2), to_blk(m_far, 3)]

    size = width // 4
    cut = -(-size // (experts * 16)) * 16
    stride = experts * cut

    def scatter_plane(quarters):
        return [quarters[0]] + [to_plane(quarters[rel], rel) for rel in (1, 2, 3)]

    def sum_cuts(parts):
        return [total_of([part[j * cut : (j + 1) * cut] for part in parts]) for j in range(experts)]

    def sum_experts(cuts, before):
        parts = [cuts[0]] + [to_expert(cuts[j], j) for j in range(1, experts)]
        return total_of(together([*parts, *before])[:experts])

    def halve_experts(cuts, bits, far):
        return [total_of([near, far[j * cut : (j + 1) * cut]]) for j, near in enumerate(cuts[:bits])]

    def far_cuts(cuts, bits):
        return to_expert(jnp.concatenate(cuts[bits:], axis=0), bits)

    def gather_experts(whole, before=()):
        parts = [whole] + [to_expert(whole, j) for j in range(1, experts)]
        return jnp.concatenate(together([*parts, *before])[:experts], axis=0)

    def gather_plane(column, before=()):
        plane = [column] + [to_plane(column, rel) for rel in (1, 2, 3)]
        plane = together([*plane, *before])[:4]
        return plane + [to_blk(part, 1) for part in plane]


    pairs = group // LANES
    tall = shape_of((length, LANES), BF)
    working = [
        pltpu.VMEM((length, LANES), BF),
        pltpu.VMEM((length, LANES), F32),
        pltpu.VMEM((length, LANES), F32),
    ]
    wide_one = group + 3 * LANES
    wide_two = 3 * LANES * (pairs - 1) + LANES
    operands = [*base, *mix_late, qkv, mixed, attn_in, stats, w_own]
    dq, dk, dv, *quarters_one, gain_sum = run_kernel(
        functools.partial(first_backward_body, cut),
        sc,
        [*operands, proj_own, proj_arrived, attn_own, attn_peer, branch],
        [tall, tall, tall] + [shape_of((stride, wide_one), BF)] * 4 + [wide_cols],
        working + [pltpu.VMEM((4 * stride, wide_one), BF)],
        name="attention_backward_one",
    )
    parts_one = scatter_plane(quarters_one)
    *grads, t0, t1, t2, t3 = run_kernel(
        functools.partial(second_backward_body, pairs, cut),
        sc,
        [*operands, gain_sum, moe_gain_cols, router_cols],
        [tall] * (3 * (pairs - 1)) + [shape_of((stride, wide_two), BF)] * 4,
        working + [pltpu.VMEM((4 * stride, wide_two), BF)],
        name="attention_backward_two",
    )
    t1, t2, t3, *parts_one = together([t1, t2, t3, *parts_one])
    parts_two = scatter_plane([t0, t1, t2, t3])
    cuts_one, bits = sum_cuts(parts_one), experts // 2
    far = far_cuts(cuts_one, bits)
    part = shape_of((span, width), BF)
    near_piece = shape_of((span // 2, width), BF)
    first_own, sent, upper, lower, near, in_grad, out_grad = run_kernel(
        norm_grad_body,
        sc,
        [dq, dk, dv, *grads, w_own, rows, active, hidden_grad, val_grad],
        [
            part,
            part,
            near_piece,
            near_piece,
            part,
            shape_of((width, hidden_units), F32),
            shape_of((hidden_units, width), F32),
        ],
        name="norm_one_grad",
        flops=10e9,
    )
    upper, lower = to_blk(upper, 1), to_blk(lower, 1)
    *parts_two, out_grad = together([*parts_two, out_grad])
    upper, lower, *parts_two = together([upper, lower, *parts_two])
    second = to_blk(total_of([near, jnp.concatenate([upper, lower], axis=0)]), 2)
    arrived = to_blk(sent, 1)
    while bits:
        cuts_one = halve_experts(cuts_one, bits, far)
        bits //= 2
        if bits:
            far = far_cuts(cuts_one, bits)
        if bits == 1:
            far, *_ = together([far, *parts_two])
    whole_one = cuts_one[0]
    column_one = gather_experts(whole_one, [second])
    whole_two = sum_experts(sum_cuts(parts_two), [])
    input_grad = run_kernel(
        input_body,
        sc,
        [x, g, cols, mid, first_own, arrived, second, gain_one_row],
        [shape_of(x.shape, BF)],
        name="input_grad",
    )[0]
    output = run_kernel(
        output_body,
        sc,
        [own0, core_rows, a10, a11, x, w_proj, cols, back],
        [shape_of(x.shape, BF)],
        name="output",
    )[0]
    one = gather_plane(column_one)
    proj_grad = pl.pallas_call(
        functools.partial(spread_proj_body, cut),
        grid_spec=pltpu.PrefetchScalarGridSpec(
            num_scalar_prefetch=1,
            grid=(6,),
            in_specs=[pl.BlockSpec((stride, group), lambda i, s: (0, 0)) for _ in one],
            out_specs=pl.BlockSpec((width, LANES), lambda i, s: (0, jnp.bitwise_xor(s[2], i // 3) * pairs + i % 3)),
        ),
        out_shape=shape_of((width, width), F32),
        compiler_params=pltpu.CompilerParams(vmem_limit_bytes=28 * 1024 * 1024),
        name="spread_proj",
    )(sc, *one)
    two = gather_plane(gather_experts(whole_two), [output, input_grad, proj_grad])

    def whole_specs(arrays):
        return [pl.BlockSpec(array.shape, lambda i, s: (0, 0)) for array in arrays]

    params = pltpu.CompilerParams(vmem_limit_bytes=28 * 1024 * 1024)
    qkv_grad, attn_gain, moe_gain, router_grad = pl.pallas_call(
        functools.partial(spread_body, cut, group, pairs, experts),
        grid_spec=pltpu.PrefetchScalarGridSpec(
            num_scalar_prefetch=1,
            grid=(4,),
            in_specs=[pl.BlockSpec((stride, 3 * LANES), lambda i, s: (0, 1)) for _ in one]
            + whole_specs(two)
            + [pl.BlockSpec(memory_space=pltpu.VMEM)],
            out_specs=[
                pl.BlockSpec((size, 3 * width), lambda i, s: (jnp.bitwise_xor(s[3], i), 0)),
                pl.BlockSpec((width,), lambda i, s: (0,)),
                pl.BlockSpec((width,), lambda i, s: (0,)),
                pl.BlockSpec((experts, width), lambda i, s: (0, 0)),
            ],
            scratch_shapes=[pltpu.VMEM((width, LANES), F32)],
        ),
        out_shape=[
            shape_of((width, 3 * width), F32),
            shape_of((width,), F32),
            shape_of((width,), F32),
            shape_of((experts, width), F32),
        ],
        compiler_params=params,
        name="spread",
    )(sc, *one, *two, gain_one_row)
    return (
        output,
        input_grad,
        attn_gain,
        qkv_grad,
        proj_grad,
        moe_gain,
        router_grad.T,
        in_grad[None],
        out_grad[None],
    )


def solution(mesh):
    rows, kept = P("batch", "blk", None), P()
    w_in, w_out = P("batch", None, "blk"), P("batch", "blk", None)
    return jax.shard_map(
        functools.partial(local, mesh.shape["blk"], mesh.shape["batch"]),
        mesh=mesh,
        in_specs=(rows, kept, kept, kept, kept, kept, w_in, w_out, P("batch", "blk"), kept, P("batch"), rows),
        out_specs=(rows, rows, kept, kept, kept, kept, kept, w_in, w_out),
        check_vma=False,
    )
```

```python
import functools
import math

import jax
import jax.numpy as jnp
from jax import lax
from jax.experimental import pallas as pl
from jax.experimental.pallas import tpu as pltpu
from jax.sharding import PartitionSpec as P

HEAD_DIM = 64
CAP = 12
SEAT = 16
LANES = 128
EPSILON = 1e-05
FAR_BELOW = -1e30
BF = jnp.bfloat16
F32 = jnp.float32


def dot(left, right):
    return jnp.dot(left, right, preferred_element_type=F32)


def dot_rows(left, right):
    return lax.dot_general(left, right, (((0,), (0,)), ((), ())), preferred_element_type=F32)


def dot_cols(left, right):
    return lax.dot_general(left, right, (((1,), (1,)), ((), ())), preferred_element_type=F32)


def norm_parts(rows):
    centred = rows - jnp.mean(rows, axis=-1, keepdims=True)
    scaling = lax.rsqrt(jnp.mean(centred * centred, axis=-1, keepdims=True) + EPSILON)
    return centred * scaling, scaling


def norm_pull(scaled, unit, scaling):
    return scaling * (
        scaled
        - jnp.mean(scaled, axis=-1, keepdims=True)
        - unit * jnp.mean(scaled * unit, axis=-1, keepdims=True)
    )


def run_kernel(body, scalars, operands, outs, scratch=(), flops=0, name=None, after=()):
    specs, arrays, held = [], [], 0
    after, given, run = list(after), len(operands), body
    if after:

        def run(sc, *refs):
            body(sc, *refs[:given], *refs[given + len(after) :])

    for operand in operands:
        if isinstance(operand, tuple):
            array, block, index = operand
            held += 2 * math.prod(block) * array.dtype.itemsize
            specs.append(pl.BlockSpec(block, functools.partial(lambda i, s, fn: fn(s), fn=index)))
        else:
            array = operand
            held += array.size * array.dtype.itemsize
            specs.append(pl.BlockSpec(memory_space=pltpu.VMEM))
        arrays.append(array)
    specs += [pl.BlockSpec(memory_space=pl.ANY)] * len(after)
    held += sum(out.size * out.dtype.itemsize for out in outs)
    out_specs = [pl.BlockSpec(memory_space=pltpu.VMEM) for _ in outs]
    return pl.pallas_call(
        run,
        grid_spec=pltpu.PrefetchScalarGridSpec(
            num_scalar_prefetch=1,
            grid=(1,),
            in_specs=specs,
            out_specs=out_specs,
            scratch_shapes=list(scratch),
        ),
        out_shape=list(outs),
        compiler_params=pltpu.CompilerParams(vmem_limit_bytes=(28 if held < 20e6 else 60) * 1024 * 1024),
        cost_estimate=pl.CostEstimate(flops=int(flops), bytes_accessed=0, transcendentals=0),
        name=name,
    )(scalars, *arrays, *after)


def together(values):
    return list(lax.optimization_barrier(tuple(values)))


def shape_of(dims, dtype):
    return jax.ShapeDtypeStruct(dims, dtype)


def half_masks(scale):
    lane = lax.broadcasted_iota(jnp.int32, (1, LANES), 1)
    low = lane < HEAD_DIM
    return lane, low, (jnp.where(low, scale, 0.0).astype(BF), jnp.where(low, 0.0, scale).astype(BF))


def one_hot(cols, count):
    seat = cols[:, :1].astype(F32) * SEAT + cols[:, 1:2].astype(F32)
    slot = lax.broadcasted_iota(jnp.int32, (cols.shape[0], count), 1).astype(F32)
    return jnp.where(slot == seat, 1.0, 0.0).astype(BF)


def forward_body(
    sc, m0, m1, m2, m3, gain, weights, attn_in, qkv, mixed, stats, o0, o1, o2, o3, pieces
):
    span, group = m2.shape[0], weights.shape[1] // 3
    place = sc[0]
    for rel, block in enumerate((m0, m1, m2, m3)):
        start = pl.multiple_of(jnp.bitwise_xor(place, rel) * span, span)
        unit, _ = norm_parts(block[...].astype(F32))
        normed = (unit * gain[...]).astype(BF)
        attn_in[pl.ds(start, span), :] = normed
        qkv[pl.ds(start, span), :] = dot(normed, weights[...]).astype(BF)
    lane, low, scaled = half_masks(HEAD_DIM**-0.5)
    _, _, ones = half_masks(1.0)
    row = lax.broadcasted_iota(jnp.int32, (span, span), 0)
    col = lax.broadcasted_iota(jnp.int32, (span, span), 1)
    causal = col <= row
    for i in range(4):
        past = i * span
        upto = past + span
        stat = jnp.zeros((span, LANES), F32)
        for g in range(group // LANES):
            at = g * LANES
            queries = qkv[past:upto, at : at + LANES]
            keys = qkv[0:upto, group + at : group + at + LANES]
            values = qkv[0:upto, 2 * group + at : 2 * group + at + LANES]
            scores = [dot_cols(queries * scaled[u], keys) for u in range(2)]
            mixes, tops = [], []
            for u in range(2):
                last = jnp.where(causal, scores[u][:, past:], FAR_BELOW)
                top = jnp.max(last, axis=-1, keepdims=True)
                if i:
                    top = jnp.maximum(top, jnp.max(scores[u][:, :past], axis=-1, keepdims=True))
                beside = values * ones[u] + ones[1 - u]
                mix = dot(jnp.exp(last - top).astype(BF), beside[past:])
                if i:
                    mix = mix + dot(jnp.exp(scores[u][:, :past] - top).astype(BF), beside[:past])
                mixes.append(mix)
                tops.append(top)
            totals = pltpu.roll(jnp.where(low, mixes[1], mixes[0]), HEAD_DIM, 1)
            both = jnp.where(low, mixes[0], mixes[1]) / totals
            logs = jnp.log(totals)
            for u in range(2):
                stat = jnp.where(lane == 2 * g + u, tops[u] + logs[:, u * HEAD_DIM : u * HEAD_DIM + 1], stat)
            mixed[past:upto, at : at + LANES] = both
            pieces[jnp.bitwise_xor(place, i), :, at : at + LANES] = both.astype(BF)
        stats[past:upto, :] = stat
    for rel, out in enumerate((o0, o1, o2, o3)):
        out[...] = pieces[rel]


def pick_body(sc, o0, o1, o2, o3, b0, b1, b2, b3, k0, core, k2, k3):
    span, group = o0.shape
    for out, rows, base in ((k0, o0, b0), (core, o1, b1), (k2, o2, b2), (k3, o3, b3)):
        kept = dot_rows(one_hot(base[:, group:], k0.shape[0]), rows[...]).astype(BF)
        if out is core:
            core[:span, :] = rows[...]
            core[span:, :] = kept
        else:
            out[...] = kept


def pair_backward(stats, pair, qkv, mixed, dmix, dq, dk, dv, dk_sum, dv_sum):
    span, group, head = qkv.shape[0] // 4, qkv.shape[1] // 3, 2 * pair
    at = [slice(j * group + pair * LANES, j * group + (pair + 1) * LANES) for j in range(3)]
    scale = HEAD_DIM**-0.5
    _, low, ones = half_masks(1.0)
    _, _, scaled = half_masks(scale)
    row = lax.broadcasted_iota(jnp.int32, (span, span), 0)
    col = lax.broadcasted_iota(jnp.int32, (span, span), 1)
    causal = col <= row
    for i in reversed(range(4)):
        past = i * span
        upto = past + span
        queries = qkv[past:upto, at[0]]
        keys = qkv[0:upto, at[1]]
        values = qkv[0:upto, at[2]]
        grads = dmix[past:upto, :]
        product = grads.astype(F32) * mixed[past:upto, at[0]]
        query = [queries * scaled[u] for u in range(2)]
        grad = [grads * ones[u] for u in range(2)]
        scores = [dot_cols(query[u], keys) for u in range(2)]
        pulls = [dot_cols(grad[u], values) for u in range(2)]
        halves, sums = [], {}
        for u in range(2):
            total = stats[past:upto, head + u : head + u + 1]
            delta = jnp.sum(jnp.where(low == (u == 0), product, 0.0), axis=-1, keepdims=True)
            half = None
            for rows in (slice(past, upto), slice(0, past))[: 2 if i else 1]:
                weights = jnp.exp(scores[u][:, rows] - total)
                if rows.start == past:
                    weights = jnp.where(causal, weights, 0.0)
                score_grad = (weights * (pulls[u][:, rows] - delta)).astype(BF)
                part = dot(score_grad, keys[rows])
                half = part if half is None else half + part
                for name, left, right in (("k", score_grad, query[u]), ("v", weights.astype(BF), grad[u])):
                    part = dot_rows(left, right)
                    sums[name, rows.start] = sums[name, rows.start] + part if u else part
            halves.append(half)
        for (name, start), part in sums.items():
            out = dk_sum if name == "k" else dv_sum
            rows = slice(start, upto if start == past else past)
            out[rows, :] = part if i == 3 else out[rows, :] + part
        dq[past:upto, :] = (jnp.where(low, halves[0], halves[1]) * scale).astype(BF)
    dk[...] = dk_sum[...].astype(BF)
    dv[...] = dv_sum[...].astype(BF)


def stage_rows(held, columns, value, stride):
    size = value.shape[0] // 4
    for k in range(4):
        held[k * stride : k * stride + size, columns] = value[k * size : (k + 1) * size, :]
        if stride > size:
            held[k * stride + size : (k + 1) * stride, columns] = jnp.zeros((stride - size, value.shape[1]), BF)


def place_cuts(cut, quarter, expert, held, outs, stride):
    for rel, out in enumerate(outs):
        first = jnp.bitwise_xor(quarter, rel) * stride
        for j in range(stride // cut):
            at = pl.multiple_of(first + jnp.bitwise_xor(expert, j) * cut, 16)
            out[j * cut : (j + 1) * cut, :] = held[pl.ds(at, cut), :]


def load_grads(place, pair, blocks, kept, dmix):
    span, group = blocks[0].shape[0], blocks[0].shape[1] - LANES
    at = slice(pair * LANES, (pair + 1) * LANES)
    for rel, block in enumerate(blocks):
        start = pl.multiple_of(jnp.bitwise_xor(place, rel) * span, span)
        late = dot(one_hot(block[:, group:], kept[rel].shape[0]), kept[rel][:, at])
        dmix[pl.ds(start, span), :] = (block[:, at].astype(F32) + late).astype(BF)


def weight_columns(attn_t, sources, weights, pair, held, first, stride):
    total, group = None, weights.shape[1] // 3
    grad = dot(attn_t[...], jnp.concatenate([source[...] for source in sources], axis=1))
    stage_rows(held, slice(first, first + 3 * LANES), grad.astype(BF), stride)
    for j in range(3):
        at = j * group + pair * LANES
        part = grad[:, j * LANES : (j + 1) * LANES] * weights[:, at : at + LANES].astype(F32)
        total = part if total is None else total + part
    return jnp.sum(total, axis=-1, keepdims=True)


def first_backward_body(cut, sc, *refs):
    base, late, rest = refs[:4], refs[4:8], refs[8:]
    qkv, mixed, attn_t, stats, weights, proj_own, proj_peer, attn_own, attn_peer, branch = rest[:10]
    dq, dk, dv, w0, w1, w2, w3, gain_sum, dmix, dk_sum, dv_sum, held = rest[10:]
    stride, group, core_late = w0.shape[0], proj_own.shape[1], late[1]
    load_grads(sc[0], 0, base, late, dmix)
    pair_backward(stats, 0, qkv, mixed, dmix, dq, dk, dv, dk_sum, dv_sum)
    core = sc[2]
    to = pl.multiple_of(core * group, LANES)
    rows = branch[:, pl.ds(to, group)]
    rows_peer = core_late[:, pl.ds(pl.multiple_of(3 * group + to, LANES), group)]
    mine = dot_rows(attn_own[...], rows) + dot_rows(core_late[:, 2 * group : 3 * group], rows_peer)
    others = dot_rows(attn_peer[...], rows) + dot_rows(core_late[:, group : 2 * group], rows_peer)
    both = jnp.concatenate([jnp.where(core == 0, mine, others), jnp.where(core == 0, others, mine)], axis=0)
    both = (proj_own[...].astype(F32) + proj_peer[...].astype(F32) + both).astype(BF)
    stage_rows(held, slice(0, group), both, stride)
    sums = weight_columns(attn_t, (dq, dk, dv), weights, 0, held, group, stride)
    gain_sum[...] = jnp.broadcast_to(sums, gain_sum.shape)
    place_cuts(cut, sc[3], sc[4], held, (w0, w1, w2, w3), stride)


def second_backward_body(pairs, cut, sc, *refs):
    base, late, rest = refs[:4], refs[4:8], refs[8:]
    qkv, mixed, attn_t, stats, weights, gain_sum, moe_row, router_rows = rest[:8]
    grads, rest = rest[8 : 8 + 3 * (pairs - 1)], rest[8 + 3 * (pairs - 1) :]
    outs, (dmix, dk_sum, dv_sum, held) = rest[:4], rest[4:]
    extra = router_rows.shape[0]
    stride = outs[0].shape[0] - extra
    sums = gain_sum[:, :1]
    for n in range(pairs - 1):
        own = grads[3 * n : 3 * n + 3]
        load_grads(sc[0], n + 1, base, late, dmix)
        pair_backward(stats, n + 1, qkv, mixed, dmix, *own, dk_sum, dv_sum)
        sums = sums + weight_columns(attn_t, own, weights, n + 1, held, 3 * LANES * n, stride)
    place_cuts(cut, sc[3], sc[4], held, outs, stride)
    row = lax.broadcasted_iota(jnp.int32, router_rows.shape, 0)
    gain_row = jnp.transpose(jnp.broadcast_to(sums, gain_sum.shape))[:1, :]
    small = jnp.where(row == 0, gain_row, jnp.where(row == 1, moe_row[...], router_rows[...])).astype(BF)
    for out in outs:
        out[stride:, :] = small


def norm_grad_body(sc, *refs):
    grads, (weights, rows_in, active, hidden_grad, val_grad, *outs) = refs[:-12], refs[-12:]
    own, sent, upper, lower, kept, in_grad, out_grad = outs
    span = own.shape[0]
    in_grad[...] = dot_rows(rows_in[...], hidden_grad[...])
    out_grad[...] = dot_rows(active[...], val_grad[...])
    for j in range(4):
        rows = pl.ds(pl.multiple_of(jnp.bitwise_xor(sc[0], j) * span, span), span)
        cols = [grads[n][rows, :] for part in range(3) for n in range(part, len(grads), 3)]
        grad = dot_cols(jnp.concatenate(cols, axis=1), weights[...]).astype(BF)
        if j == 3:
            upper[...] = grad[: span // 2]
            lower[...] = grad[span // 2 :]
        else:
            (own, sent, kept)[j][...] = grad


def proj_rows(sc, w_proj, group):
    return [
        w_proj[pl.ds(pl.multiple_of(jnp.bitwise_xor(sc[2], flip) * group, 16), group), :] for flip in range(2)
    ]


def prepare_body(
    sc, x, grads, routes, w_proj, wq, wk, wv, x_kept, tail, b00, b01, b10, b11, w_own, cols
):
    seqs, span, width = x.shape
    group, count = wq.shape[1], x_kept.shape[0]
    experts = count // SEAT
    for j, weight in enumerate((wq, wk, wv)):
        w_own[:, j * group : (j + 1) * group] = weight[...]
    proj_own, proj_peer = proj_rows(sc, w_proj, group)
    earlier = lax.broadcasted_iota(jnp.int32, (span, span), 0) < lax.broadcasted_iota(jnp.int32, (span, span), 1)
    earlier = jnp.where(earlier, 1.0, 0.0).astype(BF)
    ids = lax.broadcasted_iota(jnp.int32, (max(8, experts), span), 0)
    slots = lax.broadcasted_iota(jnp.int32, (count, span), 0)
    rows_of = lax.broadcasted_iota(jnp.int32, (LANES, span), 0)
    seen = jnp.zeros((max(8, experts), 1), F32)
    x_sum, tail_sum, flag_sum = None, None, None
    for n in range(seqs):
        route = routes[n : n + 1, :]
        mine = jnp.where(ids == route, 1.0, 0.0)
        before = dot(mine.astype(BF), earlier) + seen
        rank = jnp.sum(mine * before, axis=0, keepdims=True)
        seen = seen + jnp.sum(mine, axis=1, keepdims=True)
        limit = jnp.zeros((1, span), jnp.int32)
        for e in range(experts):
            limit = jnp.where(route == e, sc[7 + e], limit)
        kept = rank < limit.astype(F32)
        place = jnp.bitwise_xor(route, sc[4])
        seat = jnp.where(kept, place * SEAT + rank.astype(jnp.int32), -1)
        pick = jnp.where(slots == seat, 1.0, 0.0).astype(BF)
        live = jnp.where(sc[5 + n] == 1, F32(1.0), F32(0.0))
        table = jnp.where(rows_of == 0, jnp.where(kept, place.astype(F32), -1.0), 0.0)
        table = jnp.where(rows_of == 1, jnp.where(kept, rank, 0.0), table)
        table = jnp.where(rows_of == 2, live, table)
        table = jnp.where(rows_of == 3, jnp.where(kept, 0.0, 1.0), table)
        columns = jnp.transpose(table).astype(BF)
        cols[n] = columns
        parts = dot(pick, x[n]), dot(pick, grads[n]), dot(pick, columns)
        x_sum = parts[0] if n == 0 else x_sum + parts[0]
        tail_sum = parts[1] if n == 0 else tail_sum + parts[1]
        flag_sum = parts[2] if n == 0 else flag_sum + parts[2]
    x_kept[...] = x_sum.astype(BF)
    tail[:, :width] = tail_sum.astype(BF)
    tail[:, width:] = flag_sum.astype(BF)
    for rel, (own, peer) in enumerate(((b00, b01), (b10, b11))):
        at = jnp.bitwise_xor(sc[1], rel)
        own_cols = cols[at]
        rows = grads[at] * own_cols[:, 3:4]
        for out, weight in ((own, proj_own), (peer, proj_peer)):
            out[:, :group] = dot_cols(rows, weight).astype(BF)
            out[:, group:] = own_cols


def project_body(sc, k00, k01, k10, k11, x_kept, tail, w_proj, gain, after, own, peer, *boxes):
    own[...] = k00[...] + k10[...]
    peer[...] = k01[...] + k11[...]
    w_own, w_peer = proj_rows(sc, w_proj, own.shape[1])
    rows = x_kept[...].astype(F32) + (dot(own[...], w_own) + dot(peer[...], w_peer))
    after[...] = rows
    unit, _ = norm_parts(rows)
    moe_in = (unit * gain[...]).astype(BF)
    width = moe_in.shape[1]
    for j, box in enumerate(boxes):
        at = slice(j * SEAT, (j + 1) * SEAT)
        box[:, :width] = moe_in[at, :]
        box[:, width:] = tail[at, :]


def expert_body(sc, *refs):
    row_refs = refs[:8]
    router, w_in, w_out = refs[8:11]
    back_own, back_peer, rows, active, hidden_grad, val_grad, logit_grad = refs[11:]
    piece, width = row_refs[0].shape[0], rows.shape[1]
    expert = sc[4]
    for k, ref in enumerate(row_refs):
        rows[k * piece : (k + 1) * piece, :] = ref[:, :width]
    column = router[pl.ds(expert, 1), :]
    per = max(1, 512 // piece)
    for first in range(0, 8, per):
        here = slice(first * piece, (first + per) * piece)
        moe_in = rows[here, :]
        grads = jnp.concatenate([row_refs[k][:, width:] for k in range(first, first + per)], axis=0)
        live = grads[:, width + 2 : width + 3].astype(F32)
        grads = grads[:, :width].astype(F32)
        logit = jnp.sum(moe_in.astype(F32) * column, axis=-1, keepdims=True)
        gate = 1.0 / (1.0 + jnp.exp(-logit))
        value_grad = (gate * grads).astype(BF)
        hidden = dot(moe_in, w_in[...])
        bent = 0.5 * (1.0 + lax.erf(hidden * (0.5**0.5)))
        act = (hidden * bent).astype(BF)
        slope = bent + hidden * jnp.exp(-0.5 * hidden * hidden) * ((2.0 * jnp.pi) ** -0.5)
        pulled = (slope * dot_cols(value_grad, w_out[...])).astype(BF)
        part = dot(act, w_out[...])
        logit_part = jnp.sum(part * grads, axis=-1, keepdims=True) * (gate * (1.0 - gate) * live)
        back = (dot_cols(pulled, w_in[...]) + logit_part * column).astype(BF)
        value = (gate * part).astype(BF)
        active[here, :] = act
        hidden_grad[here, :] = pulled
        val_grad[here, :] = value_grad
        lane = lax.broadcasted_iota(jnp.int32, (logit_part.shape[0], LANES), 1)
        logit_grad[here, :] = jnp.where(lane == expert + 2, logit_part, 0.0).astype(BF)
        for k in range(first, first + per):
            at = slice((k - first) * piece, (k - first + 1) * piece)
            to = slice((k % 4) * piece, (k % 4 + 1) * piece)
            out = back_own if k < 4 else back_peer
            out[to, :width] = back[at, :]
            out[to, width:] = value[at, :]


def return_body(sc, back, after, tail, attn_own, attn_peer, gain, w_proj, mid, branch, gain_row, own, far, core):
    width = after.shape[1]
    upstream = back[:, :width].astype(F32)
    unit, scaling = norm_parts(after[...])
    gain_row[...] = jnp.sum(upstream * unit, axis=0, keepdims=True)
    total = tail[:, :width].astype(F32) + norm_pull(upstream * gain[...], unit, scaling)
    mid[...] = total
    low = total.astype(BF)
    branch[...] = low
    group = own.shape[1]
    w_own, w_peer = proj_rows(sc, w_proj, group)
    own[...] = dot_cols(low, w_own).astype(BF)
    pulled = dot_cols(low, w_peer).astype(BF)
    far[...] = pulled
    core[:, :group] = pulled
    core[:, group : 2 * group] = attn_own[...]
    core[:, 2 * group : 3 * group] = attn_peer[...]
    core[:, 3 * group :] = low


def projection_grad_body(
    sc, a00, a01, a10, a11, grads, cols, expert_rows, logit_grad, attn_in, own, peer, router_rows, attn_t, rows
):
    attn_t[...] = jnp.transpose(attn_in[...])
    router_rows[...] = dot_rows(logit_grad[...], expert_rows[...])[: router_rows.shape[0], :]
    span, group = a00.shape
    core = sc[2]
    for rel in range(2):
        at = jnp.bitwise_xor(sc[1], rel)
        rows[rel] = grads[at] * cols[at][:, 3:4]
    for half, out in enumerate((own, peer)):
        to = pl.ds(pl.multiple_of(jnp.bitwise_xor(core, half) * group, LANES), group)
        cut0, cut1 = rows[0, :, to], rows[1, :, to]
        for kind, (first, second) in enumerate(((a00, a10), (a01, a11))):
            at = pl.multiple_of(jnp.bitwise_xor(core, kind) * group, 16)
            total = dot_rows(first[:span, :], cut0) + dot_rows(second[...], cut1)
            out[pl.ds(at, group), :] = total.astype(BF)


def place_column(sc, cut, stride, parts, column, out):
    size = out.shape[0] // 4
    for rel, (part, offset) in enumerate(parts):
        first = jnp.bitwise_xor(sc[3], rel) * size
        for j in range(stride // cut):
            place = jnp.bitwise_xor(sc[4], j) * cut
            value = part[offset + j * cut : offset + (j + 1) * cut, pl.ds(column, LANES)].astype(F32)

            def store(place=place, value=value, first=first):
                out[pl.ds(pl.multiple_of(first + place, 16), cut), :] = value

            if stride > size:
                pl.when(place < size)(store)
            else:
                store()


def spread_proj_body(cut, sc, *refs):
    own, peer, out = refs[:4], refs[4], refs[5]
    step = pl.program_id(0)
    stride = own[0].shape[0]
    parts = [(ref, 0) for ref in own] + [(peer, rel * stride) for rel in range(4)]

    def write(side):
        place_column(sc, cut, stride, parts[4 * side : 4 * side + 4], pl.multiple_of(step % 3 * LANES, LANES), out)

    for side in range(2):
        pl.when(step // 3 == side)(functools.partial(write, side))


def spread_body(cut, group, pairs, sc, *refs):
    own, peer, second, out = refs[:4], refs[4], refs[5:13], refs[13]
    core, expert = sc[2], sc[4]
    size = out.shape[0]
    stride = own[0].shape[0]

    def write(rel):
        for half in range(2):
            side = jnp.bitwise_xor(core, half) * group
            first, offset = (peer, rel * stride) if half else (own[rel], 0)
            rest = second[4 * half + rel]
            for j in range(stride // cut):
                place = jnp.bitwise_xor(expert, j) * cut

                def store(place=place, j=j, side=side, first=first, offset=offset, rest=rest):
                    rows = pl.ds(pl.multiple_of(place, 16), cut)
                    for pair in range(pairs):
                        ref, start = (rest, j * cut) if pair else (first, offset + j * cut)
                        base = 3 * LANES * (pair - 1) if pair else group
                        for part in range(3):
                            at = base + part * LANES
                            to = pl.multiple_of(side + pair * LANES + 2 * part * group, LANES)
                            out[rows, pl.ds(to, LANES)] = ref[start : start + cut, at : at + LANES].astype(F32)

                if stride > size:
                    pl.when(place < size)(store)
                else:
                    store()

    for rel in range(4):
        pl.when(pl.program_id(0) == rel)(functools.partial(write, rel))


def small_body(experts, first, sc, own, peer, gain, attn_gain, moe_gain, router):
    rows = own[...].astype(F32) + peer[first : first + own.shape[0], :].astype(F32)
    attn_gain[...] = (rows[:1, :] / gain[...])[0]
    moe_gain[...] = rows[1]
    router[...] = rows[2 : 2 + experts, :]


def input_body(first, sc, x, grads, cols, mid, first_own, peer, second, gain, out):
    high = mid[...].astype(BF)
    rest = (mid[...] - high.astype(F32)).astype(BF)
    for rel in range(2):
        if rel == 0:
            upstream = first_own[...].astype(F32) + peer[first : first + first_own.shape[0], :].astype(F32)
        else:
            upstream = second[...].astype(F32)
        at = jnp.bitwise_xor(sc[1], rel)
        own_cols = cols[at]
        pick = one_hot(own_cols, mid.shape[0])
        total = (grads[at] * own_cols[:, 3:4]).astype(F32) + (dot(pick, high) + dot(pick, rest))
        unit, scaling = norm_parts(x[at].astype(F32))
        out[at] = (total + norm_pull(upstream * gain[...], unit, scaling)).astype(BF)


def pack_body(sc, *refs):
    at = 0
    for part in refs[:-1]:
        refs[-1][at : at + part.shape[0], :] = part[...]
        at += part.shape[0]


def output_body(sc, a00, a01, a10, a11, x, w_proj, cols, values, out):
    span, width = x.shape[1:]
    w_own, w_peer = proj_rows(sc, w_proj, a00.shape[1])
    for rel, (own, peer) in enumerate(((a00, a01), (a10, a11))):
        at = jnp.bitwise_xor(sc[1], rel)
        rows = x[at].astype(F32) + (dot(own[:span, :], w_own) + dot(peer[:span, :], w_peer))
        pick = one_hot(cols[at], values.shape[0])
        out[at] = (rows + dot(pick, values[:, width:])).astype(BF)


def local(
    blk_count,
    batch_count,
    x,
    gain_one,
    w_qkv,
    w_proj,
    gain_two,
    router,
    w_in,
    w_out,
    routes,
    quota,
    period,
    g,
):
    seq_count, span, width = x.shape
    group = width // 2
    experts = quota.shape[0]
    share = batch_count // experts
    assert blk_count == 4 and seq_count == 2 and share == 2
    blk, batch = lax.axis_index("blk"), lax.axis_index("batch")
    chip, core = blk // 2, blk % 2
    expert, half = batch // share, batch % share
    quarter = chip * 2 + half
    sc = jnp.concatenate([jnp.stack([blk, chip, core, quarter, expert]).astype(jnp.int32), period, quota])

    def to_blk(value, bits):
        return lax.ppermute(value, "blk", [(i, i ^ bits) for i in range(4)])

    def to_batch(value, bits):
        return lax.ppermute(value, "batch", [(i, i ^ bits) for i in range(batch_count)])

    def to_expert(value, bits):
        return to_batch(value, bits * share)

    def to_plane(value, rel):
        if rel == 1:
            return to_batch(value, 1)
        if rel == 2:
            return to_blk(value, 2)
        pairs = [
            (i * batch_count + j, (i ^ 2) * batch_count + (j ^ 1)) for i in range(4) for j in range(batch_count)
        ]
        return lax.ppermute(value, ("blk", "batch"), pairs)

    def third(j):
        return (w_qkv, (width, group), lambda s: (0, 2 * j + s[2]))

    mine = lax.dynamic_index_in_dim(x, chip, 0, keepdims=False)
    other = lax.dynamic_index_in_dim(x, 1 - chip, 0, keepdims=False)
    block_x = to_blk(other, 2)
    block_c = to_blk(mine, 1)

    gain_one_row, gain_two_row = gain_one.reshape(1, width), gain_two.reshape(1, width)

    seat_rows = experts * SEAT
    length = 4 * span
    piece = shape_of((span, group), BF)
    base_piece = shape_of((span, group + LANES), BF)
    kept_piece = shape_of((seat_rows, group), BF)
    kept_rows = shape_of((seat_rows, width), BF)
    x_kept, tail, b00, b01, b10, b11, w_own, cols = run_kernel(
        prepare_body,
        sc,
        [x, g, routes, w_proj, third(0), third(1), third(2)],
        [
            kept_rows,
            shape_of((seat_rows, width + LANES), BF),
            base_piece,
            base_piece,
            base_piece,
            base_piece,
            shape_of((width, 3 * group), BF),
            shape_of((seq_count, span, LANES), BF),
        ],
        name="prepare",
    )
    block_x, b01, b10, b11 = together([block_x, b01, b10, b11])
    base = [b00, to_blk(b01, 1), to_blk(b10, 2), to_blk(b11, 3)]
    block_xc = to_blk(block_x, 1)
    attn_in, qkv, mixed, stats, own0, own1, own2, own3 = run_kernel(
        forward_body,
        sc,
        [mine, block_c, block_x, block_xc, gain_one_row, w_own],
        [
            shape_of((length, width), BF),
            shape_of((length, 3 * group), BF),
            shape_of((length, group), F32),
            shape_of((length, LANES), F32),
            piece,
            piece,
            piece,
            piece,
        ],
        [pltpu.VMEM((4, span, group), BF)],
        name="attention_forward",
    )
    kept0, core_rows, kept2, kept3 = run_kernel(
        pick_body,
        sc,
        [own0, own1, own2, own3, *base],
        [kept_piece, shape_of((span + seat_rows, group), BF), kept_piece, kept_piece],
        name="pick_kept",
    )
    core_rows = to_blk(core_rows, 1)
    late = [kept0, core_rows, to_blk(kept2, 2), to_blk(kept3, 3)]
    own2, own3, *late = together([own2, own3, *late])
    core_rows = late[1]
    a10, a11 = to_blk(own2, 2), to_blk(own3, 3)
    row_box = shape_of((SEAT, 2 * width + LANES), BF)
    after_kept, attn_own, attn_peer, *boxes = run_kernel(
        project_body,
        sc,
        [
            kept0,
            (core_rows, (seat_rows, group), lambda s: (span // seat_rows, 0)) if span % seat_rows == 0 else core_rows[span:],
            *late[2:],
            x_kept,
            tail,
            w_proj,
            gain_two_row,
        ],
        [shape_of((seat_rows, width), F32), kept_piece, kept_piece] + [row_box] * experts,
        name="project",
    )

    parts = [boxes[0]] + [to_expert(boxes[j], j) for j in range(1, experts)]
    rows = jnp.concatenate(together([*parts, a10, a11])[:experts], axis=0)
    expert_rows = [rows] + [to_plane(rows, rel) for rel in (1, 2, 3)]
    expert_rows += [to_blk(part, 1) for part in expert_rows]
    total_rows = 8 * seat_rows
    hidden_units = w_in.shape[2]
    quad = shape_of((4 * seat_rows, 2 * width), BF)
    back_own, back_peer, rows, active, hidden_grad, val_grad, logit_grad = run_kernel(
        expert_body,
        sc,
        [*expert_rows, router.T.astype(F32), w_in[0], w_out[0]],
        [
            quad,
            quad,
            shape_of((total_rows, width), BF),
            shape_of((total_rows, hidden_units), BF),
            shape_of((total_rows, hidden_units), BF),
            shape_of((total_rows, width), BF),
            shape_of((total_rows, LANES), BF),
        ],
        name="expert",
    )
    def total_of(parts):
        parts = [part.astype(F32) for part in parts]
        while len(parts) > 1:
            parts = [left + right for left, right in zip(parts[::2], parts[1::2])]
        return parts[0].astype(BF)

    arrived = to_blk(back_peer, 1)
    parts = []
    for rel in range(4):
        at = slice(rel * seat_rows, (rel + 1) * seat_rows)
        part = total_of([back_own[at], arrived[at]])
        parts.append(part if rel == 0 else to_plane(part, rel))
    parts = together(parts)
    cuts = [total_of([part[j * SEAT : (j + 1) * SEAT] for part in parts]) for j in range(experts)]
    back = jnp.concatenate(together([cuts[0]] + [to_expert(cuts[j], j) for j in range(1, experts)]), axis=0)

    extra = -(-(experts + 2) // 16) * 16
    proj_own, proj_peer, router_rows, attn_t = run_kernel(
        projection_grad_body,
        sc,
        [own0, core_rows, a10, a11, g, cols, rows, logit_grad, attn_in],
        [shape_of((width, group), BF)] * 2 + [shape_of((extra, width), F32), shape_of((width, length), BF)],
        [pltpu.VMEM((seq_count, span, width), BF)],
        name="projection_grad",
        after=[back_own],
    )
    proj_arrived = to_blk(proj_peer, 1)
    wide_cols = shape_of((width, LANES), F32)
    mid, branch, moe_row, m_own, m_far, m_core = run_kernel(
        return_body,
        sc,
        [back, after_kept, tail, attn_own, attn_peer, gain_two_row, w_proj],
        [
            shape_of((seat_rows, width), F32),
            kept_rows,
            shape_of((1, width), F32),
            kept_piece,
            kept_piece,
            shape_of((seat_rows, 3 * group + width), BF),
        ],
        name="return_rows",
        after=[router_rows, proj_arrived],
    )
    mix_late = [m_own, to_blk(m_core, 1), to_blk(m_own, 2), to_blk(m_far, 3)]

    size = width // 4
    cut = -(-size // (experts * 16)) * 16
    stride = experts * cut

    def scatter_plane(quarters):
        return [quarters[0]] + [to_plane(quarters[rel], rel) for rel in (1, 2, 3)]

    def sum_cuts(parts):
        return [total_of([part[j * cut : (j + 1) * cut] for part in parts]) for j in range(experts)]

    def sum_experts(cuts):
        return total_of(together([cuts[0]] + [to_expert(cuts[j], j) for j in range(1, experts)]))

    def halve_experts(cuts, bits, far):
        return [total_of([near, far[j * cut : (j + 1) * cut]]) for j, near in enumerate(cuts[:bits])]

    def far_cuts(cuts, bits):
        return to_expert(jnp.concatenate(cuts[bits:], axis=0), bits)

    def gather_experts(whole, before=()):
        parts = [whole] + [to_expert(whole, j) for j in range(1, experts)]
        return jnp.concatenate(together([*parts, *before])[:experts], axis=0)

    def gather_plane(column):
        return [column] + [to_plane(column, rel) for rel in (1, 2, 3)]


    pairs = group // LANES
    tall = shape_of((length, LANES), BF)
    working = [
        pltpu.VMEM((length, LANES), BF),
        pltpu.VMEM((length, LANES), F32),
        pltpu.VMEM((length, LANES), F32),
    ]
    wide_one = group + 3 * LANES
    wide_two = 3 * LANES * (pairs - 1)
    operands = [*base, *mix_late, qkv, mixed, attn_t, stats, w_own]
    dq, dk, dv, *quarters_one, gain_sum = run_kernel(
        functools.partial(first_backward_body, cut),
        sc,
        [*operands, proj_own, proj_arrived, attn_own, attn_peer, branch],
        [tall, tall, tall] + [shape_of((stride, wide_one), BF)] * 4 + [wide_cols],
        working + [pltpu.VMEM((4 * stride, wide_one), BF)],
        name="attention_backward_one",
    )
    parts_one = scatter_plane(quarters_one)
    *grads, t0, t1, t2, t3 = run_kernel(
        functools.partial(second_backward_body, pairs, cut),
        sc,
        [*operands, gain_sum, moe_row, router_rows],
        [tall] * (3 * (pairs - 1)) + [shape_of((stride + extra, wide_two), BF)] * 4,
        working + [pltpu.VMEM((4 * stride, wide_two), BF)],
        name="attention_backward_two",
    )
    t1, t2, t3, *parts_one = together([t1, t2, t3, *parts_one])
    parts_two = scatter_plane([t0, t1, t2, t3])
    cuts_one, bits = sum_cuts(parts_one), experts // 2
    far = far_cuts(cuts_one, bits)
    part = shape_of((span, width), BF)
    near_piece = shape_of((span // 2, width), BF)
    first_own, sent, upper, lower, near, in_grad, out_grad = run_kernel(
        norm_grad_body,
        sc,
        [dq, dk, dv, *grads, w_own, rows, active, hidden_grad, val_grad],
        [
            part,
            part,
            near_piece,
            near_piece,
            part,
            shape_of((width, hidden_units), F32),
            shape_of((hidden_units, width), F32),
        ],
        name="norm_one_grad",
        flops=10e9,
    )
    upper, lower = to_blk(upper, 1), to_blk(lower, 1)
    *parts_two, out_grad = together([*parts_two, out_grad])
    upper, lower, *parts_two = together([upper, lower, *parts_two])
    second = to_blk(total_of([near, jnp.concatenate([upper, lower], axis=0)]), 2)
    while bits:
        cuts_one = halve_experts(cuts_one, bits, far)
        bits //= 2
        if bits:
            far = far_cuts(cuts_one, bits)
        if bits == 1:
            far, *_ = together([far, *parts_two])
    whole_one = cuts_one[0]
    column_one = gather_experts(whole_one, [second])
    small = total_of([part[stride:] for part in parts_two])
    whole_two = sum_experts([jnp.concatenate([piece, small], axis=0) for piece in sum_cuts(parts_two)])
    whole_two, small = whole_two[:cut], whole_two[cut:]
    one = gather_plane(column_one)
    sent, small, column_two, *one = together([sent, small, gather_experts(whole_two), *one])
    two = gather_plane(column_two)
    packed = [*one, small, sent]
    packed_rows = sum(part.shape[0] for part in packed)
    (pack,) = run_kernel(pack_body, sc, packed, [shape_of((packed_rows, width), BF)], name="pack")
    output = run_kernel(
        output_body,
        sc,
        [own0, core_rows, a10, a11, x, w_proj, cols, back],
        [shape_of(x.shape, BF)],
        name="output",
        after=[pack],
    )[0]
    pack = to_blk(pack, 1)
    input_grad = run_kernel(
        functools.partial(input_body, packed_rows - span),
        sc,
        [x, g, cols, mid, first_own, pack, second, gain_one_row],
        [shape_of(x.shape, BF)],
        name="input_grad",
    )[0]
    attn_gain, moe_gain, router_grad = run_kernel(
        functools.partial(small_body, experts, 4 * stride),
        sc,
        [small, pack, gain_one_row],
        [shape_of((width,), F32), shape_of((width,), F32), shape_of((experts, width), F32)],
        name="small_grads",
    )

    def grid_kernel(body, steps, arrays, out, block, index, name):
        return pl.pallas_call(
            body,
            grid_spec=pltpu.PrefetchScalarGridSpec(
                num_scalar_prefetch=1,
                grid=(steps,),
                in_specs=[pl.BlockSpec(memory_space=pltpu.VMEM)] * len(arrays),
                out_specs=pl.BlockSpec(block, index),
            ),
            out_shape=out,
            compiler_params=pltpu.CompilerParams(vmem_limit_bytes=28 * 1024 * 1024),
            name=name,
        )(sc, *arrays)

    proj_grad = grid_kernel(
        functools.partial(spread_proj_body, cut),
        6,
        [*one, pack],
        shape_of((width, width), F32),
        (width, LANES),
        lambda i, s: (0, jnp.bitwise_xor(s[2], i // 3) * pairs + i % 3),
        "spread_proj",
    )
    *two, output, input_grad, proj_grad, attn_gain = together([*two, output, input_grad, proj_grad, attn_gain])
    qkv_grad = grid_kernel(
        functools.partial(spread_body, cut, group, pairs),
        4,
        [*one, pack, *two, *[to_blk(part, 1) for part in two]],
        shape_of((width, 3 * width), F32),
        (size, 3 * width),
        lambda i, s: (jnp.bitwise_xor(s[3], i), 0),
        "spread",
    )
    return (
        output,
        input_grad,
        attn_gain,
        qkv_grad,
        proj_grad,
        moe_gain,
        router_grad.T,
        in_grad[None],
        out_grad[None],
    )


def solution(mesh):
    rows, kept = P("batch", "blk", None), P()
    w_in, w_out = P("batch", None, "blk"), P("batch", "blk", None)
    return jax.shard_map(
        functools.partial(local, mesh.shape["blk"], mesh.shape["batch"]),
        mesh=mesh,
        in_specs=(rows, kept, kept, kept, kept, kept, w_in, w_out, P("batch", "blk"), kept, P("batch"), rows),
        out_specs=(rows, rows, kept, kept, kept, kept, kept, w_in, w_out),
        check_vma=False,
    )
```

```python
import functools
import math

import jax
import jax.numpy as jnp
from jax import lax
from jax.experimental import pallas as pl
from jax.experimental.pallas import tpu as pltpu
from jax.sharding import PartitionSpec as P

HEAD_DIM = 64
CAP = 12
SEAT = 16
LANES = 128
EPSILON = 1e-05
FAR_BELOW = -1e30
BF = jnp.bfloat16
F32 = jnp.float32


def dot(left, right):
    return jnp.dot(left, right, preferred_element_type=F32)


def dot_rows(left, right):
    return lax.dot_general(left, right, (((0,), (0,)), ((), ())), preferred_element_type=F32)


def dot_cols(left, right):
    return lax.dot_general(left, right, (((1,), (1,)), ((), ())), preferred_element_type=F32)


def norm_parts(rows):
    centred = rows - jnp.mean(rows, axis=-1, keepdims=True)
    scaling = lax.rsqrt(jnp.mean(centred * centred, axis=-1, keepdims=True) + EPSILON)
    return centred * scaling, scaling


def norm_pull(scaled, unit, scaling):
    return scaling * (
        scaled
        - jnp.mean(scaled, axis=-1, keepdims=True)
        - unit * jnp.mean(scaled * unit, axis=-1, keepdims=True)
    )


def run_kernel(body, scalars, operands, outs, scratch=(), flops=0, name=None, after=()):
    specs, arrays, held = [], [], 0
    after, given, run = list(after), len(operands), body
    if after:

        def run(sc, *refs):
            body(sc, *refs[:given], *refs[given + len(after) :])

    for operand in operands:
        if isinstance(operand, tuple):
            array, block, index = operand
            held += 2 * math.prod(block) * array.dtype.itemsize
            specs.append(pl.BlockSpec(block, functools.partial(lambda i, s, fn: fn(s), fn=index)))
        else:
            array = operand
            held += array.size * array.dtype.itemsize
            specs.append(pl.BlockSpec(memory_space=pltpu.VMEM))
        arrays.append(array)
    specs += [pl.BlockSpec(memory_space=pl.ANY)] * len(after)
    held += sum(out.size * out.dtype.itemsize for out in outs)
    out_specs = [pl.BlockSpec(memory_space=pltpu.VMEM) for _ in outs]
    return pl.pallas_call(
        run,
        grid_spec=pltpu.PrefetchScalarGridSpec(
            num_scalar_prefetch=1,
            grid=(1,),
            in_specs=specs,
            out_specs=out_specs,
            scratch_shapes=list(scratch),
        ),
        out_shape=list(outs),
        compiler_params=pltpu.CompilerParams(vmem_limit_bytes=(16 if held < 24e6 else 60) * 1024 * 1024),
        cost_estimate=pl.CostEstimate(flops=int(flops), bytes_accessed=0, transcendentals=0),
        name=name,
    )(scalars, *arrays, *after)


def together(values):
    return list(lax.optimization_barrier(tuple(values)))


def shape_of(dims, dtype):
    return jax.ShapeDtypeStruct(dims, dtype)


def half_masks(scale):
    lane = lax.broadcasted_iota(jnp.int32, (1, LANES), 1)
    low = lane < HEAD_DIM
    return lane, low, (jnp.where(low, scale, 0.0).astype(BF), jnp.where(low, 0.0, scale).astype(BF))


def one_hot(cols, count):
    seat = cols[:, :1].astype(F32) * SEAT + cols[:, 1:2].astype(F32)
    slot = lax.broadcasted_iota(jnp.int32, (cols.shape[0], count), 1).astype(F32)
    return jnp.where(slot == seat, 1.0, 0.0).astype(BF)


def one_hot_rows(block, span, count):
    seat = block[span : span + 1, :span].astype(F32) * SEAT + block[span + 1 : span + 2, :span].astype(F32)
    slot = lax.broadcasted_iota(jnp.int32, (count, span), 0).astype(F32)
    return jnp.where(slot == seat, 1.0, 0.0).astype(BF)


def forward_body(
    sc, m0, m1, m2, m3, gain, weights, attn_in, qkv, mixed, stats, o0, o1, o2, o3, p0, p1, p2, p3, pieces
):
    powers = (p0, p1, p2, p3)
    span, group = m2.shape[0], weights.shape[1] // 3
    place = sc[0]
    for rel, block in enumerate((m0, m1, m2, m3)):
        start = pl.multiple_of(jnp.bitwise_xor(place, rel) * span, span)
        unit, _ = norm_parts(block[...].astype(F32))
        normed = (unit * gain[...]).astype(BF)
        attn_in[pl.ds(start, span), :] = normed
        qkv[pl.ds(start, span), :] = dot(normed, weights[...]).astype(BF)
    lane, low, scaled = half_masks(HEAD_DIM**-0.5)
    row = jnp.bitwise_and(lax.broadcasted_iota(jnp.int32, (2 * span, span), 0), span - 1)
    col = lax.broadcasted_iota(jnp.int32, (2 * span, span), 1)
    causal = col <= row
    for i in range(4):
        past = i * span
        upto = past + span
        stat = jnp.zeros((span, LANES), F32)
        for g in range(group // LANES):
            at = g * LANES
            queries = qkv[past:upto, at : at + LANES]
            keys = qkv[0:upto, group + at : group + at + LANES]
            values = qkv[0:upto, 2 * group + at : 2 * group + at + LANES]
            both = jnp.concatenate([queries * scaled[0], queries * scaled[1]], axis=0)
            last = jnp.where(causal, dot_cols(both, keys[past:]), FAR_BELOW)
            top = jnp.max(last, axis=-1, keepdims=True)
            if i:
                first = dot_cols(both, keys[:past])
                top = jnp.maximum(top, jnp.max(first, axis=-1, keepdims=True))
            beside = jnp.concatenate([values, jnp.ones_like(values)], axis=1)
            raised = jnp.exp(last - top).astype(BF)
            powers[i][g, :, past:] = raised
            mix = dot(raised, beside[past:])
            if i:
                raised = jnp.exp(first - top).astype(BF)
                powers[i][g, :, :past] = raised
                mix = mix + dot(raised, beside[:past])
            scale = 1.0 / mix[:, LANES:]
            mix = mix[:, :LANES] * scale
            mix = jnp.where(low, mix[:span], mix[span:])
            for u in range(2):
                stat = jnp.where(lane == 2 * g + u, scale[u * span : (u + 1) * span], stat)
            mixed[past:upto, at : at + LANES] = mix
            pieces[jnp.bitwise_xor(place, i), :, at : at + LANES] = mix.astype(BF)
        stats[past:upto, :] = stat
    for rel, out in enumerate((o0, o1, o2, o3)):
        out[...] = pieces[rel]


def pick_body(sc, o0, o1, o2, o3, b0, b1, b2, b3, k0, core, k2, k3):
    span, group = o0.shape
    for out, rows, base in ((k0, o0, b0), (core, o1, b1), (k2, o2, b2), (k3, o3, b3)):
        kept = dot(one_hot_rows(base, span, k0.shape[0]), rows[...]).astype(BF)
        if out is core:
            core[:span, :] = rows[...]
            core[span:, :] = kept
        else:
            out[...] = kept


def pair_backward(stats, pair, qkv, mixed, powers, dmix, dq, dk, dv, dk_sum, dv_sum):
    span, group, head = qkv.shape[0] // 4, qkv.shape[1] // 3, 2 * pair
    at = [slice(j * group + pair * LANES, j * group + (pair + 1) * LANES) for j in range(3)]
    scale = HEAD_DIM**-0.5
    _, low, ones = half_masks(1.0)
    _, _, scaled = half_masks(scale)
    for i in reversed(range(4)):
        past = i * span
        upto = past + span
        queries = qkv[past:upto, at[0]]
        keys = qkv[0:upto, at[1]]
        values = qkv[0:upto, at[2]]
        over = jnp.where(low, stats[past:upto, head : head + 1], stats[past:upto, head + 1 : head + 2])
        grads = (dmix[past:upto, :].astype(F32) * over).astype(BF)
        product = grads.astype(F32) * mixed[past:upto, at[0]]
        query = [queries * scaled[u] for u in range(2)]
        grad = [grads * ones[u] for u in range(2)]
        pulls = [dot_cols(grad[u], values) for u in range(2)]
        halves, sums = [], {}
        for u in range(2):
            delta = jnp.sum(jnp.where(low == (u == 0), product, 0.0), axis=-1, keepdims=True)
            half = None
            for rows in (slice(past, upto), slice(0, past))[: 2 if i else 1]:
                weights = powers[i][pair, u * span : (u + 1) * span, rows]
                score_grad = (weights.astype(F32) * (pulls[u][:, rows] - delta)).astype(BF)
                part = dot(score_grad, keys[rows])
                half = part if half is None else half + part
                for name, left, right in (("k", score_grad, query[u]), ("v", weights, grad[u])):
                    part = dot_rows(left, right)
                    sums[name, rows.start] = sums[name, rows.start] + part if u else part
            halves.append(half)
        for (name, start), part in sums.items():
            out = dk_sum if name == "k" else dv_sum
            rows = slice(start, upto if start == past else past)
            out[rows, :] = part if i == 3 else out[rows, :] + part
        dq[past:upto, :] = (jnp.where(low, halves[0], halves[1]) * scale).astype(BF)
    dk[...] = dk_sum[...].astype(BF)
    dv[...] = dv_sum[...].astype(BF)


def stage_rows(held, columns, value, stride):
    size = value.shape[0] // 4
    for k in range(4):
        held[k * stride : k * stride + size, columns] = value[k * size : (k + 1) * size, :]
        if stride > size:
            held[k * stride + size : (k + 1) * stride, columns] = jnp.zeros((stride - size, value.shape[1]), BF)


def place_cuts(cut, quarter, expert, held, outs, stride):
    for rel, out in enumerate(outs):
        first = jnp.bitwise_xor(quarter, rel) * stride
        for j in range(stride // cut):
            at = pl.multiple_of(first + jnp.bitwise_xor(expert, j) * cut, 16)
            out[j * cut : (j + 1) * cut, :] = held[pl.ds(at, cut), :]


def load_grads(place, pair, blocks, kept, dmix):
    span = dmix.shape[0] // 4
    at = slice(pair * LANES, (pair + 1) * LANES)
    for rel, block in enumerate(blocks):
        start = pl.multiple_of(jnp.bitwise_xor(place, rel) * span, span)
        late = dot_rows(one_hot_rows(block, span, kept[rel].shape[0]), kept[rel][:, at])
        dmix[pl.ds(start, span), :] = (block[:span, at].astype(F32) + late).astype(BF)


def weight_columns(attn_t, sources, weights, pair, held, first, stride):
    total, group = None, weights.shape[1] // 3
    grad = dot(attn_t[...], jnp.concatenate([source[...] for source in sources], axis=1))
    stage_rows(held, slice(first, first + 3 * LANES), grad.astype(BF), stride)
    for j in range(3):
        at = j * group + pair * LANES
        part = grad[:, j * LANES : (j + 1) * LANES] * weights[:, at : at + LANES].astype(F32)
        total = part if total is None else total + part
    return jnp.sum(total, axis=-1, keepdims=True)


def first_backward_body(cut, sc, *refs):
    base, late, powers, rest = refs[:4], refs[4:8], refs[8:12], refs[12:]
    qkv, mixed, attn_t, stats, weights, proj_own, proj_peer, attn_own, attn_peer, branch = rest[:10]
    dq, dk, dv, w0, w1, w2, w3, gain_sum, dmix, dk_sum, dv_sum, held = rest[10:]
    stride, group, core_late = w0.shape[0], proj_own.shape[1], late[1]
    load_grads(sc[0], 0, base, late, dmix)
    pair_backward(stats, 0, qkv, mixed, powers, dmix, dq, dk, dv, dk_sum, dv_sum)
    core = sc[2]
    to = pl.multiple_of(core * group, LANES)
    rows = branch[:, pl.ds(to, group)]
    rows_peer = core_late[:, pl.ds(pl.multiple_of(3 * group + to, LANES), group)]
    mine = dot_rows(attn_own[...], rows) + dot_rows(core_late[:, 2 * group : 3 * group], rows_peer)
    others = dot_rows(attn_peer[...], rows) + dot_rows(core_late[:, group : 2 * group], rows_peer)
    both = jnp.concatenate([jnp.where(core == 0, mine, others), jnp.where(core == 0, others, mine)], axis=0)
    both = (proj_own[...].astype(F32) + proj_peer[...].astype(F32) + both).astype(BF)
    stage_rows(held, slice(0, group), both, stride)
    sums = weight_columns(attn_t, (dq, dk, dv), weights, 0, held, group, stride)
    gain_sum[...] = jnp.broadcast_to(sums, gain_sum.shape)
    place_cuts(cut, sc[3], sc[4], held, (w0, w1, w2, w3), stride)


def second_backward_body(pairs, cut, sc, *refs):
    base, late, powers, rest = refs[:4], refs[4:8], refs[8:12], refs[12:]
    qkv, mixed, attn_t, stats, weights, gain_sum, moe_row, router_rows = rest[:8]
    grads, rest = rest[8 : 8 + 3 * (pairs - 1)], rest[8 + 3 * (pairs - 1) :]
    outs, (dmix, dk_sum, dv_sum, held) = rest[:4], rest[4:]
    extra = router_rows.shape[0]
    stride = outs[0].shape[0] - extra
    sums = gain_sum[:, :1]
    for n in range(pairs - 1):
        own = grads[3 * n : 3 * n + 3]
        load_grads(sc[0], n + 1, base, late, dmix)
        pair_backward(stats, n + 1, qkv, mixed, powers, dmix, *own, dk_sum, dv_sum)
        sums = sums + weight_columns(attn_t, own, weights, n + 1, held, 3 * LANES * n, stride)
    place_cuts(cut, sc[3], sc[4], held, outs, stride)
    row = lax.broadcasted_iota(jnp.int32, router_rows.shape, 0)
    gain_row = jnp.transpose(jnp.broadcast_to(sums, gain_sum.shape))[:1, :]
    small = jnp.where(row == 0, gain_row, jnp.where(row == 1, moe_row[...], router_rows[...])).astype(BF)
    for out in outs:
        out[stride:, :] = small


def norm_grad_body(sc, *refs):
    grads, (weights, rows_in, active, hidden_grad, val_grad, *outs) = refs[:-12], refs[-12:]
    own, sent, upper, lower, kept, in_grad, out_grad = outs
    span = own.shape[0]
    in_grad[...] = dot_rows(rows_in[...], hidden_grad[...])
    out_grad[...] = dot_rows(active[...], val_grad[...])
    for j in range(4):
        rows = pl.ds(pl.multiple_of(jnp.bitwise_xor(sc[0], j) * span, span), span)
        cols = [grads[n][rows, :] for part in range(3) for n in range(part, len(grads), 3)]
        grad = dot_cols(jnp.concatenate(cols, axis=1), weights[...]).astype(BF)
        if j == 3:
            upper[...] = grad[: span // 2]
            lower[...] = grad[span // 2 :]
        else:
            (own, sent, kept)[j][...] = grad


def proj_rows(sc, w_proj, group):
    return [
        w_proj[pl.ds(pl.multiple_of(jnp.bitwise_xor(sc[2], flip) * group, 16), group), :] for flip in range(2)
    ]


def prepare_body(
    sc, x, grads, routes, w_proj, wq, wk, wv, x_kept, tail, b00, b01, b10, b11, w_own, cols
):
    seqs, span, width = x.shape
    group, count = wq.shape[1], x_kept.shape[0]
    experts = count // SEAT
    for j, weight in enumerate((wq, wk, wv)):
        w_own[:, j * group : (j + 1) * group] = weight[...]
    proj_own, proj_peer = proj_rows(sc, w_proj, group)
    earlier = lax.broadcasted_iota(jnp.int32, (span, span), 0) < lax.broadcasted_iota(jnp.int32, (span, span), 1)
    earlier = jnp.where(earlier, 1.0, 0.0).astype(BF)
    ids = lax.broadcasted_iota(jnp.int32, (max(8, experts), span), 0)
    slots = lax.broadcasted_iota(jnp.int32, (count, span), 0)
    rows_of = lax.broadcasted_iota(jnp.int32, (LANES, span), 0)
    seen = jnp.zeros((max(8, experts), 1), F32)
    x_sum, tail_sum, flag_sum, tables = None, None, None, []
    for n in range(seqs):
        route = routes[n : n + 1, :]
        mine = jnp.where(ids == route, 1.0, 0.0)
        before = dot(mine.astype(BF), earlier) + seen
        rank = jnp.sum(mine * before, axis=0, keepdims=True)
        seen = seen + jnp.sum(mine, axis=1, keepdims=True)
        limit = jnp.zeros((1, span), jnp.int32)
        for e in range(experts):
            limit = jnp.where(route == e, sc[7 + e], limit)
        kept = rank < limit.astype(F32)
        place = jnp.bitwise_xor(route, sc[4])
        seat = jnp.where(kept, place * SEAT + rank.astype(jnp.int32), -1)
        pick = jnp.where(slots == seat, 1.0, 0.0).astype(BF)
        live = jnp.where(sc[5 + n] == 1, F32(1.0), F32(0.0))
        table = jnp.where(rows_of == 0, jnp.where(kept, place.astype(F32), -1.0), 0.0)
        table = jnp.where(rows_of == 1, jnp.where(kept, rank, 0.0), table)
        table = jnp.where(rows_of == 2, live, table)
        table = jnp.where(rows_of == 3, jnp.where(kept, 0.0, 1.0), table)
        tables.append(table[:16, :].astype(BF))
        columns = jnp.transpose(table).astype(BF)
        cols[n] = columns
        parts = dot(pick, x[n]), dot(pick, grads[n]), dot(pick, columns)
        x_sum = parts[0] if n == 0 else x_sum + parts[0]
        tail_sum = parts[1] if n == 0 else tail_sum + parts[1]
        flag_sum = parts[2] if n == 0 else flag_sum + parts[2]
    x_kept[...] = x_sum.astype(BF)
    tail[:, :width] = tail_sum.astype(BF)
    tail[:, width:] = flag_sum.astype(BF)
    for rel, (own, peer) in enumerate(((b00, b01), (b10, b11))):
        at = jnp.bitwise_xor(sc[1], rel)
        own_cols = cols[at]
        rows = grads[at] * own_cols[:, 3:4]
        for out, weight in ((own, proj_own), (peer, proj_peer)):
            out[:span, :] = dot_cols(rows, weight).astype(BF)
            out[span:, :span] = jnp.where(at == 0, tables[0], tables[1])
            if group > span:
                out[span:, span:] = jnp.zeros((out.shape[0] - span, group - span), BF)


def project_body(sc, k00, k01, k10, k11, x_kept, tail, w_proj, gain, after, own, peer, *boxes):
    own[...] = k00[...] + k10[...]
    peer[...] = k01[...] + k11[...]
    w_own, w_peer = proj_rows(sc, w_proj, own.shape[1])
    rows = x_kept[...].astype(F32) + (dot(own[...], w_own) + dot(peer[...], w_peer))
    after[...] = rows
    unit, _ = norm_parts(rows)
    moe_in = (unit * gain[...]).astype(BF)
    width = moe_in.shape[1]
    for j, box in enumerate(boxes):
        at = slice(j * SEAT, (j + 1) * SEAT)
        box[:, :width] = moe_in[at, :]
        box[:, width:] = tail[at, :]


def expert_body(sc, *refs):
    row_refs = refs[:8]
    router, w_in, w_out = refs[8:11]
    back_own, back_peer, rows, active, hidden_grad, val_grad, logit_grad = refs[11:]
    piece, width = row_refs[0].shape[0], rows.shape[1]
    expert = sc[4]
    for k, ref in enumerate(row_refs):
        rows[k * piece : (k + 1) * piece, :] = ref[:, :width]
    column = router[pl.ds(expert, 1), :]
    per = max(1, 512 // piece)
    for first in range(0, 8, per):
        here = slice(first * piece, (first + per) * piece)
        moe_in = rows[here, :]
        grads = jnp.concatenate([row_refs[k][:, width:] for k in range(first, first + per)], axis=0)
        live = grads[:, width + 2 : width + 3].astype(F32)
        grads = grads[:, :width].astype(F32)
        logit = jnp.sum(moe_in.astype(F32) * column, axis=-1, keepdims=True)
        gate = 1.0 / (1.0 + jnp.exp(-logit))
        value_grad = (gate * grads).astype(BF)
        hidden = dot(moe_in, w_in[...])
        bent = 0.5 * (1.0 + lax.erf(hidden * (0.5**0.5)))
        act = (hidden * bent).astype(BF)
        slope = bent + hidden * jnp.exp(-0.5 * hidden * hidden) * ((2.0 * jnp.pi) ** -0.5)
        pulled = (slope * dot_cols(value_grad, w_out[...])).astype(BF)
        part = dot(act, w_out[...])
        logit_part = jnp.sum(part * grads, axis=-1, keepdims=True) * (gate * (1.0 - gate) * live)
        back = (dot_cols(pulled, w_in[...]) + logit_part * column).astype(BF)
        value = (gate * part).astype(BF)
        active[here, :] = act
        hidden_grad[here, :] = pulled
        val_grad[here, :] = value_grad
        lane = lax.broadcasted_iota(jnp.int32, (logit_part.shape[0], LANES), 1)
        logit_grad[here, :] = jnp.where(lane == expert + 2, logit_part, 0.0).astype(BF)
        for k in range(first, first + per):
            at = slice((k - first) * piece, (k - first + 1) * piece)
            to = slice((k % 4) * piece, (k % 4 + 1) * piece)
            out = back_own if k < 4 else back_peer
            out[to, :width] = back[at, :]
            out[to, width:] = value[at, :]


def return_body(sc, back, after, tail, attn_own, attn_peer, gain, w_proj, mid, branch, gain_row, own, far, core):
    width = after.shape[1]
    upstream = back[:, :width].astype(F32)
    unit, scaling = norm_parts(after[...])
    gain_row[...] = jnp.sum(upstream * unit, axis=0, keepdims=True)
    total = tail[:, :width].astype(F32) + norm_pull(upstream * gain[...], unit, scaling)
    mid[...] = total
    low = total.astype(BF)
    branch[...] = low
    group = own.shape[1]
    w_own, w_peer = proj_rows(sc, w_proj, group)
    own[...] = dot_cols(low, w_own).astype(BF)
    pulled = dot_cols(low, w_peer).astype(BF)
    far[...] = pulled
    core[:, :group] = pulled
    core[:, group : 2 * group] = attn_own[...]
    core[:, 2 * group : 3 * group] = attn_peer[...]
    core[:, 3 * group :] = low


def projection_grad_body(
    sc, a00, a01, a10, a11, grads, cols, expert_rows, logit_grad, attn_in, own, peer, router_rows, attn_t, rows
):
    attn_t[...] = jnp.transpose(attn_in[...])
    router_rows[...] = dot_rows(logit_grad[...], expert_rows[...])[: router_rows.shape[0], :]
    span, group = a00.shape
    core = sc[2]
    for rel in range(2):
        at = jnp.bitwise_xor(sc[1], rel)
        rows[rel] = grads[at] * cols[at][:, 3:4]
    for half, out in enumerate((own, peer)):
        to = pl.ds(pl.multiple_of(jnp.bitwise_xor(core, half) * group, LANES), group)
        cut0, cut1 = rows[0, :, to], rows[1, :, to]
        for kind, (first, second) in enumerate(((a00, a10), (a01, a11))):
            at = pl.multiple_of(jnp.bitwise_xor(core, kind) * group, 16)
            total = dot_rows(first[:span, :], cut0) + dot_rows(second[...], cut1)
            out[pl.ds(at, group), :] = total.astype(BF)


def place_column(sc, cut, stride, parts, column, out):
    size = out.shape[0] // 4
    for rel, (part, offset) in enumerate(parts):
        first = jnp.bitwise_xor(sc[3], rel) * size
        for j in range(stride // cut):
            place = jnp.bitwise_xor(sc[4], j) * cut
            value = part[offset + j * cut : offset + (j + 1) * cut, pl.ds(column, LANES)].astype(F32)

            def store(place=place, value=value, first=first):
                out[pl.ds(pl.multiple_of(first + place, 16), cut), :] = value

            if stride > size:
                pl.when(place < size)(store)
            else:
                store()


def spread_proj_body(cut, sc, *refs):
    own, peer, out = refs[:4], refs[4], refs[5]
    step = pl.program_id(0)
    stride = own[0].shape[0]
    parts = [(ref, 0) for ref in own] + [(peer, rel * stride) for rel in range(4)]

    def write(side):
        place_column(sc, cut, stride, parts[4 * side : 4 * side + 4], pl.multiple_of(step % 3 * LANES, LANES), out)

    for side in range(2):
        pl.when(step // 3 == side)(functools.partial(write, side))


def spread_body(cut, group, pairs, sc, *refs):
    own, peer, second, out = refs[:4], refs[4], refs[5:13], refs[13]
    core, expert = sc[2], sc[4]
    size = out.shape[0]
    stride = own[0].shape[0]

    def write(rel):
        for half in range(2):
            side = jnp.bitwise_xor(core, half) * group
            first, offset = (peer, rel * stride) if half else (own[rel], 0)
            rest = second[4 * half + rel]
            for j in range(stride // cut):
                place = jnp.bitwise_xor(expert, j) * cut

                def store(place=place, j=j, side=side, first=first, offset=offset, rest=rest):
                    rows = pl.ds(pl.multiple_of(place, 16), cut)
                    for pair in range(pairs):
                        ref, start = (rest, j * cut) if pair else (first, offset + j * cut)
                        base = 3 * LANES * (pair - 1) if pair else group
                        for part in range(3):
                            at = base + part * LANES
                            to = pl.multiple_of(side + pair * LANES + 2 * part * group, LANES)
                            out[rows, pl.ds(to, LANES)] = ref[start : start + cut, at : at + LANES].astype(F32)

                if stride > size:
                    pl.when(place < size)(store)
                else:
                    store()

    for rel in range(4):
        pl.when(pl.program_id(0) == rel)(functools.partial(write, rel))


def small_body(experts, first, sc, own, peer, gain, attn_gain, moe_gain, router):
    rows = own[...].astype(F32) + peer[first : first + own.shape[0], :].astype(F32)
    attn_gain[...] = (rows[:1, :] / gain[...])[0]
    moe_gain[...] = rows[1]
    router[...] = rows[2 : 2 + experts, :]


def input_body(first, sc, x, grads, cols, mid, first_own, peer, second, gain, out):
    high = mid[...].astype(BF)
    rest = (mid[...] - high.astype(F32)).astype(BF)
    for rel in range(2):
        if rel == 0:
            upstream = first_own[...].astype(F32) + peer[first : first + first_own.shape[0], :].astype(F32)
        else:
            upstream = second[...].astype(F32)
        at = jnp.bitwise_xor(sc[1], rel)
        own_cols = cols[at]
        pick = one_hot(own_cols, mid.shape[0])
        total = (grads[at] * own_cols[:, 3:4]).astype(F32) + (dot(pick, high) + dot(pick, rest))
        unit, scaling = norm_parts(x[at].astype(F32))
        out[at] = (total + norm_pull(upstream * gain[...], unit, scaling)).astype(BF)


def pack_body(sc, *refs):
    at = 0
    for part in refs[:-1]:
        refs[-1][at : at + part.shape[0], :] = part[...]
        at += part.shape[0]


def output_body(sc, a00, a01, a10, a11, x, w_proj, cols, values, out):
    span, width = x.shape[1:]
    w_own, w_peer = proj_rows(sc, w_proj, a00.shape[1])
    for rel, (own, peer) in enumerate(((a00, a01), (a10, a11))):
        at = jnp.bitwise_xor(sc[1], rel)
        rows = x[at].astype(F32) + (dot(own[:span, :], w_own) + dot(peer[:span, :], w_peer))
        pick = one_hot(cols[at], values.shape[0])
        out[at] = (rows + dot(pick, values[:, width:])).astype(BF)


def local(
    blk_count,
    batch_count,
    x,
    gain_one,
    w_qkv,
    w_proj,
    gain_two,
    router,
    w_in,
    w_out,
    routes,
    quota,
    period,
    g,
):
    seq_count, span, width = x.shape
    group = width // 2
    experts = quota.shape[0]
    share = batch_count // experts
    assert blk_count == 4 and seq_count == 2 and share == 2
    blk, batch = lax.axis_index("blk"), lax.axis_index("batch")
    chip, core = blk // 2, blk % 2
    expert, half = batch // share, batch % share
    quarter = chip * 2 + half
    sc = jnp.concatenate([jnp.stack([blk, chip, core, quarter, expert]).astype(jnp.int32), period, quota])

    def to_blk(value, bits):
        return lax.ppermute(value, "blk", [(i, i ^ bits) for i in range(4)])

    def to_batch(value, bits):
        return lax.ppermute(value, "batch", [(i, i ^ bits) for i in range(batch_count)])

    def to_expert(value, bits):
        return to_batch(value, bits * share)

    def to_plane(value, rel):
        if rel == 1:
            return to_batch(value, 1)
        if rel == 2:
            return to_blk(value, 2)
        pairs = [
            (i * batch_count + j, (i ^ 2) * batch_count + (j ^ 1)) for i in range(4) for j in range(batch_count)
        ]
        return lax.ppermute(value, ("blk", "batch"), pairs)

    def third(j):
        return (w_qkv, (width, group), lambda s: (0, 2 * j + s[2]))

    mine = lax.dynamic_index_in_dim(x, chip, 0, keepdims=False)
    other = lax.dynamic_index_in_dim(x, 1 - chip, 0, keepdims=False)
    block_x = to_blk(other, 2)
    block_c = to_blk(mine, 1)

    gain_one_row, gain_two_row = gain_one.reshape(1, width), gain_two.reshape(1, width)

    seat_rows = experts * SEAT
    length = 4 * span
    piece = shape_of((span, group), BF)
    base_piece = shape_of((span + 16, group), BF)
    kept_piece = shape_of((seat_rows, group), BF)
    kept_rows = shape_of((seat_rows, width), BF)
    x_kept, tail, b00, b01, b10, b11, w_own, cols = run_kernel(
        prepare_body,
        sc,
        [x, g, routes, w_proj, third(0), third(1), third(2)],
        [
            kept_rows,
            shape_of((seat_rows, width + LANES), BF),
            base_piece,
            base_piece,
            base_piece,
            base_piece,
            shape_of((width, 3 * group), BF),
            shape_of((seq_count, span, LANES), BF),
        ],
        name="prepare",
    )
    block_x, b01, b10, b11 = together([block_x, b01, b10, b11])
    base = [b00, to_blk(b01, 1), to_blk(b10, 2), to_blk(b11, 3)]
    block_xc = to_blk(block_x, 1)
    pairs = group // LANES
    attn_in, qkv, mixed, stats, own0, own1, own2, own3, *powers = run_kernel(
        forward_body,
        sc,
        [mine, block_c, block_x, block_xc, gain_one_row, w_own],
        [
            shape_of((length, width), BF),
            shape_of((length, 3 * group), BF),
            shape_of((length, group), F32),
            shape_of((length, LANES), F32),
            piece,
            piece,
            piece,
            piece,
        ]
        + [shape_of((pairs, 2 * span, (i + 1) * span), BF) for i in range(4)],
        [pltpu.VMEM((4, span, group), BF)],
        name="attention_forward",
    )
    kept0, core_rows, kept2, kept3 = run_kernel(
        pick_body,
        sc,
        [own0, own1, own2, own3, *base],
        [kept_piece, shape_of((span + seat_rows, group), BF), kept_piece, kept_piece],
        name="pick_kept",
    )
    core_rows = to_blk(core_rows, 1)
    late = [kept0, core_rows, to_blk(kept2, 2), to_blk(kept3, 3)]
    own2, own3, *late = together([own2, own3, *late])
    core_rows = late[1]
    a10, a11 = to_blk(own2, 2), to_blk(own3, 3)
    row_box = shape_of((SEAT, 2 * width + LANES), BF)
    after_kept, attn_own, attn_peer, *boxes = run_kernel(
        project_body,
        sc,
        [
            kept0,
            (core_rows, (seat_rows, group), lambda s: (span // seat_rows, 0)) if span % seat_rows == 0 else core_rows[span:],
            *late[2:],
            x_kept,
            tail,
            w_proj,
            gain_two_row,
        ],
        [shape_of((seat_rows, width), F32), kept_piece, kept_piece] + [row_box] * experts,
        name="project",
    )

    order = [0, *reversed(range(1, experts))]
    parts = [to_expert(boxes[j], j) if j else boxes[0] for j in order]
    rows = jnp.concatenate(together([*parts, a10, a11])[:experts], axis=0)
    expert_rows = [rows] + [to_plane(rows, rel) for rel in (1, 2, 3)]
    expert_rows += [to_blk(part, 1) for part in expert_rows]
    total_rows = 8 * seat_rows
    hidden_units = w_in.shape[2]
    quad = shape_of((4 * seat_rows, 2 * width), BF)
    back_own, back_peer, rows, active, hidden_grad, val_grad, logit_grad = run_kernel(
        expert_body,
        sc,
        [*expert_rows, router.T.astype(F32), w_in[0], w_out[0]],
        [
            quad,
            quad,
            shape_of((total_rows, width), BF),
            shape_of((total_rows, hidden_units), BF),
            shape_of((total_rows, hidden_units), BF),
            shape_of((total_rows, width), BF),
            shape_of((total_rows, LANES), BF),
        ],
        name="expert",
    )
    def total_of(parts):
        parts = [part.astype(F32) for part in parts]
        while len(parts) > 1:
            parts = [left + right for left, right in zip(parts[::2], parts[1::2])]
        return parts[0].astype(BF)

    arrived = to_blk(back_peer, 1)
    parts = []
    for rel in range(4):
        at = slice(rel * seat_rows, (rel + 1) * seat_rows)
        part = total_of([back_own[at], arrived[at]])
        parts.append(part if rel == 0 else to_plane(part, rel))
    parts = together(parts)
    cuts = [total_of([part[n * SEAT : (n + 1) * SEAT] for part in parts]) for n in range(experts)]
    cuts = [cuts[order.index(j)] for j in range(experts)]
    back = jnp.concatenate(together([cuts[0]] + [to_expert(cuts[j], j) for j in range(1, experts)]), axis=0)

    extra = -(-(experts + 2) // 16) * 16
    proj_own, proj_peer, router_rows, attn_t = run_kernel(
        projection_grad_body,
        sc,
        [own0, core_rows, a10, a11, g, cols, rows, logit_grad, attn_in],
        [shape_of((width, group), BF)] * 2 + [shape_of((extra, width), F32), shape_of((width, length), BF)],
        [pltpu.VMEM((seq_count, span, width), BF)],
        name="projection_grad",
        after=[back_own],
    )
    proj_arrived = to_blk(proj_peer, 1)
    wide_cols = shape_of((width, LANES), F32)
    mid, branch, moe_row, m_own, m_far, m_core = run_kernel(
        return_body,
        sc,
        [back, after_kept, tail, attn_own, attn_peer, gain_two_row, w_proj],
        [
            shape_of((seat_rows, width), F32),
            kept_rows,
            shape_of((1, width), F32),
            kept_piece,
            kept_piece,
            shape_of((seat_rows, 3 * group + width), BF),
        ],
        name="return_rows",
        after=[router_rows, proj_arrived],
    )
    mix_late = [m_own, to_blk(m_core, 1), to_blk(m_own, 2), to_blk(m_far, 3)]

    size = width // 4
    cut = -(-size // (experts * 16)) * 16
    stride = experts * cut

    def scatter_plane(quarters):
        return [quarters[0]] + [to_plane(quarters[rel], rel) for rel in (1, 2, 3)]

    def sum_cuts(parts):
        return [total_of([part[j * cut : (j + 1) * cut] for part in parts]) for j in range(experts)]

    def sum_experts(cuts):
        return total_of(together([cuts[0]] + [to_expert(cuts[j], j) for j in range(1, experts)]))

    def halve_experts(cuts, bits, far):
        return [total_of([near, far[j * cut : (j + 1) * cut]]) for j, near in enumerate(cuts[:bits])]

    def far_cuts(cuts, bits):
        return to_expert(jnp.concatenate(cuts[bits:], axis=0), bits)

    def gather_experts(whole, before=()):
        parts = [whole] + [to_expert(whole, j) for j in range(1, experts)]
        return jnp.concatenate(together([*parts, *before])[:experts], axis=0)

    def gather_plane(column):
        return [column] + [to_plane(column, rel) for rel in (1, 2, 3)]


    tall = shape_of((length, LANES), BF)
    working = [
        pltpu.VMEM((length, LANES), BF),
        pltpu.VMEM((length, LANES), F32),
        pltpu.VMEM((length, LANES), F32),
    ]
    wide_one = group + 3 * LANES
    wide_two = 3 * LANES * (pairs - 1)
    operands = [*base, *mix_late, *powers, qkv, mixed, attn_t, stats, w_own]
    dq, dk, dv, *quarters_one, gain_sum = run_kernel(
        functools.partial(first_backward_body, cut),
        sc,
        [*operands, proj_own, proj_arrived, attn_own, attn_peer, branch],
        [tall, tall, tall] + [shape_of((stride, wide_one), BF)] * 4 + [wide_cols],
        working + [pltpu.VMEM((4 * stride, wide_one), BF)],
        name="attention_backward_one",
    )
    parts_one = scatter_plane(quarters_one)
    *grads, t0, t1, t2, t3 = run_kernel(
        functools.partial(second_backward_body, pairs, cut),
        sc,
        [*operands, gain_sum, moe_row, router_rows],
        [tall] * (3 * (pairs - 1)) + [shape_of((stride + extra, wide_two), BF)] * 4,
        working + [pltpu.VMEM((4 * stride, wide_two), BF)],
        name="attention_backward_two",
    )
    t1, t2, t3, *parts_one = together([t1, t2, t3, *parts_one])
    parts_two = scatter_plane([t0, t1, t2, t3])
    cuts_one, bits = sum_cuts(parts_one), experts // 2
    far = far_cuts(cuts_one, bits)
    part = shape_of((span, width), BF)
    near_piece = shape_of((span // 2, width), BF)
    first_own, sent, upper, lower, near, in_grad, out_grad = run_kernel(
        norm_grad_body,
        sc,
        [dq, dk, dv, *grads, w_own, rows, active, hidden_grad, val_grad],
        [
            part,
            part,
            near_piece,
            near_piece,
            part,
            shape_of((width, hidden_units), F32),
            shape_of((hidden_units, width), F32),
        ],
        name="norm_one_grad",
        flops=10e9,
    )
    upper, lower = to_blk(upper, 1), to_blk(lower, 1)
    *parts_two, out_grad = together([*parts_two, out_grad])
    upper, lower, *parts_two = together([upper, lower, *parts_two])
    second = to_blk(total_of([near, jnp.concatenate([upper, lower], axis=0)]), 2)
    while bits:
        cuts_one = halve_experts(cuts_one, bits, far)
        bits //= 2
        if bits:
            far = far_cuts(cuts_one, bits)
        if bits == 1:
            far, *_ = together([far, *parts_two])
    whole_one = cuts_one[0]
    column_one = gather_experts(whole_one, [second])
    small = total_of([part[stride:] for part in parts_two])
    whole_two = sum_experts([jnp.concatenate([piece, small], axis=0) for piece in sum_cuts(parts_two)])
    whole_two, small = whole_two[:cut], whole_two[cut:]
    one = gather_plane(column_one)
    sent, small, column_two, *one = together([sent, small, gather_experts(whole_two), *one])
    two = gather_plane(column_two)
    packed = [*one, small, sent]
    packed_rows = sum(part.shape[0] for part in packed)
    (pack,) = run_kernel(pack_body, sc, packed, [shape_of((packed_rows, width), BF)], name="pack")
    output = run_kernel(
        output_body,
        sc,
        [own0, core_rows, a10, a11, x, w_proj, cols, back],
        [shape_of(x.shape, BF)],
        name="output",
        after=[pack],
    )[0]
    pack = to_blk(pack, 1)
    input_grad = run_kernel(
        functools.partial(input_body, packed_rows - span),
        sc,
        [x, g, cols, mid, first_own, pack, second, gain_one_row],
        [shape_of(x.shape, BF)],
        name="input_grad",
    )[0]
    attn_gain, moe_gain, router_grad = run_kernel(
        functools.partial(small_body, experts, 4 * stride),
        sc,
        [small, pack, gain_one_row],
        [shape_of((width,), F32), shape_of((width,), F32), shape_of((experts, width), F32)],
        name="small_grads",
    )

    def grid_kernel(body, steps, arrays, out, block, index, name):
        return pl.pallas_call(
            body,
            grid_spec=pltpu.PrefetchScalarGridSpec(
                num_scalar_prefetch=1,
                grid=(steps,),
                in_specs=[pl.BlockSpec(memory_space=pltpu.VMEM)] * len(arrays),
                out_specs=pl.BlockSpec(block, index),
            ),
            out_shape=out,
            compiler_params=pltpu.CompilerParams(vmem_limit_bytes=16 * 1024 * 1024),
            name=name,
        )(sc, *arrays)

    proj_grad = grid_kernel(
        functools.partial(spread_proj_body, cut),
        6,
        [*one, pack],
        shape_of((width, width), F32),
        (width, LANES),
        lambda i, s: (0, jnp.bitwise_xor(s[2], i // 3) * pairs + i % 3),
        "spread_proj",
    )
    *two, output, input_grad, proj_grad, attn_gain = together([*two, output, input_grad, proj_grad, attn_gain])
    qkv_grad = grid_kernel(
        functools.partial(spread_body, cut, group, pairs),
        4,
        [*one, pack, *two, *[to_blk(part, 1) for part in two]],
        shape_of((width, 3 * width), F32),
        (size, 3 * width),
        lambda i, s: (jnp.bitwise_xor(s[3], i), 0),
        "spread",
    )
    return (
        output,
        input_grad,
        attn_gain,
        qkv_grad,
        proj_grad,
        moe_gain,
        router_grad.T,
        in_grad[None],
        out_grad[None],
    )


def solution(mesh):
    rows, kept = P("batch", "blk", None), P()
    w_in, w_out = P("batch", None, "blk"), P("batch", "blk", None)
    return jax.shard_map(
        functools.partial(local, mesh.shape["blk"], mesh.shape["batch"]),
        mesh=mesh,
        in_specs=(rows, kept, kept, kept, kept, kept, w_in, w_out, P("batch", "blk"), kept, P("batch"), rows),
        out_specs=(rows, rows, kept, kept, kept, kept, kept, w_in, w_out),
        check_vma=False,
    )
```

```python
import functools
import math

import jax
import jax.numpy as jnp
from jax import lax
from jax.experimental import pallas as pl
from jax.experimental.pallas import tpu as pltpu
from jax.sharding import PartitionSpec as P

HEAD_DIM = 64
CAP = 12
SEAT = 16
LANES = 128
EPSILON = 1e-05
FAR_BELOW = -1e30
BF = jnp.bfloat16
F32 = jnp.float32


def dot(left, right):
    return jnp.dot(left, right, preferred_element_type=F32)


def dot_rows(left, right):
    return lax.dot_general(left, right, (((0,), (0,)), ((), ())), preferred_element_type=F32)


def dot_cols(left, right):
    return lax.dot_general(left, right, (((1,), (1,)), ((), ())), preferred_element_type=F32)


def norm_parts(rows):
    centred = rows - jnp.mean(rows, axis=-1, keepdims=True)
    scaling = lax.rsqrt(jnp.mean(centred * centred, axis=-1, keepdims=True) + EPSILON)
    return centred * scaling, scaling


def norm_pull(scaled, unit, scaling):
    return scaling * (
        scaled
        - jnp.mean(scaled, axis=-1, keepdims=True)
        - unit * jnp.mean(scaled * unit, axis=-1, keepdims=True)
    )


def run_kernel(body, scalars, operands, outs, scratch=(), flops=0, name=None, after=()):
    specs, arrays, held = [], [], 0
    after, given, run = list(after), len(operands), body
    if after:

        def run(sc, *refs):
            body(sc, *refs[:given], *refs[given + len(after) :])

    for operand in operands:
        if isinstance(operand, tuple):
            array, block, index = operand
            held += 2 * math.prod(block) * array.dtype.itemsize
            specs.append(pl.BlockSpec(block, functools.partial(lambda i, s, fn: fn(s), fn=index)))
        else:
            array = operand
            held += array.size * array.dtype.itemsize
            specs.append(pl.BlockSpec(memory_space=pltpu.VMEM))
        arrays.append(array)
    specs += [pl.BlockSpec(memory_space=pl.ANY)] * len(after)
    held += sum(out.size * out.dtype.itemsize for out in outs)
    out_specs = [pl.BlockSpec(memory_space=pltpu.VMEM) for _ in outs]
    return pl.pallas_call(
        run,
        grid_spec=pltpu.PrefetchScalarGridSpec(
            num_scalar_prefetch=1,
            grid=(1,),
            in_specs=specs,
            out_specs=out_specs,
            scratch_shapes=list(scratch),
        ),
        out_shape=list(outs),
        compiler_params=pltpu.CompilerParams(vmem_limit_bytes=(16 if held < 24e6 else 60) * 1024 * 1024),
        cost_estimate=pl.CostEstimate(flops=int(flops), bytes_accessed=0, transcendentals=0),
        name=name,
    )(scalars, *arrays, *after)


def together(values):
    return list(lax.optimization_barrier(tuple(values)))


def shape_of(dims, dtype):
    return jax.ShapeDtypeStruct(dims, dtype)


def half_masks(scale):
    lane = lax.broadcasted_iota(jnp.int32, (1, LANES), 1)
    low = lane < HEAD_DIM
    return lane, low, (jnp.where(low, scale, 0.0).astype(BF), jnp.where(low, 0.0, scale).astype(BF))


def one_hot(cols, count):
    seat = cols[:, :1].astype(F32) * SEAT + cols[:, 1:2].astype(F32)
    slot = lax.broadcasted_iota(jnp.int32, (cols.shape[0], count), 1).astype(F32)
    return jnp.where(slot == seat, 1.0, 0.0).astype(BF)


def one_hot_rows(block, span, count):
    seat = block[span : span + 1, :span].astype(F32) * SEAT + block[span + 1 : span + 2, :span].astype(F32)
    slot = lax.broadcasted_iota(jnp.int32, (count, span), 0).astype(F32)
    return jnp.where(slot == seat, 1.0, 0.0).astype(BF)


def forward_body(
    sc, m0, m1, m2, m3, gain, weights, attn_in, qkv, mixed, stats, o0, o1, o2, o3, p0, p1, p2, p3, pieces
):
    powers = (p0, p1, p2, p3)
    span, group = m2.shape[0], weights.shape[1] // 3
    place = sc[0]
    for rel, block in enumerate((m0, m1, m2, m3)):
        start = pl.multiple_of(jnp.bitwise_xor(place, rel) * span, span)
        unit, _ = norm_parts(block[...].astype(F32))
        normed = (unit * gain[...]).astype(BF)
        attn_in[pl.ds(start, span), :] = normed
        qkv[pl.ds(start, span), :] = dot(normed, weights[...]).astype(BF)
    lane, low, scaled = half_masks(HEAD_DIM**-0.5)
    row = jnp.bitwise_and(lax.broadcasted_iota(jnp.int32, (2 * span, span), 0), span - 1)
    col = lax.broadcasted_iota(jnp.int32, (2 * span, span), 1)
    causal = col <= row
    for i in range(4):
        past = i * span
        upto = past + span
        stat = jnp.zeros((span, LANES), F32)
        for g in range(group // LANES):
            at = g * LANES
            queries = qkv[past:upto, at : at + LANES]
            keys = qkv[0:upto, group + at : group + at + LANES]
            values = qkv[0:upto, 2 * group + at : 2 * group + at + LANES]
            both = jnp.concatenate([queries * scaled[0], queries * scaled[1]], axis=0)
            last = jnp.where(causal, dot_cols(both, keys[past:]), FAR_BELOW)
            top = jnp.max(last, axis=-1, keepdims=True)
            if i:
                first = dot_cols(both, keys[:past])
                top = jnp.maximum(top, jnp.max(first, axis=-1, keepdims=True))
            beside = jnp.concatenate([values, jnp.ones_like(values)], axis=1)
            raised = jnp.exp(last - top).astype(BF)
            powers[i][g, :, past:] = raised
            mix = dot(raised, beside[past:])
            if i:
                raised = jnp.exp(first - top).astype(BF)
                powers[i][g, :, :past] = raised
                mix = mix + dot(raised, beside[:past])
            scale = 1.0 / mix[:, LANES:]
            mix = mix[:, :LANES] * scale
            mix = jnp.where(low, mix[:span], mix[span:])
            for u in range(2):
                stat = jnp.where(lane == 2 * g + u, scale[u * span : (u + 1) * span], stat)
            mixed[past:upto, at : at + LANES] = mix
            pieces[jnp.bitwise_xor(place, i), :, at : at + LANES] = mix.astype(BF)
        stats[past:upto, :] = stat
    for rel, out in enumerate((o0, o1, o2, o3)):
        out[...] = pieces[rel]


def pick_body(sc, o0, o1, o2, o3, b0, b1, b2, b3, k0, core, k2, k3):
    span, group = o0.shape
    for out, rows, base in ((k0, o0, b0), (core, o1, b1), (k2, o2, b2), (k3, o3, b3)):
        kept = dot(one_hot_rows(base, span, k0.shape[0]), rows[...]).astype(BF)
        if out is core:
            core[:span, :] = rows[...]
            core[span:, :] = kept
        else:
            out[...] = kept


def pair_backward(stats, pair, qkv, mixed, powers, dmix, dq, dk, dv, dk_sum, dv_sum):
    span, group, head = qkv.shape[0] // 4, qkv.shape[1] // 3, 2 * pair
    at = [slice(j * group + pair * LANES, j * group + (pair + 1) * LANES) for j in range(3)]
    scale = HEAD_DIM**-0.5
    _, low, ones = half_masks(1.0)
    _, _, scaled = half_masks(scale)
    for i in reversed(range(4)):
        past = i * span
        upto = past + span
        queries = qkv[past:upto, at[0]]
        keys = qkv[0:upto, at[1]]
        values = qkv[0:upto, at[2]]
        over = jnp.where(low, stats[past:upto, head : head + 1], stats[past:upto, head + 1 : head + 2])
        grads = (dmix[past:upto, :].astype(F32) * over).astype(BF)
        product = grads.astype(F32) * mixed[past:upto, at[0]]
        query = [queries * scaled[u] for u in range(2)]
        grad = [grads * ones[u] for u in range(2)]
        pulls = [dot_cols(grad[u], values) for u in range(2)]
        halves, sums = [], {}
        for u in range(2):
            delta = jnp.sum(jnp.where(low == (u == 0), product, 0.0), axis=-1, keepdims=True)
            half = None
            for rows in (slice(past, upto), slice(0, past))[: 2 if i else 1]:
                weights = powers[i][pair, u * span : (u + 1) * span, rows]
                score_grad = (weights.astype(F32) * (pulls[u][:, rows] - delta)).astype(BF)
                part = dot(score_grad, keys[rows])
                half = part if half is None else half + part
                for name, left, right in (("k", score_grad, query[u]), ("v", weights, grad[u])):
                    part = dot_rows(left, right)
                    sums[name, rows.start] = sums[name, rows.start] + part if u else part
            halves.append(half)
        for (name, start), part in sums.items():
            out = dk_sum if name == "k" else dv_sum
            rows = slice(start, upto if start == past else past)
            out[rows, :] = part if i == 3 else out[rows, :] + part
        dq[past:upto, :] = (jnp.where(low, halves[0], halves[1]) * scale).astype(BF)
    dk[...] = dk_sum[...].astype(BF)
    dv[...] = dv_sum[...].astype(BF)


def stage_rows(held, columns, value, stride):
    size = value.shape[0] // 4
    for k in range(4):
        held[k * stride : k * stride + size, columns] = value[k * size : (k + 1) * size, :]
        if stride > size:
            held[k * stride + size : (k + 1) * stride, columns] = jnp.zeros((stride - size, value.shape[1]), BF)


def place_cuts(cut, quarter, expert, held, outs, stride):
    for rel, out in enumerate(outs):
        first = jnp.bitwise_xor(quarter, rel) * stride
        for j in range(stride // cut):
            at = pl.multiple_of(first + jnp.bitwise_xor(expert, j) * cut, 16)
            out[j * cut : (j + 1) * cut, :] = held[pl.ds(at, cut), :]


def load_grads(place, pair, blocks, kept, dmix):
    span = dmix.shape[0] // 4
    at = slice(pair * LANES, (pair + 1) * LANES)
    for rel, block in enumerate(blocks):
        start = pl.multiple_of(jnp.bitwise_xor(place, rel) * span, span)
        late = dot_rows(one_hot_rows(block, span, kept[rel].shape[0]), kept[rel][:, at])
        dmix[pl.ds(start, span), :] = (block[:span, at].astype(F32) + late).astype(BF)


def weight_columns(attn_t, sources, weights, pair, held, first, stride):
    total, group = None, weights.shape[1] // 3
    grad = dot(attn_t[...], jnp.concatenate([source[...] for source in sources], axis=1))
    stage_rows(held, slice(first, first + 3 * LANES), grad.astype(BF), stride)
    for j in range(3):
        at = j * group + pair * LANES
        part = grad[:, j * LANES : (j + 1) * LANES] * weights[:, at : at + LANES].astype(F32)
        total = part if total is None else total + part
    return jnp.sum(total, axis=-1, keepdims=True)


def first_backward_body(cut, sc, *refs):
    base, late, powers, rest = refs[:4], refs[4:8], refs[8:12], refs[12:]
    qkv, mixed, attn_t, stats, weights, proj_own, proj_peer, attn_own, attn_peer, branch = rest[:10]
    dq, dk, dv, w0, w1, w2, w3, gain_sum, dmix, dk_sum, dv_sum, held = rest[10:]
    stride, group, core_late = w0.shape[0], proj_own.shape[1], late[1]
    load_grads(sc[0], 0, base, late, dmix)
    pair_backward(stats, 0, qkv, mixed, powers, dmix, dq, dk, dv, dk_sum, dv_sum)
    core = sc[2]
    to = pl.multiple_of(core * group, LANES)
    rows = branch[:, pl.ds(to, group)]
    rows_peer = core_late[:, pl.ds(pl.multiple_of(3 * group + to, LANES), group)]
    mine = dot_rows(attn_own[...], rows) + dot_rows(core_late[:, 2 * group : 3 * group], rows_peer)
    others = dot_rows(attn_peer[...], rows) + dot_rows(core_late[:, group : 2 * group], rows_peer)
    both = jnp.concatenate([jnp.where(core == 0, mine, others), jnp.where(core == 0, others, mine)], axis=0)
    both = (proj_own[...].astype(F32) + proj_peer[...].astype(F32) + both).astype(BF)
    stage_rows(held, slice(0, group), both, stride)
    sums = weight_columns(attn_t, (dq, dk, dv), weights, 0, held, group, stride)
    gain_sum[...] = jnp.broadcast_to(sums, gain_sum.shape)
    place_cuts(cut, sc[3], sc[4], held, (w0, w1, w2, w3), stride)


def second_backward_body(pairs, cut, sc, *refs):
    base, late, powers, rest = refs[:4], refs[4:8], refs[8:12], refs[12:]
    qkv, mixed, attn_t, stats, weights, gain_sum, moe_row, router_rows = rest[:8]
    grads, rest = rest[8 : 8 + 3 * (pairs - 1)], rest[8 + 3 * (pairs - 1) :]
    outs, (dmix, dk_sum, dv_sum, held) = rest[:4], rest[4:]
    extra = router_rows.shape[0]
    stride = outs[0].shape[0] - extra
    sums = gain_sum[:, :1]
    for n in range(pairs - 1):
        own = grads[3 * n : 3 * n + 3]
        load_grads(sc[0], n + 1, base, late, dmix)
        pair_backward(stats, n + 1, qkv, mixed, powers, dmix, *own, dk_sum, dv_sum)
        sums = sums + weight_columns(attn_t, own, weights, n + 1, held, 3 * LANES * n, stride)
    place_cuts(cut, sc[3], sc[4], held, outs, stride)
    row = lax.broadcasted_iota(jnp.int32, router_rows.shape, 0)
    gain_row = jnp.transpose(jnp.broadcast_to(sums, gain_sum.shape))[:1, :]
    small = jnp.where(row == 0, gain_row, jnp.where(row == 1, moe_row[...], router_rows[...])).astype(BF)
    for out in outs:
        out[stride:, :] = small


def norm_grad_body(sc, *refs):
    grads, (weights, rows_in, active, hidden_grad, val_grad, *outs) = refs[:-12], refs[-12:]
    own, sent, upper, lower, kept, in_grad, out_grad = outs
    span = own.shape[0]
    in_grad[...] = dot_rows(rows_in[...], hidden_grad[...])
    out_grad[...] = dot_rows(active[...], val_grad[...])
    for j in range(4):
        rows = pl.ds(pl.multiple_of(jnp.bitwise_xor(sc[0], j) * span, span), span)
        cols = [grads[n][rows, :] for part in range(3) for n in range(part, len(grads), 3)]
        grad = dot_cols(jnp.concatenate(cols, axis=1), weights[...]).astype(BF)
        if j == 3:
            upper[...] = grad[: span // 2]
            lower[...] = grad[span // 2 :]
        else:
            (own, sent, kept)[j][...] = grad


def proj_rows(sc, w_proj, group):
    return [
        w_proj[pl.ds(pl.multiple_of(jnp.bitwise_xor(sc[2], flip) * group, 16), group), :] for flip in range(2)
    ]


def prepare_body(
    sc, x, grads, routes, w_proj, wq, wk, wv, x_kept, tail, b00, b01, b10, b11, w_own, cols
):
    seqs, span, width = x.shape
    group, count = wq.shape[1], x_kept.shape[0]
    experts = count // SEAT
    for j, weight in enumerate((wq, wk, wv)):
        w_own[:, j * group : (j + 1) * group] = weight[...]
    proj_own, proj_peer = proj_rows(sc, w_proj, group)
    earlier = lax.broadcasted_iota(jnp.int32, (span, span), 0) < lax.broadcasted_iota(jnp.int32, (span, span), 1)
    earlier = jnp.where(earlier, 1.0, 0.0).astype(BF)
    ids = lax.broadcasted_iota(jnp.int32, (max(8, experts), span), 0)
    slots = lax.broadcasted_iota(jnp.int32, (count, span), 0)
    rows_of = lax.broadcasted_iota(jnp.int32, (LANES, span), 0)
    seen = jnp.zeros((max(8, experts), 1), F32)
    x_sum, tail_sum, flag_sum, tables = None, None, None, []
    for n in range(seqs):
        route = routes[n : n + 1, :]
        mine = jnp.where(ids == route, 1.0, 0.0)
        before = dot(mine.astype(BF), earlier) + seen
        rank = jnp.sum(mine * before, axis=0, keepdims=True)
        seen = seen + jnp.sum(mine, axis=1, keepdims=True)
        limit = jnp.zeros((1, span), jnp.int32)
        for e in range(experts):
            limit = jnp.where(route == e, sc[7 + e], limit)
        kept = rank < limit.astype(F32)
        place = jnp.bitwise_xor(route, sc[4])
        seat = jnp.where(kept, place * SEAT + rank.astype(jnp.int32), -1)
        pick = jnp.where(slots == seat, 1.0, 0.0).astype(BF)
        live = jnp.where(sc[5 + n] == 1, F32(1.0), F32(0.0))
        table = jnp.where(rows_of == 0, jnp.where(kept, place.astype(F32), -1.0), 0.0)
        table = jnp.where(rows_of == 1, jnp.where(kept, rank, 0.0), table)
        table = jnp.where(rows_of == 2, live, table)
        table = jnp.where(rows_of == 3, jnp.where(kept, 0.0, 1.0), table)
        tables.append(table[:16, :].astype(BF))
        columns = jnp.transpose(table).astype(BF)
        cols[n] = columns
        parts = dot(pick, x[n]), dot(pick, grads[n]), dot(pick, columns)
        x_sum = parts[0] if n == 0 else x_sum + parts[0]
        tail_sum = parts[1] if n == 0 else tail_sum + parts[1]
        flag_sum = parts[2] if n == 0 else flag_sum + parts[2]
    x_kept[...] = x_sum.astype(BF)
    tail[:, :width] = tail_sum.astype(BF)
    tail[:, width:] = flag_sum.astype(BF)
    for rel, (own, peer) in enumerate(((b00, b01), (b10, b11))):
        at = jnp.bitwise_xor(sc[1], rel)
        own_cols = cols[at]
        rows = grads[at] * own_cols[:, 3:4]
        for out, weight in ((own, proj_own), (peer, proj_peer)):
            out[:span, :] = dot_cols(rows, weight).astype(BF)
            out[span:, :span] = jnp.where(at == 0, tables[0], tables[1])
            if group > span:
                out[span:, span:] = jnp.zeros((out.shape[0] - span, group - span), BF)


def project_body(sc, k00, k01, k10, k11, x_kept, tail, w_proj, gain, after, own, peer, *boxes):
    own[...] = k00[...] + k10[...]
    peer[...] = k01[...] + k11[...]
    w_own, w_peer = proj_rows(sc, w_proj, own.shape[1])
    rows = x_kept[...].astype(F32) + (dot(own[...], w_own) + dot(peer[...], w_peer))
    after[...] = rows
    unit, _ = norm_parts(rows)
    moe_in = (unit * gain[...]).astype(BF)
    width = moe_in.shape[1]
    for j, box in enumerate(boxes):
        at = slice(j * SEAT, (j + 1) * SEAT)
        box[:, :width] = moe_in[at, :]
        box[:, width:] = tail[at, :]


def expert_body(sc, *refs):
    row_refs = refs[:8]
    router, w_in, w_out = refs[8:11]
    back_own, back_peer, rows, active, hidden_grad, val_grad, logit_grad = refs[11:]
    piece, width = row_refs[0].shape[0], rows.shape[1]
    expert = sc[4]
    for k, ref in enumerate(row_refs):
        rows[k * piece : (k + 1) * piece, :] = ref[:, :width]
    column = router[pl.ds(expert, 1), :]
    per = max(1, 512 // piece)
    for first in range(0, 8, per):
        here = slice(first * piece, (first + per) * piece)
        moe_in = rows[here, :]
        grads = jnp.concatenate([row_refs[k][:, width:] for k in range(first, first + per)], axis=0)
        live = grads[:, width + 2 : width + 3].astype(F32)
        grads = grads[:, :width].astype(F32)
        logit = jnp.sum(moe_in.astype(F32) * column, axis=-1, keepdims=True)
        gate = 1.0 / (1.0 + jnp.exp(-logit))
        value_grad = (gate * grads).astype(BF)
        hidden = dot(moe_in, w_in[...])
        bent = 0.5 * (1.0 + lax.erf(hidden * (0.5**0.5)))
        act = (hidden * bent).astype(BF)
        slope = bent + hidden * jnp.exp(-0.5 * hidden * hidden) * ((2.0 * jnp.pi) ** -0.5)
        pulled = (slope * dot_cols(value_grad, w_out[...])).astype(BF)
        part = dot(act, w_out[...])
        logit_part = jnp.sum(part * grads, axis=-1, keepdims=True) * (gate * (1.0 - gate) * live)
        back = (dot_cols(pulled, w_in[...]) + logit_part * column).astype(BF)
        value = (gate * part).astype(BF)
        active[here, :] = act
        hidden_grad[here, :] = pulled
        val_grad[here, :] = value_grad
        lane = lax.broadcasted_iota(jnp.int32, (logit_part.shape[0], LANES), 1)
        logit_grad[here, :] = jnp.where(lane == expert + 2, logit_part, 0.0).astype(BF)
        for k in range(first, first + per):
            at = slice((k - first) * piece, (k - first + 1) * piece)
            to = slice((k % 4) * piece, (k % 4 + 1) * piece)
            out = back_own if k < 4 else back_peer
            out[to, :width] = back[at, :]
            out[to, width:] = value[at, :]


def return_body(sc, back, after, tail, attn_own, attn_peer, gain, w_proj, mid, branch, gain_row, own, far, core):
    width = after.shape[1]
    upstream = back[:, :width].astype(F32)
    unit, scaling = norm_parts(after[...])
    gain_row[...] = jnp.sum(upstream * unit, axis=0, keepdims=True)
    total = tail[:, :width].astype(F32) + norm_pull(upstream * gain[...], unit, scaling)
    mid[...] = total
    low = total.astype(BF)
    branch[...] = low
    group = own.shape[1]
    w_own, w_peer = proj_rows(sc, w_proj, group)
    own[...] = dot_cols(low, w_own).astype(BF)
    pulled = dot_cols(low, w_peer).astype(BF)
    far[...] = pulled
    core[:, :group] = pulled
    core[:, group : 2 * group] = attn_own[...]
    core[:, 2 * group : 3 * group] = attn_peer[...]
    core[:, 3 * group :] = low


def projection_grad_body(
    sc, a00, a01, a10, a11, grads, cols, expert_rows, logit_grad, attn_in, own, peer, router_rows, attn_t, rows
):
    attn_t[...] = jnp.transpose(attn_in[...])
    router_rows[...] = dot_rows(logit_grad[...], expert_rows[...])[: router_rows.shape[0], :]
    span, group = a00.shape
    core = sc[2]
    for rel in range(2):
        at = jnp.bitwise_xor(sc[1], rel)
        rows[rel] = grads[at] * cols[at][:, 3:4]
    for half, out in enumerate((own, peer)):
        to = pl.ds(pl.multiple_of(jnp.bitwise_xor(core, half) * group, LANES), group)
        cut0, cut1 = rows[0, :, to], rows[1, :, to]
        for kind, (first, second) in enumerate(((a00, a10), (a01, a11))):
            at = pl.multiple_of(jnp.bitwise_xor(core, kind) * group, 16)
            total = dot_rows(first[:span, :], cut0) + dot_rows(second[...], cut1)
            out[pl.ds(at, group), :] = total.astype(BF)


def place_column(sc, cut, stride, parts, column, out):
    size = out.shape[0] // 4
    for rel, (part, offset) in enumerate(parts):
        first = jnp.bitwise_xor(sc[3], rel) * size
        for j in range(stride // cut):
            place = jnp.bitwise_xor(sc[4], j) * cut
            value = part[offset + j * cut : offset + (j + 1) * cut, pl.ds(column, LANES)].astype(F32)

            def store(place=place, value=value, first=first):
                out[pl.ds(pl.multiple_of(first + place, 16), cut), :] = value

            if stride > size:
                pl.when(place < size)(store)
            else:
                store()


def spread_proj_body(cut, sc, *refs):
    own, peer, out = refs[:4], refs[4], refs[5]
    step = pl.program_id(0)
    stride = own[0].shape[0]
    parts = [(ref, 0) for ref in own] + [(peer, rel * stride) for rel in range(4)]

    def write(side):
        place_column(sc, cut, stride, parts[4 * side : 4 * side + 4], pl.multiple_of(step % 3 * LANES, LANES), out)

    for side in range(2):
        pl.when(step // 3 == side)(functools.partial(write, side))


def spread_body(cut, group, pairs, sc, *refs):
    own, peer, second, out = refs[:4], refs[4], refs[5:13], refs[13]
    core, expert = sc[2], sc[4]
    size = out.shape[0]
    stride = own[0].shape[0]

    def write(rel):
        for half in range(2):
            side = jnp.bitwise_xor(core, half) * group
            first, offset = (peer, rel * stride) if half else (own[rel], 0)
            rest = second[4 * half + rel]
            for j in range(stride // cut):
                place = jnp.bitwise_xor(expert, j) * cut

                def store(place=place, j=j, side=side, first=first, offset=offset, rest=rest):
                    rows = pl.ds(pl.multiple_of(place, 16), cut)
                    for pair in range(pairs):
                        ref, start = (rest, j * cut) if pair else (first, offset + j * cut)
                        base = 3 * LANES * (pair - 1) if pair else group
                        for part in range(3):
                            at = base + part * LANES
                            to = pl.multiple_of(side + pair * LANES + 2 * part * group, LANES)
                            out[rows, pl.ds(to, LANES)] = ref[start : start + cut, at : at + LANES].astype(F32)

                if stride > size:
                    pl.when(place < size)(store)
                else:
                    store()

    for rel in range(4):
        pl.when(pl.program_id(0) == rel)(functools.partial(write, rel))


def small_body(experts, first, sc, own, peer, gain, attn_gain, moe_gain, router):
    rows = own[...].astype(F32) + peer[first : first + own.shape[0], :].astype(F32)
    attn_gain[...] = (rows[:1, :] / gain[...])[0]
    moe_gain[...] = rows[1]
    router[...] = rows[2 : 2 + experts, :]


def input_body(first, sc, x, grads, cols, mid, first_own, peer, second, gain, out):
    high = mid[...].astype(BF)
    rest = (mid[...] - high.astype(F32)).astype(BF)
    for rel in range(2):
        if rel == 0:
            upstream = first_own[...].astype(F32) + peer[first : first + first_own.shape[0], :].astype(F32)
        else:
            upstream = second[...].astype(F32)
        at = jnp.bitwise_xor(sc[1], rel)
        own_cols = cols[at]
        pick = one_hot(own_cols, mid.shape[0])
        total = (grads[at] * own_cols[:, 3:4]).astype(F32) + (dot(pick, high) + dot(pick, rest))
        unit, scaling = norm_parts(x[at].astype(F32))
        out[at] = (total + norm_pull(upstream * gain[...], unit, scaling)).astype(BF)


def pack_body(sc, *refs):
    at = 0
    for part in refs[:-1]:
        refs[-1][at : at + part.shape[0], :] = part[...]
        at += part.shape[0]


def output_body(sc, a00, a01, a10, a11, x, w_proj, cols, values, out):
    span, width = x.shape[1:]
    w_own, w_peer = proj_rows(sc, w_proj, a00.shape[1])
    for rel, (own, peer) in enumerate(((a00, a01), (a10, a11))):
        at = jnp.bitwise_xor(sc[1], rel)
        rows = x[at].astype(F32) + (dot(own[:span, :], w_own) + dot(peer[:span, :], w_peer))
        pick = one_hot(cols[at], values.shape[0])
        out[at] = (rows + dot(pick, values[:, width:])).astype(BF)


def local(
    blk_count,
    batch_count,
    x,
    gain_one,
    w_qkv,
    w_proj,
    gain_two,
    router,
    w_in,
    w_out,
    routes,
    quota,
    period,
    g,
):
    seq_count, span, width = x.shape
    group = width // 2
    experts = quota.shape[0]
    share = batch_count // experts
    assert blk_count == 4 and seq_count == 2 and share == 2
    blk, batch = lax.axis_index("blk"), lax.axis_index("batch")
    chip, core = blk // 2, blk % 2
    expert, half = batch // share, batch % share
    quarter = chip * 2 + half
    sc = jnp.concatenate([jnp.stack([blk, chip, core, quarter, expert]).astype(jnp.int32), period, quota])

    def to_blk(value, bits):
        return lax.ppermute(value, "blk", [(i, i ^ bits) for i in range(4)])

    def to_batch(value, bits):
        return lax.ppermute(value, "batch", [(i, i ^ bits) for i in range(batch_count)])

    def to_expert(value, bits):
        return to_batch(value, bits * share)

    def to_plane(value, rel):
        if rel == 1:
            return to_batch(value, 1)
        if rel == 2:
            return to_blk(value, 2)
        pairs = [
            (i * batch_count + j, (i ^ 2) * batch_count + (j ^ 1)) for i in range(4) for j in range(batch_count)
        ]
        return lax.ppermute(value, ("blk", "batch"), pairs)

    def third(j):
        return (w_qkv, (width, group), lambda s: (0, 2 * j + s[2]))

    mine = lax.dynamic_index_in_dim(x, chip, 0, keepdims=False)
    other = lax.dynamic_index_in_dim(x, 1 - chip, 0, keepdims=False)
    block_x = to_blk(other, 2)
    block_c = to_blk(mine, 1)

    gain_one_row, gain_two_row = gain_one.reshape(1, width), gain_two.reshape(1, width)

    seat_rows = experts * SEAT
    length = 4 * span
    piece = shape_of((span, group), BF)
    base_piece = shape_of((span + 16, group), BF)
    kept_piece = shape_of((seat_rows, group), BF)
    kept_rows = shape_of((seat_rows, width), BF)
    x_kept, tail, b00, b01, b10, b11, w_own, cols = run_kernel(
        prepare_body,
        sc,
        [x, g, routes, w_proj, third(0), third(1), third(2)],
        [
            kept_rows,
            shape_of((seat_rows, width + LANES), BF),
            base_piece,
            base_piece,
            base_piece,
            base_piece,
            shape_of((width, 3 * group), BF),
            shape_of((seq_count, span, LANES), BF),
        ],
        name="prepare",
    )
    block_x, b01, b10, b11 = together([block_x, b01, b10, b11])
    base = [b00, to_blk(b01, 1), to_blk(b10, 2), to_blk(b11, 3)]
    block_xc = to_blk(block_x, 1)
    pairs = group // LANES
    attn_in, qkv, mixed, stats, own0, own1, own2, own3, *powers = run_kernel(
        forward_body,
        sc,
        [mine, block_c, block_x, block_xc, gain_one_row, w_own],
        [
            shape_of((length, width), BF),
            shape_of((length, 3 * group), BF),
            shape_of((length, group), F32),
            shape_of((length, LANES), F32),
            piece,
            piece,
            piece,
            piece,
        ]
        + [shape_of((pairs, 2 * span, (i + 1) * span), BF) for i in range(4)],
        [pltpu.VMEM((4, span, group), BF)],
        name="attention_forward",
    )
    kept0, core_rows, kept2, kept3 = run_kernel(
        pick_body,
        sc,
        [own0, own1, own2, own3, *base],
        [kept_piece, shape_of((span + seat_rows, group), BF), kept_piece, kept_piece],
        name="pick_kept",
    )
    core_rows = to_blk(core_rows, 1)
    late = [kept0, core_rows, to_blk(kept2, 2), to_blk(kept3, 3)]
    own2, own3, *late = together([own2, own3, *late])
    core_rows = late[1]
    a10, a11 = to_blk(own2, 2), to_blk(own3, 3)
    row_box = shape_of((SEAT, 2 * width + LANES), BF)
    after_kept, attn_own, attn_peer, *boxes = run_kernel(
        project_body,
        sc,
        [
            kept0,
            (core_rows, (seat_rows, group), lambda s: (span // seat_rows, 0)) if span % seat_rows == 0 else core_rows[span:],
            *late[2:],
            x_kept,
            tail,
            w_proj,
            gain_two_row,
        ],
        [shape_of((seat_rows, width), F32), kept_piece, kept_piece] + [row_box] * experts,
        name="project",
    )

    order = [0, *reversed(range(1, experts))]
    parts = [to_expert(boxes[j], j) if j else boxes[0] for j in order]
    rows = jnp.concatenate(together([*parts, a10, a11])[:experts], axis=0)
    expert_rows = [rows] + [to_plane(rows, rel) for rel in (1, 2, 3)]
    expert_rows += [to_blk(part, 1) for part in expert_rows]
    total_rows = 8 * seat_rows
    hidden_units = w_in.shape[2]
    quad = shape_of((4 * seat_rows, 2 * width), BF)
    back_own, back_peer, rows, active, hidden_grad, val_grad, logit_grad = run_kernel(
        expert_body,
        sc,
        [*expert_rows, router.T.astype(F32), w_in[0], w_out[0]],
        [
            quad,
            quad,
            shape_of((total_rows, width), BF),
            shape_of((total_rows, hidden_units), BF),
            shape_of((total_rows, hidden_units), BF),
            shape_of((total_rows, width), BF),
            shape_of((total_rows, LANES), BF),
        ],
        name="expert",
    )
    def total_of(parts):
        parts = [part.astype(F32) for part in parts]
        while len(parts) > 1:
            parts = [left + right for left, right in zip(parts[::2], parts[1::2])]
        return parts[0].astype(BF)

    arrived = to_blk(back_peer, 1)
    parts = []
    for rel in range(4):
        at = slice(rel * seat_rows, (rel + 1) * seat_rows)
        part = total_of([back_own[at], arrived[at]])
        parts.append(part if rel == 0 else to_plane(part, rel))
    parts = together(parts)
    cuts = [total_of([part[n * SEAT : (n + 1) * SEAT] for part in parts]) for n in range(experts)]
    cuts = [cuts[order.index(j)] for j in range(experts)]
    back = jnp.concatenate(together([cuts[0]] + [to_expert(cuts[j], j) for j in range(1, experts)]), axis=0)

    extra = -(-(experts + 2) // 16) * 16
    proj_own, proj_peer, router_rows, attn_t = run_kernel(
        projection_grad_body,
        sc,
        [own0, core_rows, a10, a11, g, cols, rows, logit_grad, attn_in],
        [shape_of((width, group), BF)] * 2 + [shape_of((extra, width), F32), shape_of((width, length), BF)],
        [pltpu.VMEM((seq_count, span, width), BF)],
        name="projection_grad",
        after=[back_own],
    )
    proj_arrived = to_blk(proj_peer, 1)
    wide_cols = shape_of((width, LANES), F32)
    mid, branch, moe_row, m_own, m_far, m_core = run_kernel(
        return_body,
        sc,
        [back, after_kept, tail, attn_own, attn_peer, gain_two_row, w_proj],
        [
            shape_of((seat_rows, width), F32),
            kept_rows,
            shape_of((1, width), F32),
            kept_piece,
            kept_piece,
            shape_of((seat_rows, 3 * group + width), BF),
        ],
        name="return_rows",
        after=[router_rows, proj_arrived],
    )
    mix_late = [m_own, to_blk(m_core, 1), to_blk(m_own, 2), to_blk(m_far, 3)]

    size = width // 4
    cut = -(-size // (experts * 16)) * 16
    stride = experts * cut

    def scatter_plane(quarters):
        sent = [to_plane(quarters[rel], rel) for rel in (3, 2, 1)]
        return [quarters[0], *sent[::-1]]

    def sum_cuts(parts):
        return [total_of([part[j * cut : (j + 1) * cut] for part in parts]) for j in range(experts)]

    def sum_experts(cuts):
        return total_of(together([cuts[0]] + [to_expert(cuts[j], j) for j in range(1, experts)]))

    def halve_experts(cuts, bits, far):
        return [total_of([near, far[j * cut : (j + 1) * cut]]) for j, near in enumerate(cuts[:bits])]

    def far_cuts(cuts, bits):
        return to_expert(jnp.concatenate(cuts[bits:], axis=0), bits)

    def gather_experts(whole, before=()):
        parts = [whole] + [to_expert(whole, j) for j in range(1, experts)]
        return jnp.concatenate(together([*parts, *before])[:experts], axis=0)

    def gather_plane(column):
        return [column] + [to_plane(column, rel) for rel in (1, 2, 3)]


    tall = shape_of((length, LANES), BF)
    working = [
        pltpu.VMEM((length, LANES), BF),
        pltpu.VMEM((length, LANES), F32),
        pltpu.VMEM((length, LANES), F32),
    ]
    wide_one = group + 3 * LANES
    wide_two = 3 * LANES * (pairs - 1)
    operands = [*base, *mix_late, *powers, qkv, mixed, attn_t, stats, w_own]
    dq, dk, dv, *quarters_one, gain_sum = run_kernel(
        functools.partial(first_backward_body, cut),
        sc,
        [*operands, proj_own, proj_arrived, attn_own, attn_peer, branch],
        [tall, tall, tall] + [shape_of((stride, wide_one), BF)] * 4 + [wide_cols],
        working + [pltpu.VMEM((4 * stride, wide_one), BF)],
        name="attention_backward_one",
    )
    parts_one = scatter_plane(quarters_one)
    *grads, t0, t1, t2, t3 = run_kernel(
        functools.partial(second_backward_body, pairs, cut),
        sc,
        [*operands, gain_sum, moe_row, router_rows],
        [tall] * (3 * (pairs - 1)) + [shape_of((stride + extra, wide_two), BF)] * 4,
        working + [pltpu.VMEM((4 * stride, wide_two), BF)],
        name="attention_backward_two",
    )
    t1, t2, t3, *parts_one = together([t1, t2, t3, *parts_one])
    parts_two = scatter_plane([t0, t1, t2, t3])
    cuts_one, bits = sum_cuts(parts_one), experts // 2
    far = far_cuts(cuts_one, bits)
    part = shape_of((span, width), BF)
    near_piece = shape_of((span // 2, width), BF)
    first_own, sent, upper, lower, near, in_grad, out_grad = run_kernel(
        norm_grad_body,
        sc,
        [dq, dk, dv, *grads, w_own, rows, active, hidden_grad, val_grad],
        [
            part,
            part,
            near_piece,
            near_piece,
            part,
            shape_of((width, hidden_units), F32),
            shape_of((hidden_units, width), F32),
        ],
        name="norm_one_grad",
        flops=10e9,
    )
    upper, lower = to_blk(upper, 1), to_blk(lower, 1)
    *parts_two, out_grad = together([*parts_two, out_grad])
    upper, lower, *parts_two = together([upper, lower, *parts_two])
    second = to_blk(total_of([near, jnp.concatenate([upper, lower], axis=0)]), 2)
    while bits:
        cuts_one = halve_experts(cuts_one, bits, far)
        bits //= 2
        if bits:
            far = far_cuts(cuts_one, bits)
        if bits == 1:
            far, *_ = together([far, *parts_two])
    whole_one = cuts_one[0]
    column_one = gather_experts(whole_one, [second])
    small = total_of([part[stride:] for part in parts_two])
    whole_two = sum_experts([jnp.concatenate([piece, small], axis=0) for piece in sum_cuts(parts_two)])
    whole_two, small = whole_two[:cut], whole_two[cut:]
    one = gather_plane(column_one)
    sent, small, column_two, *one = together([sent, small, gather_experts(whole_two), *one])
    two = gather_plane(column_two)
    packed = [*one, small, sent]
    packed_rows = sum(part.shape[0] for part in packed)
    (pack,) = run_kernel(pack_body, sc, packed, [shape_of((packed_rows, width), BF)], name="pack")
    output = run_kernel(
        output_body,
        sc,
        [own0, core_rows, a10, a11, x, w_proj, cols, back],
        [shape_of(x.shape, BF)],
        name="output",
        after=[pack],
    )[0]
    pack = to_blk(pack, 1)
    input_grad = run_kernel(
        functools.partial(input_body, packed_rows - span),
        sc,
        [x, g, cols, mid, first_own, pack, second, gain_one_row],
        [shape_of(x.shape, BF)],
        name="input_grad",
    )[0]
    attn_gain, moe_gain, router_grad = run_kernel(
        functools.partial(small_body, experts, 4 * stride),
        sc,
        [small, pack, gain_one_row],
        [shape_of((width,), F32), shape_of((width,), F32), shape_of((experts, width), F32)],
        name="small_grads",
    )

    def grid_kernel(body, steps, arrays, out, block, index, name):
        return pl.pallas_call(
            body,
            grid_spec=pltpu.PrefetchScalarGridSpec(
                num_scalar_prefetch=1,
                grid=(steps,),
                in_specs=[pl.BlockSpec(memory_space=pltpu.VMEM)] * len(arrays),
                out_specs=pl.BlockSpec(block, index),
            ),
            out_shape=out,
            compiler_params=pltpu.CompilerParams(vmem_limit_bytes=16 * 1024 * 1024),
            name=name,
        )(sc, *arrays)

    proj_grad = grid_kernel(
        functools.partial(spread_proj_body, cut),
        6,
        [*one, pack],
        shape_of((width, width), F32),
        (width, LANES),
        lambda i, s: (0, jnp.bitwise_xor(s[2], i // 3) * pairs + i % 3),
        "spread_proj",
    )
    two[3], output, input_grad, proj_grad, attn_gain = together([two[3], output, input_grad, proj_grad, attn_gain])
    peers = [to_blk(two[0], 1), None, None, to_blk(two[3], 1)]
    two[1], two[2], peers[0], peers[3] = together([two[1], two[2], peers[0], peers[3]])
    peers[1], peers[2] = to_blk(two[1], 1), to_blk(two[2], 1)
    qkv_grad = grid_kernel(
        functools.partial(spread_body, cut, group, pairs),
        4,
        [*one, pack, *two, *peers],
        shape_of((width, 3 * width), F32),
        (size, 3 * width),
        lambda i, s: (jnp.bitwise_xor(s[3], i), 0),
        "spread",
    )
    return (
        output,
        input_grad,
        attn_gain,
        qkv_grad,
        proj_grad,
        moe_gain,
        router_grad.T,
        in_grad[None],
        out_grad[None],
    )


def solution(mesh):
    rows, kept = P("batch", "blk", None), P()
    w_in, w_out = P("batch", None, "blk"), P("batch", "blk", None)
    return jax.shard_map(
        functools.partial(local, mesh.shape["blk"], mesh.shape["batch"]),
        mesh=mesh,
        in_specs=(rows, kept, kept, kept, kept, kept, w_in, w_out, P("batch", "blk"), kept, P("batch"), rows),
        out_specs=(rows, rows, kept, kept, kept, kept, kept, w_in, w_out),
        check_vma=False,
    )
```

```python
import functools
import math

import jax
import jax.numpy as jnp
from jax import lax
from jax.experimental import pallas as pl
from jax.experimental.pallas import tpu as pltpu
from jax.sharding import PartitionSpec as P

HEAD_DIM = 64
CAP = 12
SEAT = 16
LANES = 128
EPSILON = 1e-05
FAR_BELOW = -1e30
BF = jnp.bfloat16
F32 = jnp.float32


def dot(left, right):
    return jnp.dot(left, right, preferred_element_type=F32)


def dot_rows(left, right):
    return lax.dot_general(left, right, (((0,), (0,)), ((), ())), preferred_element_type=F32)


def dot_cols(left, right):
    return lax.dot_general(left, right, (((1,), (1,)), ((), ())), preferred_element_type=F32)


def norm_parts(rows):
    centred = rows - jnp.mean(rows, axis=-1, keepdims=True)
    scaling = lax.rsqrt(jnp.mean(centred * centred, axis=-1, keepdims=True) + EPSILON)
    return centred * scaling, scaling


def norm_pull(scaled, unit, scaling):
    return scaling * (
        scaled
        - jnp.mean(scaled, axis=-1, keepdims=True)
        - unit * jnp.mean(scaled * unit, axis=-1, keepdims=True)
    )


def run_kernel(body, scalars, operands, outs, scratch=(), flops=0, name=None, after=()):
    specs, arrays, held = [], [], 0
    after, given, run = list(after), len(operands), body
    if after:

        def run(sc, *refs):
            body(sc, *refs[:given], *refs[given + len(after) :])

    for operand in operands:
        if isinstance(operand, tuple):
            array, block, index = operand
            held += 2 * math.prod(block) * array.dtype.itemsize
            specs.append(pl.BlockSpec(block, functools.partial(lambda i, s, fn: fn(s), fn=index)))
        else:
            array = operand
            held += array.size * array.dtype.itemsize
            specs.append(pl.BlockSpec(memory_space=pltpu.VMEM))
        arrays.append(array)
    specs += [pl.BlockSpec(memory_space=pl.ANY)] * len(after)
    held += sum(out.size * out.dtype.itemsize for out in outs)
    out_specs = [pl.BlockSpec(memory_space=pltpu.VMEM) for _ in outs]
    return pl.pallas_call(
        run,
        grid_spec=pltpu.PrefetchScalarGridSpec(
            num_scalar_prefetch=1,
            grid=(1,),
            in_specs=specs,
            out_specs=out_specs,
            scratch_shapes=list(scratch),
        ),
        out_shape=list(outs),
        compiler_params=pltpu.CompilerParams(vmem_limit_bytes=(16 if held < 24e6 else 60) * 1024 * 1024),
        cost_estimate=pl.CostEstimate(flops=int(flops), bytes_accessed=0, transcendentals=0),
        name=name,
    )(scalars, *arrays, *after)


def together(values):
    return list(lax.optimization_barrier(tuple(values)))


def shape_of(dims, dtype):
    return jax.ShapeDtypeStruct(dims, dtype)


def half_masks(scale):
    lane = lax.broadcasted_iota(jnp.int32, (1, LANES), 1)
    low = lane < HEAD_DIM
    return lane, low, (jnp.where(low, scale, 0.0).astype(BF), jnp.where(low, 0.0, scale).astype(BF))


def one_hot(cols, count):
    seat = cols[:, :1].astype(F32) * SEAT + cols[:, 1:2].astype(F32)
    slot = lax.broadcasted_iota(jnp.int32, (cols.shape[0], count), 1).astype(F32)
    return jnp.where(slot == seat, 1.0, 0.0).astype(BF)


def one_hot_rows(block, span, count):
    table = block[span : span + 16, :span].astype(F32)
    seat = table[:1, :] * SEAT + table[1:2, :]
    slot = lax.broadcasted_iota(jnp.int32, (count, span), 0).astype(F32)
    return jnp.where(slot == seat, 1.0, 0.0).astype(BF)


def forward_body(
    sc, m0, m1, m2, m3, gain, weights, attn_in, qkv, mixed, stats, o0, o1, o2, o3, p0, p1, p2, p3, pieces
):
    powers = (p0, p1, p2, p3)
    span, group = m2.shape[0], weights.shape[1] // 3
    place = sc[0]
    for rel, block in enumerate((m0, m1, m2, m3)):
        start = pl.multiple_of(jnp.bitwise_xor(place, rel) * span, span)
        unit, _ = norm_parts(block[...].astype(F32))
        normed = (unit * gain[...]).astype(BF)
        attn_in[pl.ds(start, span), :] = normed
        qkv[pl.ds(start, span), :] = dot(normed, weights[...]).astype(BF)
    lane, low, scaled = half_masks(HEAD_DIM**-0.5)
    row = jnp.bitwise_and(lax.broadcasted_iota(jnp.int32, (2 * span, span), 0), span - 1)
    col = lax.broadcasted_iota(jnp.int32, (2 * span, span), 1)
    causal = col <= row
    for i in range(4):
        past = i * span
        upto = past + span
        stat = jnp.zeros((span, LANES), F32)
        for g in range(group // LANES):
            at = g * LANES
            queries = qkv[past:upto, at : at + LANES]
            keys = qkv[0:upto, group + at : group + at + LANES]
            values = qkv[0:upto, 2 * group + at : 2 * group + at + LANES]
            both = jnp.concatenate([queries * scaled[0], queries * scaled[1]], axis=0)
            last = jnp.where(causal, dot_cols(both, keys[past:]), FAR_BELOW)
            top = jnp.max(last, axis=-1, keepdims=True)
            if i:
                first = dot_cols(both, keys[:past])
                top = jnp.maximum(top, jnp.max(first, axis=-1, keepdims=True))
            beside = jnp.concatenate([values, jnp.ones_like(values)], axis=1)
            raised = jnp.exp(last - top).astype(BF)
            powers[i][g, :, past:] = raised
            mix = dot(raised, beside[past:])
            if i:
                raised = jnp.exp(first - top).astype(BF)
                powers[i][g, :, :past] = raised
                mix = mix + dot(raised, beside[:past])
            scale = 1.0 / mix[:, LANES:]
            mix = mix[:, :LANES] * scale
            mix = jnp.where(low, mix[:span], mix[span:])
            for u in range(2):
                stat = jnp.where(lane == 2 * g + u, scale[u * span : (u + 1) * span], stat)
            mixed[past:upto, at : at + LANES] = mix
            pieces[jnp.bitwise_xor(place, i), :, at : at + LANES] = mix.astype(BF)
        stats[past:upto, :] = stat
    for rel, out in enumerate((o0, o1, o2, o3)):
        out[...] = pieces[rel]


def pick_body(sc, o0, o1, o2, o3, b0, b1, b2, b3, k0, core, k2, k3):
    span, group = o0.shape
    for out, rows, base in ((k0, o0, b0), (core, o1, b1), (k2, o2, b2), (k3, o3, b3)):
        kept = dot(one_hot_rows(base, span, k0.shape[0]), rows[...]).astype(BF)
        if out is core:
            core[:span, :] = rows[...]
            core[span:, :] = kept
        else:
            out[...] = kept


def pair_backward(stats, pair, qkv, mixed, powers, dmix, dq, dk, dv, dk_sum, dv_sum):
    span, group, head = qkv.shape[0] // 4, qkv.shape[1] // 3, 2 * pair
    at = [slice(j * group + pair * LANES, j * group + (pair + 1) * LANES) for j in range(3)]
    scale = HEAD_DIM**-0.5
    _, low, ones = half_masks(1.0)
    _, _, scaled = half_masks(scale)
    for i in reversed(range(4)):
        past = i * span
        upto = past + span
        queries = qkv[past:upto, at[0]]
        keys = qkv[0:upto, at[1]]
        values = qkv[0:upto, at[2]]
        over = jnp.where(low, stats[past:upto, head : head + 1], stats[past:upto, head + 1 : head + 2])
        grads = (dmix[past:upto, :].astype(F32) * over).astype(BF)
        product = grads.astype(F32) * mixed[past:upto, at[0]]
        query = [queries * scaled[u] for u in range(2)]
        grad = [grads * ones[u] for u in range(2)]
        pulls = [dot_cols(grad[u], values) for u in range(2)]
        halves, sums = [], {}
        for u in range(2):
            delta = jnp.sum(jnp.where(low == (u == 0), product, 0.0), axis=-1, keepdims=True)
            half = None
            for rows in (slice(past, upto), slice(0, past))[: 2 if i else 1]:
                weights = powers[i][pair, u * span : (u + 1) * span, rows]
                score_grad = (weights.astype(F32) * (pulls[u][:, rows] - delta)).astype(BF)
                part = dot(score_grad, keys[rows])
                half = part if half is None else half + part
                for name, left, right in (("k", score_grad, query[u]), ("v", weights, grad[u])):
                    part = dot_rows(left, right)
                    sums[name, rows.start] = sums[name, rows.start] + part if u else part
            halves.append(half)
        for (name, start), part in sums.items():
            out = dk_sum if name == "k" else dv_sum
            rows = slice(start, upto if start == past else past)
            out[rows, :] = part if i == 3 else out[rows, :] + part
        dq[past:upto, :] = (jnp.where(low, halves[0], halves[1]) * scale).astype(BF)
    dk[...] = dk_sum[...].astype(BF)
    dv[...] = dv_sum[...].astype(BF)


def stage_rows(held, columns, value, stride):
    size = value.shape[0] // 4
    for k in range(4):
        held[k * stride : k * stride + size, columns] = value[k * size : (k + 1) * size, :]
        if stride > size:
            held[k * stride + size : (k + 1) * stride, columns] = jnp.zeros((stride - size, value.shape[1]), BF)


def place_cuts(cut, quarter, expert, held, outs, stride):
    for rel, out in enumerate(outs):
        first = jnp.bitwise_xor(quarter, rel) * stride
        for j in range(stride // cut):
            at = pl.multiple_of(first + jnp.bitwise_xor(expert, j) * cut, 16)
            out[j * cut : (j + 1) * cut, :] = held[pl.ds(at, cut), :]


def load_grads(place, pair, blocks, kept, dmix):
    span = dmix.shape[0] // 4
    at = slice(pair * LANES, (pair + 1) * LANES)
    for rel, block in enumerate(blocks):
        start = pl.multiple_of(jnp.bitwise_xor(place, rel) * span, span)
        late = dot_rows(one_hot_rows(block, span, kept[rel].shape[0]), kept[rel][:, at])
        dmix[pl.ds(start, span), :] = (block[:span, at].astype(F32) + late).astype(BF)


def weight_columns(attn_t, sources, weights, pair, held, first, stride):
    total, group = None, weights.shape[1] // 3
    grad = dot(attn_t[...], jnp.concatenate([source[...] for source in sources], axis=1))
    stage_rows(held, slice(first, first + 3 * LANES), grad.astype(BF), stride)
    for j in range(3):
        at = j * group + pair * LANES
        part = grad[:, j * LANES : (j + 1) * LANES] * weights[:, at : at + LANES].astype(F32)
        total = part if total is None else total + part
    return jnp.sum(total, axis=-1, keepdims=True)


def first_backward_body(cut, sc, *refs):
    base, late, powers, rest = refs[:4], refs[4:8], refs[8:12], refs[12:]
    qkv, mixed, attn_t, stats, weights, proj_own, proj_peer, attn_own, attn_peer, branch = rest[:10]
    dq, dk, dv, w0, w1, w2, w3, gain_sum, dmix, dk_sum, dv_sum, held = rest[10:]
    stride, group, core_late = w0.shape[0], proj_own.shape[1], late[1]
    load_grads(sc[0], 0, base, late, dmix)
    pair_backward(stats, 0, qkv, mixed, powers, dmix, dq, dk, dv, dk_sum, dv_sum)
    core = sc[2]
    to = pl.multiple_of(core * group, LANES)
    rows = branch[:, pl.ds(to, group)]
    rows_peer = core_late[:, pl.ds(pl.multiple_of(3 * group + to, LANES), group)]
    mine = dot_rows(attn_own[...], rows) + dot_rows(core_late[:, 2 * group : 3 * group], rows_peer)
    others = dot_rows(attn_peer[...], rows) + dot_rows(core_late[:, group : 2 * group], rows_peer)
    both = jnp.concatenate([jnp.where(core == 0, mine, others), jnp.where(core == 0, others, mine)], axis=0)
    both = (proj_own[...].astype(F32) + proj_peer[...].astype(F32) + both).astype(BF)
    stage_rows(held, slice(0, group), both, stride)
    sums = weight_columns(attn_t, (dq, dk, dv), weights, 0, held, group, stride)
    gain_sum[...] = jnp.broadcast_to(sums, gain_sum.shape)
    place_cuts(cut, sc[3], sc[4], held, (w0, w1, w2, w3), stride)


def second_backward_body(pairs, cut, sc, *refs):
    base, late, powers, rest = refs[:4], refs[4:8], refs[8:12], refs[12:]
    qkv, mixed, attn_t, stats, weights, gain_sum, moe_row, router_rows = rest[:8]
    grads, rest = rest[8 : 8 + 3 * (pairs - 1)], rest[8 + 3 * (pairs - 1) :]
    outs, (dmix, dk_sum, dv_sum, held) = rest[:4], rest[4:]
    extra = router_rows.shape[0]
    stride = outs[0].shape[0] - extra
    sums = gain_sum[:, :1]
    for n in range(pairs - 1):
        own = grads[3 * n : 3 * n + 3]
        load_grads(sc[0], n + 1, base, late, dmix)
        pair_backward(stats, n + 1, qkv, mixed, powers, dmix, *own, dk_sum, dv_sum)
        sums = sums + weight_columns(attn_t, own, weights, n + 1, held, 3 * LANES * n, stride)
    place_cuts(cut, sc[3], sc[4], held, outs, stride)
    row = lax.broadcasted_iota(jnp.int32, router_rows.shape, 0)
    gain_row = jnp.transpose(jnp.broadcast_to(sums, gain_sum.shape))[:1, :]
    small = jnp.where(row == 0, gain_row, jnp.where(row == 1, moe_row[...], router_rows[...])).astype(BF)
    for out in outs:
        out[stride:, :] = small


def norm_grad_body(sc, *refs):
    grads, (weights, rows_in, active, hidden_grad, val_grad, *outs) = refs[:-12], refs[-12:]
    own, sent, upper, lower, kept, in_grad, out_grad = outs
    span = own.shape[0]
    in_grad[...] = dot_rows(rows_in[...], hidden_grad[...])
    out_grad[...] = dot_rows(active[...], val_grad[...])
    for j in range(4):
        rows = pl.ds(pl.multiple_of(jnp.bitwise_xor(sc[0], j) * span, span), span)
        cols = [grads[n][rows, :] for part in range(3) for n in range(part, len(grads), 3)]
        grad = dot_cols(jnp.concatenate(cols, axis=1), weights[...]).astype(BF)
        if j == 3:
            upper[...] = grad[: span // 2]
            lower[...] = grad[span // 2 :]
        else:
            (own, sent, kept)[j][...] = grad


def proj_rows(sc, w_proj, group):
    return [
        w_proj[pl.ds(pl.multiple_of(jnp.bitwise_xor(sc[2], flip) * group, 16), group), :] for flip in range(2)
    ]


def prepare_body(
    sc, x, grads, routes, w_proj, wq, wk, wv, x_kept, tail, b00, b01, b10, b11, w_own, cols
):
    seqs, span, width = x.shape
    group, count = wq.shape[1], x_kept.shape[0]
    experts = count // SEAT
    for j, weight in enumerate((wq, wk, wv)):
        w_own[:, j * group : (j + 1) * group] = weight[...]
    proj_own, proj_peer = proj_rows(sc, w_proj, group)
    earlier = lax.broadcasted_iota(jnp.int32, (span, span), 0) < lax.broadcasted_iota(jnp.int32, (span, span), 1)
    earlier = jnp.where(earlier, 1.0, 0.0).astype(BF)
    ids = lax.broadcasted_iota(jnp.int32, (max(8, experts), span), 0)
    slots = lax.broadcasted_iota(jnp.int32, (count, span), 0)
    rows_of = lax.broadcasted_iota(jnp.int32, (LANES, span), 0)
    seen = jnp.zeros((max(8, experts), 1), F32)
    x_sum, tail_sum, flag_sum, tables = None, None, None, []
    for n in range(seqs):
        route = routes[n : n + 1, :]
        mine = jnp.where(ids == route, 1.0, 0.0)
        before = dot(mine.astype(BF), earlier) + seen
        rank = jnp.sum(mine * before, axis=0, keepdims=True)
        seen = seen + jnp.sum(mine, axis=1, keepdims=True)
        limit = jnp.zeros((1, span), jnp.int32)
        for e in range(experts):
            limit = jnp.where(route == e, sc[7 + e], limit)
        kept = rank < limit.astype(F32)
        place = jnp.bitwise_xor(route, sc[4])
        seat = jnp.where(kept, place * SEAT + rank.astype(jnp.int32), -1)
        pick = jnp.where(slots == seat, 1.0, 0.0).astype(BF)
        live = jnp.where(sc[5 + n] == 1, F32(1.0), F32(0.0))
        table = jnp.where(rows_of == 0, jnp.where(kept, place.astype(F32), -1.0), 0.0)
        table = jnp.where(rows_of == 1, jnp.where(kept, rank, 0.0), table)
        table = jnp.where(rows_of == 2, live, table)
        table = jnp.where(rows_of == 3, jnp.where(kept, 0.0, 1.0), table)
        tables.append(table[:16, :].astype(BF))
        columns = jnp.transpose(table).astype(BF)
        cols[n] = columns
        parts = dot(pick, x[n]), dot(pick, grads[n]), dot(pick, columns)
        x_sum = parts[0] if n == 0 else x_sum + parts[0]
        tail_sum = parts[1] if n == 0 else tail_sum + parts[1]
        flag_sum = parts[2] if n == 0 else flag_sum + parts[2]
    x_kept[...] = x_sum.astype(BF)
    tail[:, :width] = tail_sum.astype(BF)
    tail[:, width:] = flag_sum.astype(BF)
    for rel, (own, peer) in enumerate(((b00, b01), (b10, b11))):
        at = jnp.bitwise_xor(sc[1], rel)
        own_cols = cols[at]
        rows = grads[at] * own_cols[:, 3:4]
        for out, weight in ((own, proj_own), (peer, proj_peer)):
            out[:span, :] = dot_cols(rows, weight).astype(BF)
            out[span:, :span] = jnp.where(at == 0, tables[0], tables[1])
            if group > span:
                out[span:, span:] = jnp.zeros((out.shape[0] - span, group - span), BF)


def project_body(sc, k00, k01, k10, k11, x_kept, tail, w_proj, gain, after, own, peer, *boxes):
    own[...] = k00[...] + k10[...]
    peer[...] = k01[...] + k11[...]
    w_own, w_peer = proj_rows(sc, w_proj, own.shape[1])
    rows = x_kept[...].astype(F32) + (dot(own[...], w_own) + dot(peer[...], w_peer))
    after[...] = rows
    unit, _ = norm_parts(rows)
    moe_in = (unit * gain[...]).astype(BF)
    width = moe_in.shape[1]
    for j, box in enumerate(boxes):
        at = slice(j * SEAT, (j + 1) * SEAT)
        box[:, :width] = moe_in[at, :]
        box[:, width:] = tail[at, :]


def expert_body(sc, *refs):
    row_refs = refs[:8]
    router, w_in, w_out = refs[8:11]
    back_own, back_peer, rows, active, hidden_grad, val_grad, logit_grad = refs[11:]
    piece, width = row_refs[0].shape[0], rows.shape[1]
    expert = sc[4]
    for k, ref in enumerate(row_refs):
        rows[k * piece : (k + 1) * piece, :] = ref[:, :width]
    column = router[pl.ds(expert, 1), :]
    per = max(1, 512 // piece)
    for first in range(0, 8, per):
        here = slice(first * piece, (first + per) * piece)
        moe_in = rows[here, :]
        grads = jnp.concatenate([row_refs[k][:, width:] for k in range(first, first + per)], axis=0)
        live = grads[:, width + 2 : width + 3].astype(F32)
        grads = grads[:, :width].astype(F32)
        logit = jnp.sum(moe_in.astype(F32) * column, axis=-1, keepdims=True)
        gate = 1.0 / (1.0 + jnp.exp(-logit))
        value_grad = (gate * grads).astype(BF)
        hidden = dot(moe_in, w_in[...])
        bent = 0.5 * (1.0 + lax.erf(hidden * (0.5**0.5)))
        act = (hidden * bent).astype(BF)
        slope = bent + hidden * jnp.exp(-0.5 * hidden * hidden) * ((2.0 * jnp.pi) ** -0.5)
        pulled = (slope * dot_cols(value_grad, w_out[...])).astype(BF)
        part = dot(act, w_out[...])
        logit_part = jnp.sum(part * grads, axis=-1, keepdims=True) * (gate * (1.0 - gate) * live)
        back = (dot_cols(pulled, w_in[...]) + logit_part * column).astype(BF)
        value = (gate * part).astype(BF)
        active[here, :] = act
        hidden_grad[here, :] = pulled
        val_grad[here, :] = value_grad
        lane = lax.broadcasted_iota(jnp.int32, (logit_part.shape[0], LANES), 1)
        logit_grad[here, :] = jnp.where(lane == expert + 2, logit_part, 0.0).astype(BF)
        for k in range(first, first + per):
            at = slice((k - first) * piece, (k - first + 1) * piece)
            to = slice((k % 4) * piece, (k % 4 + 1) * piece)
            out = back_own if k < 4 else back_peer
            out[to, :width] = back[at, :]
            out[to, width:] = value[at, :]


def return_body(sc, back, after, tail, attn_own, attn_peer, gain, w_proj, mid, branch, gain_row, own, far, core):
    width = after.shape[1]
    upstream = back[:, :width].astype(F32)
    unit, scaling = norm_parts(after[...])
    gain_row[...] = jnp.sum(upstream * unit, axis=0, keepdims=True)
    total = tail[:, :width].astype(F32) + norm_pull(upstream * gain[...], unit, scaling)
    mid[...] = total
    low = total.astype(BF)
    branch[...] = low
    group = own.shape[1]
    w_own, w_peer = proj_rows(sc, w_proj, group)
    own[...] = dot_cols(low, w_own).astype(BF)
    pulled = dot_cols(low, w_peer).astype(BF)
    far[...] = pulled
    core[:, :group] = pulled
    core[:, group : 2 * group] = attn_own[...]
    core[:, 2 * group : 3 * group] = attn_peer[...]
    core[:, 3 * group :] = low


def projection_grad_body(
    sc, a00, a01, a10, a11, grads, cols, expert_rows, logit_grad, attn_in, own, peer, router_rows, attn_t, rows
):
    attn_t[...] = jnp.transpose(attn_in[...])
    router_rows[...] = dot_rows(logit_grad[...], expert_rows[...])[: router_rows.shape[0], :]
    span, group = a00.shape
    core = sc[2]
    for rel in range(2):
        at = jnp.bitwise_xor(sc[1], rel)
        rows[rel] = grads[at] * cols[at][:, 3:4]
    for half, out in enumerate((own, peer)):
        to = pl.ds(pl.multiple_of(jnp.bitwise_xor(core, half) * group, LANES), group)
        cut0, cut1 = rows[0, :, to], rows[1, :, to]
        for kind, (first, second) in enumerate(((a00, a10), (a01, a11))):
            at = pl.multiple_of(jnp.bitwise_xor(core, kind) * group, 16)
            total = dot_rows(first[:span, :], cut0) + dot_rows(second[...], cut1)
            out[pl.ds(at, group), :] = total.astype(BF)


def place_column(sc, cut, stride, parts, column, out):
    size = out.shape[0] // 4
    for rel, (part, offset) in enumerate(parts):
        first = jnp.bitwise_xor(sc[3], rel) * size
        for j in range(stride // cut):
            place = jnp.bitwise_xor(sc[4], j) * cut
            value = part[offset + j * cut : offset + (j + 1) * cut, pl.ds(column, LANES)].astype(F32)

            def store(place=place, value=value, first=first):
                out[pl.ds(pl.multiple_of(first + place, 16), cut), :] = value

            if stride > size:
                pl.when(place < size)(store)
            else:
                store()


def spread_proj_body(cut, sc, *refs):
    own, peer, out = refs[:4], refs[4], refs[5]
    step = pl.program_id(0)
    stride = own[0].shape[0]
    parts = [(ref, 0) for ref in own] + [(peer, rel * stride) for rel in range(4)]

    def write(side):
        place_column(sc, cut, stride, parts[4 * side : 4 * side + 4], pl.multiple_of(step % 3 * LANES, LANES), out)

    for side in range(2):
        pl.when(step // 3 == side)(functools.partial(write, side))


def spread_body(cut, group, pairs, sc, *refs):
    own, peer, second, out = refs[:4], refs[4], refs[5:13], refs[13]
    core, expert = sc[2], sc[4]
    size = out.shape[0]
    stride = own[0].shape[0]

    def write(rel):
        for half in range(2):
            side = jnp.bitwise_xor(core, half) * group
            first, offset = (peer, rel * stride) if half else (own[rel], 0)
            rest = second[4 * half + rel]
            for j in range(stride // cut):
                place = jnp.bitwise_xor(expert, j) * cut

                def store(place=place, j=j, side=side, first=first, offset=offset, rest=rest):
                    rows = pl.ds(pl.multiple_of(place, 16), cut)
                    for pair in range(pairs):
                        ref, start = (rest, j * cut) if pair else (first, offset + j * cut)
                        base = 3 * LANES * (pair - 1) if pair else group
                        for part in range(3):
                            at = base + part * LANES
                            to = pl.multiple_of(side + pair * LANES + 2 * part * group, LANES)
                            out[rows, pl.ds(to, LANES)] = ref[start : start + cut, at : at + LANES].astype(F32)

                if stride > size:
                    pl.when(place < size)(store)
                else:
                    store()

    for rel in range(4):
        pl.when(pl.program_id(0) == rel)(functools.partial(write, rel))


def small_body(experts, first, sc, own, peer, gain, attn_gain, moe_gain, router):
    rows = own[...].astype(F32) + peer[first : first + own.shape[0], :].astype(F32)
    attn_gain[...] = (rows[:1, :] / gain[...])[0]
    moe_gain[...] = rows[1]
    router[...] = rows[2 : 2 + experts, :]


def input_body(first, sc, x, grads, cols, mid, first_own, peer, second, gain, out):
    high = mid[...].astype(BF)
    rest = (mid[...] - high.astype(F32)).astype(BF)
    for rel in range(2):
        if rel == 0:
            upstream = first_own[...].astype(F32) + peer[first : first + first_own.shape[0], :].astype(F32)
        else:
            upstream = second[...].astype(F32)
        at = jnp.bitwise_xor(sc[1], rel)
        own_cols = cols[at]
        pick = one_hot(own_cols, mid.shape[0])
        total = (grads[at] * own_cols[:, 3:4]).astype(F32) + (dot(pick, high) + dot(pick, rest))
        unit, scaling = norm_parts(x[at].astype(F32))
        out[at] = (total + norm_pull(upstream * gain[...], unit, scaling)).astype(BF)


def pack_body(sc, *refs):
    at = 0
    for part in refs[:-1]:
        refs[-1][at : at + part.shape[0], :] = part[...]
        at += part.shape[0]


def output_body(sc, a00, a01, a10, a11, x, w_proj, cols, values, out):
    span, width = x.shape[1:]
    w_own, w_peer = proj_rows(sc, w_proj, a00.shape[1])
    for rel, (own, peer) in enumerate(((a00, a01), (a10, a11))):
        at = jnp.bitwise_xor(sc[1], rel)
        rows = x[at].astype(F32) + (dot(own[:span, :], w_own) + dot(peer[:span, :], w_peer))
        pick = one_hot(cols[at], values.shape[0])
        out[at] = (rows + dot(pick, values[:, width:])).astype(BF)


def local(
    blk_count,
    batch_count,
    x,
    gain_one,
    w_qkv,
    w_proj,
    gain_two,
    router,
    w_in,
    w_out,
    routes,
    quota,
    period,
    g,
):
    seq_count, span, width = x.shape
    group = width // 2
    experts = quota.shape[0]
    share = batch_count // experts
    assert blk_count == 4 and seq_count == 2 and share == 2
    blk, batch = lax.axis_index("blk"), lax.axis_index("batch")
    chip, core = blk // 2, blk % 2
    expert, half = batch // share, batch % share
    quarter = chip * 2 + half
    sc = jnp.concatenate([jnp.stack([blk, chip, core, quarter, expert]).astype(jnp.int32), period, quota])

    def to_blk(value, bits):
        return lax.ppermute(value, "blk", [(i, i ^ bits) for i in range(4)])

    def to_batch(value, bits):
        return lax.ppermute(value, "batch", [(i, i ^ bits) for i in range(batch_count)])

    def to_expert(value, bits):
        return to_batch(value, bits * share)

    def to_plane(value, rel):
        if rel == 1:
            return to_batch(value, 1)
        if rel == 2:
            return to_blk(value, 2)
        pairs = [
            (i * batch_count + j, (i ^ 2) * batch_count + (j ^ 1)) for i in range(4) for j in range(batch_count)
        ]
        return lax.ppermute(value, ("blk", "batch"), pairs)

    def third(j):
        return (w_qkv, (width, group), lambda s: (0, 2 * j + s[2]))

    mine = lax.dynamic_index_in_dim(x, chip, 0, keepdims=False)
    other = lax.dynamic_index_in_dim(x, 1 - chip, 0, keepdims=False)
    block_x = to_blk(other, 2)
    block_c = to_blk(mine, 1)

    gain_one_row, gain_two_row = gain_one.reshape(1, width), gain_two.reshape(1, width)

    seat_rows = experts * SEAT
    length = 4 * span
    piece = shape_of((span, group), BF)
    base_piece = shape_of((span + 16, group), BF)
    kept_piece = shape_of((seat_rows, group), BF)
    kept_rows = shape_of((seat_rows, width), BF)
    x_kept, tail, b00, b01, b10, b11, w_own, cols = run_kernel(
        prepare_body,
        sc,
        [x, g, routes, w_proj, third(0), third(1), third(2)],
        [
            kept_rows,
            shape_of((seat_rows, width + LANES), BF),
            base_piece,
            base_piece,
            base_piece,
            base_piece,
            shape_of((width, 3 * group), BF),
            shape_of((seq_count, span, LANES), BF),
        ],
        name="prepare",
    )
    block_x, b01, b10, b11 = together([block_x, b01, b10, b11])
    base = [b00, to_blk(b01, 1), to_blk(b10, 2), to_blk(b11, 3)]
    block_xc = to_blk(block_x, 1)
    pairs = group // LANES
    attn_in, qkv, mixed, stats, own0, own1, own2, own3, *powers = run_kernel(
        forward_body,
        sc,
        [mine, block_c, block_x, block_xc, gain_one_row, w_own],
        [
            shape_of((length, width), BF),
            shape_of((length, 3 * group), BF),
            shape_of((length, group), F32),
            shape_of((length, LANES), F32),
            piece,
            piece,
            piece,
            piece,
        ]
        + [shape_of((pairs, 2 * span, (i + 1) * span), BF) for i in range(4)],
        [pltpu.VMEM((4, span, group), BF)],
        name="attention_forward",
    )
    kept0, core_rows, kept2, kept3 = run_kernel(
        pick_body,
        sc,
        [own0, own1, own2, own3, *base],
        [kept_piece, shape_of((span + seat_rows, group), BF), kept_piece, kept_piece],
        name="pick_kept",
    )
    core_rows = to_blk(core_rows, 1)
    late = [kept0, core_rows, to_blk(kept2, 2), to_blk(kept3, 3)]
    own2, own3, *late = together([own2, own3, *late])
    core_rows = late[1]
    a10, a11 = to_blk(own2, 2), to_blk(own3, 3)
    row_box = shape_of((SEAT, 2 * width + LANES), BF)
    after_kept, attn_own, attn_peer, *boxes = run_kernel(
        project_body,
        sc,
        [
            kept0,
            (core_rows, (seat_rows, group), lambda s: (span // seat_rows, 0)) if span % seat_rows == 0 else core_rows[span:],
            *late[2:],
            x_kept,
            tail,
            w_proj,
            gain_two_row,
        ],
        [shape_of((seat_rows, width), F32), kept_piece, kept_piece] + [row_box] * experts,
        name="project",
    )

    order = [0, *reversed(range(1, experts))]
    parts = [to_expert(boxes[j], j) if j else boxes[0] for j in order]
    rows = jnp.concatenate(together([*parts, a10, a11])[:experts], axis=0)
    expert_rows = [rows] + [to_plane(rows, rel) for rel in (1, 2, 3)]
    expert_rows += [to_blk(part, 1) for part in expert_rows]
    total_rows = 8 * seat_rows
    hidden_units = w_in.shape[2]
    quad = shape_of((4 * seat_rows, 2 * width), BF)
    back_own, back_peer, rows, active, hidden_grad, val_grad, logit_grad = run_kernel(
        expert_body,
        sc,
        [*expert_rows, router.T.astype(F32), w_in[0], w_out[0]],
        [
            quad,
            quad,
            shape_of((total_rows, width), BF),
            shape_of((total_rows, hidden_units), BF),
            shape_of((total_rows, hidden_units), BF),
            shape_of((total_rows, width), BF),
            shape_of((total_rows, LANES), BF),
        ],
        name="expert",
    )
    def total_of(parts):
        parts = [part.astype(F32) for part in parts]
        while len(parts) > 1:
            parts = [left + right for left, right in zip(parts[::2], parts[1::2])]
        return parts[0].astype(BF)

    arrived = to_blk(back_peer, 1)
    parts = []
    for rel in range(4):
        at = slice(rel * seat_rows, (rel + 1) * seat_rows)
        part = total_of([back_own[at], arrived[at]])
        parts.append(part if rel == 0 else to_plane(part, rel))
    parts = together(parts)
    cuts = [total_of([part[n * SEAT : (n + 1) * SEAT] for part in parts]) for n in range(experts)]
    cuts = [cuts[order.index(j)] for j in range(experts)]
    back = jnp.concatenate(together([cuts[0]] + [to_expert(cuts[j], j) for j in range(1, experts)]), axis=0)

    extra = -(-(experts + 2) // 16) * 16
    proj_own, proj_peer, router_rows, attn_t = run_kernel(
        projection_grad_body,
        sc,
        [own0, core_rows, a10, a11, g, cols, rows, logit_grad, attn_in],
        [shape_of((width, group), BF)] * 2 + [shape_of((extra, width), F32), shape_of((width, length), BF)],
        [pltpu.VMEM((seq_count, span, width), BF)],
        name="projection_grad",
        after=[back_own],
    )
    proj_arrived = to_blk(proj_peer, 1)
    wide_cols = shape_of((width, LANES), F32)
    mid, branch, moe_row, m_own, m_far, m_core = run_kernel(
        return_body,
        sc,
        [back, after_kept, tail, attn_own, attn_peer, gain_two_row, w_proj],
        [
            shape_of((seat_rows, width), F32),
            kept_rows,
            shape_of((1, width), F32),
            kept_piece,
            kept_piece,
            shape_of((seat_rows, 3 * group + width), BF),
        ],
        name="return_rows",
        after=[router_rows, proj_arrived],
    )
    mix_late = [m_own, to_blk(m_core, 1), to_blk(m_own, 2), to_blk(m_far, 3)]

    size = width // 4
    cut = -(-size // (experts * 16)) * 16
    stride = experts * cut

    def scatter_plane(quarters):
        sent = [to_plane(quarters[rel], rel) for rel in (3, 2, 1)]
        return [quarters[0], *sent[::-1]]

    def sum_cuts(parts):
        return [total_of([part[j * cut : (j + 1) * cut] for part in parts]) for j in range(experts)]

    def sum_experts(cuts):
        return total_of(together([cuts[0]] + [to_expert(cuts[j], j) for j in range(1, experts)]))

    def halve_experts(cuts, bits, far):
        return [total_of([near, far[j * cut : (j + 1) * cut]]) for j, near in enumerate(cuts[:bits])]

    def far_cuts(cuts, bits):
        return to_expert(jnp.concatenate(cuts[bits:], axis=0), bits)

    def gather_experts(whole, before=()):
        parts = [whole] + [to_expert(whole, j) for j in range(1, experts)]
        return jnp.concatenate(together([*parts, *before])[:experts], axis=0)

    def gather_plane(column):
        return [column] + [to_plane(column, rel) for rel in (1, 2, 3)]


    tall = shape_of((length, LANES), BF)
    working = [
        pltpu.VMEM((length, LANES), BF),
        pltpu.VMEM((length, LANES), F32),
        pltpu.VMEM((length, LANES), F32),
    ]
    wide_one = group + 3 * LANES
    wide_two = 3 * LANES * (pairs - 1)
    operands = [*base, *mix_late, *powers, qkv, mixed, attn_t, stats, w_own]
    dq, dk, dv, *quarters_one, gain_sum = run_kernel(
        functools.partial(first_backward_body, cut),
        sc,
        [*operands, proj_own, proj_arrived, attn_own, attn_peer, branch],
        [tall, tall, tall] + [shape_of((stride, wide_one), BF)] * 4 + [wide_cols],
        working + [pltpu.VMEM((4 * stride, wide_one), BF)],
        name="attention_backward_one",
    )
    parts_one = scatter_plane(quarters_one)
    *grads, t0, t1, t2, t3 = run_kernel(
        functools.partial(second_backward_body, pairs, cut),
        sc,
        [*operands, gain_sum, moe_row, router_rows],
        [tall] * (3 * (pairs - 1)) + [shape_of((stride + extra, wide_two), BF)] * 4,
        working + [pltpu.VMEM((4 * stride, wide_two), BF)],
        name="attention_backward_two",
    )
    t1, t2, t3, *parts_one = together([t1, t2, t3, *parts_one])
    parts_two = scatter_plane([t0, t1, t2, t3])
    cuts_one, bits = sum_cuts(parts_one), experts // 2
    far = far_cuts(cuts_one, bits)
    part = shape_of((span, width), BF)
    near_piece = shape_of((span // 2, width), BF)
    first_own, sent, upper, lower, near, in_grad, out_grad = run_kernel(
        norm_grad_body,
        sc,
        [dq, dk, dv, *grads, w_own, rows, active, hidden_grad, val_grad],
        [
            part,
            part,
            near_piece,
            near_piece,
            part,
            shape_of((width, hidden_units), F32),
            shape_of((hidden_units, width), F32),
        ],
        name="norm_one_grad",
        flops=10e9,
    )
    upper, lower = to_blk(upper, 1), to_blk(lower, 1)
    *parts_two, out_grad = together([*parts_two, out_grad])
    upper, lower, *parts_two = together([upper, lower, *parts_two])
    second = to_blk(total_of([near, jnp.concatenate([upper, lower], axis=0)]), 2)
    while bits:
        cuts_one = halve_experts(cuts_one, bits, far)
        bits //= 2
        if bits:
            far = far_cuts(cuts_one, bits)
        if bits == 1:
            far, *_ = together([far, *parts_two])
    whole_one = cuts_one[0]
    column_one = gather_experts(whole_one, [second])
    small = total_of([part[stride:] for part in parts_two])
    whole_two = sum_experts([jnp.concatenate([piece, small], axis=0) for piece in sum_cuts(parts_two)])
    whole_two, small = whole_two[:cut], whole_two[cut:]
    one = gather_plane(column_one)
    sent, small, column_two, *one = together([sent, small, gather_experts(whole_two), *one])
    two = gather_plane(column_two)
    packed = [*one, small, sent]
    packed_rows = sum(part.shape[0] for part in packed)
    (pack,) = run_kernel(pack_body, sc, packed, [shape_of((packed_rows, width), BF)], name="pack")
    output = run_kernel(
        output_body,
        sc,
        [own0, core_rows, a10, a11, x, w_proj, cols, back],
        [shape_of(x.shape, BF)],
        name="output",
        after=[pack],
    )[0]
    pack = to_blk(pack, 1)
    input_grad = run_kernel(
        functools.partial(input_body, packed_rows - span),
        sc,
        [x, g, cols, mid, first_own, pack, second, gain_one_row],
        [shape_of(x.shape, BF)],
        name="input_grad",
    )[0]
    attn_gain, moe_gain, router_grad = run_kernel(
        functools.partial(small_body, experts, 4 * stride),
        sc,
        [small, pack, gain_one_row],
        [shape_of((width,), F32), shape_of((width,), F32), shape_of((experts, width), F32)],
        name="small_grads",
    )

    def grid_kernel(body, steps, arrays, out, block, index, name):
        return pl.pallas_call(
            body,
            grid_spec=pltpu.PrefetchScalarGridSpec(
                num_scalar_prefetch=1,
                grid=(steps,),
                in_specs=[pl.BlockSpec(memory_space=pltpu.VMEM)] * len(arrays),
                out_specs=pl.BlockSpec(block, index),
            ),
            out_shape=out,
            compiler_params=pltpu.CompilerParams(vmem_limit_bytes=16 * 1024 * 1024),
            name=name,
        )(sc, *arrays)

    proj_grad = grid_kernel(
        functools.partial(spread_proj_body, cut),
        6,
        [*one, pack],
        shape_of((width, width), F32),
        (width, LANES),
        lambda i, s: (0, jnp.bitwise_xor(s[2], i // 3) * pairs + i % 3),
        "spread_proj",
    )
    two[3], output, input_grad, proj_grad, attn_gain = together([two[3], output, input_grad, proj_grad, attn_gain])
    peers = [to_blk(two[0], 1), None, None, to_blk(two[3], 1)]
    two[1], two[2], peers[0], peers[3] = together([two[1], two[2], peers[0], peers[3]])
    peers[1], peers[2] = to_blk(two[1], 1), to_blk(two[2], 1)
    qkv_grad = grid_kernel(
        functools.partial(spread_body, cut, group, pairs),
        4,
        [*one, pack, *two, *peers],
        shape_of((width, 3 * width), F32),
        (size, 3 * width),
        lambda i, s: (jnp.bitwise_xor(s[3], i), 0),
        "spread",
    )
    return (
        output,
        input_grad,
        attn_gain,
        qkv_grad,
        proj_grad,
        moe_gain,
        router_grad.T,
        in_grad[None],
        out_grad[None],
    )


def solution(mesh):
    rows, kept = P("batch", "blk", None), P()
    w_in, w_out = P("batch", None, "blk"), P("batch", "blk", None)
    return jax.shard_map(
        functools.partial(local, mesh.shape["blk"], mesh.shape["batch"]),
        mesh=mesh,
        in_specs=(rows, kept, kept, kept, kept, kept, w_in, w_out, P("batch", "blk"), kept, P("batch"), rows),
        out_specs=(rows, rows, kept, kept, kept, kept, kept, w_in, w_out),
        check_vma=False,
    )
```

```python
import functools
import math

import jax
import jax.numpy as jnp
from jax import lax
from jax.experimental import pallas as pl
from jax.experimental.pallas import tpu as pltpu
from jax.sharding import PartitionSpec as P

HEAD_DIM = 64
CAP = 12
SEAT = 16
LANES = 128
EPSILON = 1e-05
FAR_BELOW = -1e30
BF = jnp.bfloat16
F32 = jnp.float32


def dot(left, right):
    return jnp.dot(left, right, preferred_element_type=F32)


def dot_rows(left, right):
    return lax.dot_general(left, right, (((0,), (0,)), ((), ())), preferred_element_type=F32)


def dot_cols(left, right):
    return lax.dot_general(left, right, (((1,), (1,)), ((), ())), preferred_element_type=F32)


def norm_parts(rows):
    centred = rows - jnp.mean(rows, axis=-1, keepdims=True)
    scaling = lax.rsqrt(jnp.mean(centred * centred, axis=-1, keepdims=True) + EPSILON)
    return centred * scaling, scaling


def norm_pull(scaled, unit, scaling):
    return scaling * (
        scaled
        - jnp.mean(scaled, axis=-1, keepdims=True)
        - unit * jnp.mean(scaled * unit, axis=-1, keepdims=True)
    )


def run_kernel(body, scalars, operands, outs, scratch=(), flops=0, name=None, after=()):
    specs, arrays, held = [], [], 0
    after, given, run = list(after), len(operands), body
    if after:

        def run(sc, *refs):
            body(sc, *refs[:given], *refs[given + len(after) :])

    for operand in operands:
        if isinstance(operand, tuple):
            array, block, index = operand
            held += 2 * math.prod(block) * array.dtype.itemsize
            specs.append(pl.BlockSpec(block, functools.partial(lambda i, s, fn: fn(s), fn=index)))
        else:
            array = operand
            held += array.size * array.dtype.itemsize
            specs.append(pl.BlockSpec(memory_space=pltpu.VMEM))
        arrays.append(array)
    specs += [pl.BlockSpec(memory_space=pl.ANY)] * len(after)
    held += sum(out.size * out.dtype.itemsize for out in outs)
    out_specs = [pl.BlockSpec(memory_space=pltpu.VMEM) for _ in outs]
    return pl.pallas_call(
        run,
        grid_spec=pltpu.PrefetchScalarGridSpec(
            num_scalar_prefetch=1,
            grid=(1,),
            in_specs=specs,
            out_specs=out_specs,
            scratch_shapes=list(scratch),
        ),
        out_shape=list(outs),
        compiler_params=pltpu.CompilerParams(vmem_limit_bytes=(16 if held < 24e6 else 60) * 1024 * 1024),
        cost_estimate=pl.CostEstimate(flops=int(flops), bytes_accessed=0, transcendentals=0),
        name=name,
    )(scalars, *arrays, *after)


def together(values):
    return list(lax.optimization_barrier(tuple(values)))


def shape_of(dims, dtype):
    return jax.ShapeDtypeStruct(dims, dtype)


def half_masks(scale):
    lane = lax.broadcasted_iota(jnp.int32, (1, LANES), 1)
    low = lane < HEAD_DIM
    return lane, low, (jnp.where(low, scale, 0.0).astype(BF), jnp.where(low, 0.0, scale).astype(BF))


def one_hot(cols, count):
    seat = cols[:, :1].astype(F32) * SEAT + cols[:, 1:2].astype(F32)
    slot = lax.broadcasted_iota(jnp.int32, (cols.shape[0], count), 1).astype(F32)
    return jnp.where(slot == seat, 1.0, 0.0).astype(BF)


def one_hot_rows(block, span, count):
    table = block[span : span + 16, :span].astype(F32)
    seat = table[:1, :] * SEAT + table[1:2, :]
    slot = lax.broadcasted_iota(jnp.int32, (count, span), 0).astype(F32)
    return jnp.where(slot == seat, 1.0, 0.0).astype(BF)


def forward_body(
    sc, m0, m1, m2, m3, gain, weights, attn_in, qkv, mixed, stats, o0, o1, o2, o3, p0, p1, p2, p3, pieces
):
    powers = (p0, p1, p2, p3)
    span, group = m2.shape[0], weights.shape[1] // 3
    place = sc[0]
    for rel, block in enumerate((m0, m1, m2, m3)):
        start = pl.multiple_of(jnp.bitwise_xor(place, rel) * span, span)
        unit, _ = norm_parts(block[...].astype(F32))
        normed = (unit * gain[...]).astype(BF)
        attn_in[pl.ds(start, span), :] = normed
        qkv[pl.ds(start, span), :] = dot(normed, weights[...]).astype(BF)
    lane, low, scaled = half_masks(HEAD_DIM**-0.5)
    row = jnp.bitwise_and(lax.broadcasted_iota(jnp.int32, (2 * span, span), 0), span - 1)
    col = lax.broadcasted_iota(jnp.int32, (2 * span, span), 1)
    causal = col <= row
    for i in range(4):
        past = i * span
        upto = past + span
        stat = jnp.zeros((span, LANES), F32)
        for g in range(group // LANES):
            at = g * LANES
            queries = qkv[past:upto, at : at + LANES]
            keys = qkv[0:upto, group + at : group + at + LANES]
            values = qkv[0:upto, 2 * group + at : 2 * group + at + LANES]
            both = jnp.concatenate([queries * scaled[0], queries * scaled[1]], axis=0)
            last = jnp.where(causal, dot_cols(both, keys[past:]), FAR_BELOW)
            top = jnp.max(last, axis=-1, keepdims=True)
            if i:
                first = dot_cols(both, keys[:past])
                top = jnp.maximum(top, jnp.max(first, axis=-1, keepdims=True))
            beside = jnp.concatenate([values, jnp.ones_like(values)], axis=1)
            raised = jnp.exp(last - top).astype(BF)
            powers[i][g, :, past:] = raised
            mix = dot(raised, beside[past:])
            if i:
                raised = jnp.exp(first - top).astype(BF)
                powers[i][g, :, :past] = raised
                mix = mix + dot(raised, beside[:past])
            scale = 1.0 / mix[:, LANES:]
            mix = mix[:, :LANES] * scale
            mix = jnp.where(low, mix[:span], mix[span:])
            for u in range(2):
                stat = jnp.where(lane == 2 * g + u, scale[u * span : (u + 1) * span], stat)
            mixed[past:upto, at : at + LANES] = mix
            pieces[jnp.bitwise_xor(place, i), :, at : at + LANES] = mix.astype(BF)
        stats[past:upto, :] = stat
    for rel, out in enumerate((o0, o1, o2, o3)):
        out[...] = pieces[rel]


def pick_body(sc, o0, o1, o2, o3, b0, b1, b2, b3, k0, core, k2, k3):
    span, group = o0.shape
    for out, rows, base in ((k0, o0, b0), (core, o1, b1), (k2, o2, b2), (k3, o3, b3)):
        kept = dot(one_hot_rows(base, span, k0.shape[0]), rows[...]).astype(BF)
        if out is core:
            core[:span, :] = rows[...]
            core[span:, :] = kept
        else:
            out[...] = kept


def pair_backward(stats, pair, qkv, mixed, powers, dmix, dq, dk, dv, dk_sum, dv_sum):
    span, group, head = qkv.shape[0] // 4, qkv.shape[1] // 3, 2 * pair
    at = [slice(j * group + pair * LANES, j * group + (pair + 1) * LANES) for j in range(3)]
    scale = HEAD_DIM**-0.5
    _, low, ones = half_masks(1.0)
    _, _, scaled = half_masks(scale)
    for i in reversed(range(4)):
        past = i * span
        upto = past + span
        queries = qkv[past:upto, at[0]]
        keys = qkv[0:upto, at[1]]
        values = qkv[0:upto, at[2]]
        over = jnp.where(low, stats[past:upto, head : head + 1], stats[past:upto, head + 1 : head + 2])
        grads = (dmix[past:upto, :].astype(F32) * over).astype(BF)
        product = grads.astype(F32) * mixed[past:upto, at[0]]
        query = [queries * scaled[u] for u in range(2)]
        grad = [grads * ones[u] for u in range(2)]
        pulls = [dot_cols(grad[u], values) for u in range(2)]
        halves, sums = [], {}
        for u in range(2):
            delta = jnp.sum(jnp.where(low == (u == 0), product, 0.0), axis=-1, keepdims=True)
            half = None
            for rows in (slice(past, upto), slice(0, past))[: 2 if i else 1]:
                weights = powers[i][pair, u * span : (u + 1) * span, rows]
                score_grad = (weights.astype(F32) * (pulls[u][:, rows] - delta)).astype(BF)
                part = dot(score_grad, keys[rows])
                half = part if half is None else half + part
                for name, left, right in (("k", score_grad, query[u]), ("v", weights, grad[u])):
                    part = dot_rows(left, right)
                    sums[name, rows.start] = sums[name, rows.start] + part if u else part
            halves.append(half)
        for (name, start), part in sums.items():
            out = dk_sum if name == "k" else dv_sum
            rows = slice(start, upto if start == past else past)
            out[rows, :] = part if i == 3 else out[rows, :] + part
        dq[past:upto, :] = (jnp.where(low, halves[0], halves[1]) * scale).astype(BF)
    dk[...] = dk_sum[...].astype(BF)
    dv[...] = dv_sum[...].astype(BF)


def stage_rows(held, columns, value, stride):
    size = value.shape[0] // 4
    for k in range(4):
        held[k * stride : k * stride + size, columns] = value[k * size : (k + 1) * size, :]
        if stride > size:
            held[k * stride + size : (k + 1) * stride, columns] = jnp.zeros((stride - size, value.shape[1]), BF)


def place_cuts(cut, quarter, expert, held, outs, stride):
    for rel, out in enumerate(outs):
        first = jnp.bitwise_xor(quarter, rel) * stride
        for j in range(stride // cut):
            at = pl.multiple_of(first + jnp.bitwise_xor(expert, j) * cut, 16)
            out[j * cut : (j + 1) * cut, :] = held[pl.ds(at, cut), :]


def load_grads(place, pair, blocks, kept, dmix):
    span = dmix.shape[0] // 4
    at = slice(pair * LANES, (pair + 1) * LANES)
    for rel, block in enumerate(blocks):
        start = pl.multiple_of(jnp.bitwise_xor(place, rel) * span, span)
        late = dot_rows(one_hot_rows(block, span, kept[rel].shape[0]), kept[rel][:, at])
        dmix[pl.ds(start, span), :] = (block[:span, at].astype(F32) + late).astype(BF)


def weight_columns(attn_t, sources, weights, pair, held, first, stride):
    total, group = None, weights.shape[1] // 3
    grad = dot(attn_t[...], jnp.concatenate([source[...] for source in sources], axis=1))
    stage_rows(held, slice(first, first + 3 * LANES), grad.astype(BF), stride)
    for j in range(3):
        at = j * group + pair * LANES
        part = grad[:, j * LANES : (j + 1) * LANES] * weights[:, at : at + LANES].astype(F32)
        total = part if total is None else total + part
    return jnp.sum(total, axis=-1, keepdims=True)


def first_backward_body(cut, sc, *refs):
    base, late, powers, rest = refs[:4], refs[4:8], refs[8:12], refs[12:]
    qkv, mixed, attn_t, stats, weights, proj_own, proj_peer, attn_own, attn_peer, branch = rest[:10]
    dq, dk, dv, w0, w1, w2, w3, gain_sum, dmix, dk_sum, dv_sum, held = rest[10:]
    stride, group, core_late = w0.shape[0], proj_own.shape[1], late[1]
    load_grads(sc[0], 0, base, late, dmix)
    pair_backward(stats, 0, qkv, mixed, powers, dmix, dq, dk, dv, dk_sum, dv_sum)
    core = sc[2]
    to = pl.multiple_of(core * group, LANES)
    rows = branch[:, pl.ds(to, group)]
    rows_peer = core_late[:, pl.ds(pl.multiple_of(3 * group + to, LANES), group)]
    mine = dot_rows(attn_own[...], rows) + dot_rows(core_late[:, 2 * group : 3 * group], rows_peer)
    others = dot_rows(attn_peer[...], rows) + dot_rows(core_late[:, group : 2 * group], rows_peer)
    both = jnp.concatenate([jnp.where(core == 0, mine, others), jnp.where(core == 0, others, mine)], axis=0)
    both = (proj_own[...].astype(F32) + proj_peer[...].astype(F32) + both).astype(BF)
    stage_rows(held, slice(0, group), both, stride)
    sums = weight_columns(attn_t, (dq, dk, dv), weights, 0, held, group, stride)
    gain_sum[...] = jnp.broadcast_to(sums, gain_sum.shape)
    place_cuts(cut, sc[3], sc[4], held, (w0, w1, w2, w3), stride)


def second_backward_body(pairs, cut, sc, *refs):
    base, late, powers, rest = refs[:4], refs[4:8], refs[8:12], refs[12:]
    qkv, mixed, attn_t, stats, weights, gain_sum, moe_row, router_rows = rest[:8]
    grads, rest = rest[8 : 8 + 3 * (pairs - 1)], rest[8 + 3 * (pairs - 1) :]
    outs, (dmix, dk_sum, dv_sum, held) = rest[:4], rest[4:]
    extra = router_rows.shape[0]
    stride = outs[0].shape[0] - extra
    sums = gain_sum[:, :1]
    for n in range(pairs - 1):
        own = grads[3 * n : 3 * n + 3]
        load_grads(sc[0], n + 1, base, late, dmix)
        pair_backward(stats, n + 1, qkv, mixed, powers, dmix, *own, dk_sum, dv_sum)
        sums = sums + weight_columns(attn_t, own, weights, n + 1, held, 3 * LANES * n, stride)
    place_cuts(cut, sc[3], sc[4], held, outs, stride)
    row = lax.broadcasted_iota(jnp.int32, router_rows.shape, 0)
    gain_row = jnp.transpose(jnp.broadcast_to(sums, gain_sum.shape))[:1, :]
    small = jnp.where(row == 0, gain_row, jnp.where(row == 1, moe_row[...], router_rows[...])).astype(BF)
    for out in outs:
        out[stride:, :] = small


def norm_grad_body(sc, *refs):
    grads, (weights, *halves), outs = refs[:-16], refs[-16:-7], refs[-7:]
    own, sent, upper, lower, kept, in_grad, out_grad = outs
    span = own.shape[0]
    halves = halves[:4], halves[4:]
    in_grad[...] = sum(dot_rows(rows_in[...], hidden_grad[...]) for rows_in, _, hidden_grad, _ in halves)
    out_grad[...] = sum(dot_rows(active[...], val_grad[...]) for _, active, _, val_grad in halves)
    for j in range(4):
        rows = pl.ds(pl.multiple_of(jnp.bitwise_xor(sc[0], j) * span, span), span)
        cols = [grads[n][rows, :] for part in range(3) for n in range(part, len(grads), 3)]
        grad = dot_cols(jnp.concatenate(cols, axis=1), weights[...]).astype(BF)
        if j == 3:
            upper[...] = grad[: span // 2]
            lower[...] = grad[span // 2 :]
        else:
            (own, sent, kept)[j][...] = grad


def proj_rows(sc, w_proj, group):
    return [
        w_proj[pl.ds(pl.multiple_of(jnp.bitwise_xor(sc[2], flip) * group, 16), group), :] for flip in range(2)
    ]


def prepare_body(
    sc, x, grads, routes, w_proj, wq, wk, wv, x_kept, tail, b00, b01, b10, b11, w_own, cols
):
    seqs, span, width = x.shape
    group, count = wq.shape[1], x_kept.shape[0]
    experts = count // SEAT
    for j, weight in enumerate((wq, wk, wv)):
        w_own[:, j * group : (j + 1) * group] = weight[...]
    proj_own, proj_peer = proj_rows(sc, w_proj, group)
    earlier = lax.broadcasted_iota(jnp.int32, (span, span), 0) < lax.broadcasted_iota(jnp.int32, (span, span), 1)
    earlier = jnp.where(earlier, 1.0, 0.0).astype(BF)
    ids = lax.broadcasted_iota(jnp.int32, (max(8, experts), span), 0)
    slots = lax.broadcasted_iota(jnp.int32, (count, span), 0)
    rows_of = lax.broadcasted_iota(jnp.int32, (LANES, span), 0)
    seen = jnp.zeros((max(8, experts), 1), F32)
    x_sum, tail_sum, flag_sum, tables = None, None, None, []
    for n in range(seqs):
        route = routes[n : n + 1, :]
        mine = jnp.where(ids == route, 1.0, 0.0)
        before = dot(mine.astype(BF), earlier) + seen
        rank = jnp.sum(mine * before, axis=0, keepdims=True)
        seen = seen + jnp.sum(mine, axis=1, keepdims=True)
        limit = jnp.zeros((1, span), jnp.int32)
        for e in range(experts):
            limit = jnp.where(route == e, sc[7 + e], limit)
        kept = rank < limit.astype(F32)
        place = jnp.bitwise_xor(route, sc[4])
        seat = jnp.where(kept, place * SEAT + rank.astype(jnp.int32), -1)
        pick = jnp.where(slots == seat, 1.0, 0.0).astype(BF)
        live = jnp.where(sc[5 + n] == 1, F32(1.0), F32(0.0))
        table = jnp.where(rows_of == 0, jnp.where(kept, place.astype(F32), -1.0), 0.0)
        table = jnp.where(rows_of == 1, jnp.where(kept, rank, 0.0), table)
        table = jnp.where(rows_of == 2, live, table)
        table = jnp.where(rows_of == 3, jnp.where(kept, 0.0, 1.0), table)
        tables.append(table[:16, :].astype(BF))
        columns = jnp.transpose(table).astype(BF)
        cols[n] = columns
        parts = dot(pick, x[n]), dot(pick, grads[n]), dot(pick, columns)
        x_sum = parts[0] if n == 0 else x_sum + parts[0]
        tail_sum = parts[1] if n == 0 else tail_sum + parts[1]
        flag_sum = parts[2] if n == 0 else flag_sum + parts[2]
    x_kept[...] = x_sum.astype(BF)
    tail[:, :width] = tail_sum.astype(BF)
    tail[:, width:] = flag_sum.astype(BF)
    for rel, (own, peer) in enumerate(((b00, b01), (b10, b11))):
        at = jnp.bitwise_xor(sc[1], rel)
        own_cols = cols[at]
        rows = grads[at] * own_cols[:, 3:4]
        for out, weight in ((own, proj_own), (peer, proj_peer)):
            out[:span, :] = dot_cols(rows, weight).astype(BF)
            out[span:, :span] = jnp.where(at == 0, tables[0], tables[1])
            if group > span:
                out[span:, span:] = jnp.zeros((out.shape[0] - span, group - span), BF)


def project_body(sc, k00, k01, k10, k11, x_kept, tail, w_proj, gain, after, own, peer, *boxes):
    own[...] = k00[...] + k10[...]
    peer[...] = k01[...] + k11[...]
    w_own, w_peer = proj_rows(sc, w_proj, own.shape[1])
    rows = x_kept[...].astype(F32) + (dot(own[...], w_own) + dot(peer[...], w_peer))
    after[...] = rows
    unit, _ = norm_parts(rows)
    moe_in = (unit * gain[...]).astype(BF)
    width = moe_in.shape[1]
    for j, box in enumerate(boxes):
        at = slice(j * SEAT, (j + 1) * SEAT)
        box[:, :width] = moe_in[at, :]
        box[:, width:] = tail[at, :]


def expert_body(sc, *refs):
    row_refs = refs[:4]
    router, w_in, w_out = refs[4:7]
    out, rows, active, hidden_grad, val_grad, logit_grad = refs[7:]
    piece, width = row_refs[0].shape[0], rows.shape[1]
    expert = sc[4]
    for k, ref in enumerate(row_refs):
        rows[k * piece : (k + 1) * piece, :] = ref[:, :width]
    column = router[pl.ds(expert, 1), :]
    per = max(1, min(4, 512 // piece))
    for first in range(0, 4, per):
        here = slice(first * piece, (first + per) * piece)
        moe_in = rows[here, :]
        grads = jnp.concatenate([row_refs[k][:, width:] for k in range(first, first + per)], axis=0)
        live = grads[:, width + 2 : width + 3].astype(F32)
        grads = grads[:, :width].astype(F32)
        logit = jnp.sum(moe_in.astype(F32) * column, axis=-1, keepdims=True)
        gate = 1.0 / (1.0 + jnp.exp(-logit))
        value_grad = (gate * grads).astype(BF)
        hidden = dot(moe_in, w_in[...])
        bent = 0.5 * (1.0 + lax.erf(hidden * (0.5**0.5)))
        act = (hidden * bent).astype(BF)
        slope = bent + hidden * jnp.exp(-0.5 * hidden * hidden) * ((2.0 * jnp.pi) ** -0.5)
        pulled = (slope * dot_cols(value_grad, w_out[...])).astype(BF)
        part = dot(act, w_out[...])
        logit_part = jnp.sum(part * grads, axis=-1, keepdims=True) * (gate * (1.0 - gate) * live)
        out[here, :width] = (dot_cols(pulled, w_in[...]) + logit_part * column).astype(BF)
        out[here, width:] = (gate * part).astype(BF)
        active[here, :] = act
        hidden_grad[here, :] = pulled
        val_grad[here, :] = value_grad
        lane = lax.broadcasted_iota(jnp.int32, (logit_part.shape[0], LANES), 1)
        logit_grad[here, :] = jnp.where(lane == expert + 2, logit_part, 0.0).astype(BF)


def return_body(sc, back, after, tail, attn_own, attn_peer, gain, w_proj, mid, branch, gain_row, own, far, core):
    width = after.shape[1]
    upstream = back[:, :width].astype(F32)
    unit, scaling = norm_parts(after[...])
    gain_row[...] = jnp.sum(upstream * unit, axis=0, keepdims=True)
    total = tail[:, :width].astype(F32) + norm_pull(upstream * gain[...], unit, scaling)
    mid[...] = total
    low = total.astype(BF)
    branch[...] = low
    group = own.shape[1]
    w_own, w_peer = proj_rows(sc, w_proj, group)
    own[...] = dot_cols(low, w_own).astype(BF)
    pulled = dot_cols(low, w_peer).astype(BF)
    far[...] = pulled
    core[:, :group] = pulled
    core[:, group : 2 * group] = attn_own[...]
    core[:, 2 * group : 3 * group] = attn_peer[...]
    core[:, 3 * group :] = low


def projection_grad_body(
    sc, a00, a01, a10, a11, grads, cols, rows0, rows1, logit0, logit1, attn_in, own, peer, router_rows, attn_t, rows
):
    attn_t[...] = jnp.transpose(attn_in[...])
    router = dot_rows(logit0[...], rows0[...]) + dot_rows(logit1[...], rows1[...])
    router_rows[...] = router[: router_rows.shape[0], :]
    span, group = a00.shape
    core = sc[2]
    for rel in range(2):
        at = jnp.bitwise_xor(sc[1], rel)
        rows[rel] = grads[at] * cols[at][:, 3:4]
    for half, out in enumerate((own, peer)):
        to = pl.ds(pl.multiple_of(jnp.bitwise_xor(core, half) * group, LANES), group)
        cut0, cut1 = rows[0, :, to], rows[1, :, to]
        for kind, (first, second) in enumerate(((a00, a10), (a01, a11))):
            at = pl.multiple_of(jnp.bitwise_xor(core, kind) * group, 16)
            total = dot_rows(first[:span, :], cut0) + dot_rows(second[...], cut1)
            out[pl.ds(at, group), :] = total.astype(BF)


def place_column(sc, cut, stride, parts, column, out):
    size = out.shape[0] // 4
    for rel, (part, offset) in enumerate(parts):
        first = jnp.bitwise_xor(sc[3], rel) * size
        for j in range(stride // cut):
            place = jnp.bitwise_xor(sc[4], j) * cut
            value = part[offset + j * cut : offset + (j + 1) * cut, pl.ds(column, LANES)].astype(F32)

            def store(place=place, value=value, first=first):
                out[pl.ds(pl.multiple_of(first + place, 16), cut), :] = value

            if stride > size:
                pl.when(place < size)(store)
            else:
                store()


def spread_proj_body(cut, sc, *refs):
    own, peer, out = refs[:4], refs[4], refs[5]
    step = pl.program_id(0)
    stride = own[0].shape[0]
    parts = [(ref, 0) for ref in own] + [(peer, rel * stride) for rel in range(4)]

    def write(side):
        place_column(sc, cut, stride, parts[4 * side : 4 * side + 4], pl.multiple_of(step % 3 * LANES, LANES), out)

    for side in range(2):
        pl.when(step // 3 == side)(functools.partial(write, side))


def spread_body(cut, group, pairs, sc, *refs):
    own, peer, second, out = refs[:4], refs[4], refs[5:13], refs[13]
    core, expert = sc[2], sc[4]
    size = out.shape[0]
    stride = own[0].shape[0]

    def write(rel):
        for half in range(2):
            side = jnp.bitwise_xor(core, half) * group
            first, offset = (peer, rel * stride) if half else (own[rel], 0)
            rest = second[4 * half + rel]
            for j in range(stride // cut):
                place = jnp.bitwise_xor(expert, j) * cut

                def store(place=place, j=j, side=side, first=first, offset=offset, rest=rest):
                    rows = pl.ds(pl.multiple_of(place, 16), cut)
                    for pair in range(pairs):
                        ref, start = (rest, j * cut) if pair else (first, offset + j * cut)
                        base = 3 * LANES * (pair - 1) if pair else group
                        for part in range(3):
                            at = base + part * LANES
                            to = pl.multiple_of(side + pair * LANES + 2 * part * group, LANES)
                            out[rows, pl.ds(to, LANES)] = ref[start : start + cut, at : at + LANES].astype(F32)

                if stride > size:
                    pl.when(place < size)(store)
                else:
                    store()

    for rel in range(4):
        pl.when(pl.program_id(0) == rel)(functools.partial(write, rel))


def small_body(experts, first, sc, own, peer, gain, attn_gain, moe_gain, router):
    rows = own[...].astype(F32) + peer[first : first + own.shape[0], :].astype(F32)
    attn_gain[...] = (rows[:1, :] / gain[...])[0]
    moe_gain[...] = rows[1]
    router[...] = rows[2 : 2 + experts, :]


def input_body(first, sc, x, grads, cols, mid, first_own, peer, second, gain, out):
    high = mid[...].astype(BF)
    rest = (mid[...] - high.astype(F32)).astype(BF)
    for rel in range(2):
        if rel == 0:
            upstream = first_own[...].astype(F32) + peer[first : first + first_own.shape[0], :].astype(F32)
        else:
            upstream = second[...].astype(F32)
        at = jnp.bitwise_xor(sc[1], rel)
        own_cols = cols[at]
        pick = one_hot(own_cols, mid.shape[0])
        total = (grads[at] * own_cols[:, 3:4]).astype(F32) + (dot(pick, high) + dot(pick, rest))
        unit, scaling = norm_parts(x[at].astype(F32))
        out[at] = (total + norm_pull(upstream * gain[...], unit, scaling)).astype(BF)


def pack_body(sc, *refs):
    at = 0
    for part in refs[:-1]:
        refs[-1][at : at + part.shape[0], :] = part[...]
        at += part.shape[0]


def output_body(sc, a00, a01, a10, a11, x, w_proj, cols, values, out):
    span, width = x.shape[1:]
    w_own, w_peer = proj_rows(sc, w_proj, a00.shape[1])
    for rel, (own, peer) in enumerate(((a00, a01), (a10, a11))):
        at = jnp.bitwise_xor(sc[1], rel)
        rows = x[at].astype(F32) + (dot(own[:span, :], w_own) + dot(peer[:span, :], w_peer))
        pick = one_hot(cols[at], values.shape[0])
        out[at] = (rows + dot(pick, values[:, width:])).astype(BF)


def local(
    blk_count,
    batch_count,
    x,
    gain_one,
    w_qkv,
    w_proj,
    gain_two,
    router,
    w_in,
    w_out,
    routes,
    quota,
    period,
    g,
):
    seq_count, span, width = x.shape
    group = width // 2
    experts = quota.shape[0]
    share = batch_count // experts
    assert blk_count == 4 and seq_count == 2 and share == 2
    blk, batch = lax.axis_index("blk"), lax.axis_index("batch")
    chip, core = blk // 2, blk % 2
    expert, half = batch // share, batch % share
    quarter = chip * 2 + half
    sc = jnp.concatenate([jnp.stack([blk, chip, core, quarter, expert]).astype(jnp.int32), period, quota])

    def to_blk(value, bits):
        return lax.ppermute(value, "blk", [(i, i ^ bits) for i in range(4)])

    def to_batch(value, bits):
        return lax.ppermute(value, "batch", [(i, i ^ bits) for i in range(batch_count)])

    def to_expert(value, bits):
        return to_batch(value, bits * share)

    def to_plane(value, rel):
        if rel == 1:
            return to_batch(value, 1)
        if rel == 2:
            return to_blk(value, 2)
        pairs = [
            (i * batch_count + j, (i ^ 2) * batch_count + (j ^ 1)) for i in range(4) for j in range(batch_count)
        ]
        return lax.ppermute(value, ("blk", "batch"), pairs)

    def third(j):
        return (w_qkv, (width, group), lambda s: (0, 2 * j + s[2]))

    mine = lax.dynamic_index_in_dim(x, chip, 0, keepdims=False)
    other = lax.dynamic_index_in_dim(x, 1 - chip, 0, keepdims=False)
    block_x = to_blk(other, 2)
    block_c = to_blk(mine, 1)

    gain_one_row, gain_two_row = gain_one.reshape(1, width), gain_two.reshape(1, width)

    seat_rows = experts * SEAT
    length = 4 * span
    piece = shape_of((span, group), BF)
    base_piece = shape_of((span + 16, group), BF)
    kept_piece = shape_of((seat_rows, group), BF)
    kept_rows = shape_of((seat_rows, width), BF)
    x_kept, tail, b00, b01, b10, b11, w_own, cols = run_kernel(
        prepare_body,
        sc,
        [x, g, routes, w_proj, third(0), third(1), third(2)],
        [
            kept_rows,
            shape_of((seat_rows, width + LANES), BF),
            base_piece,
            base_piece,
            base_piece,
            base_piece,
            shape_of((width, 3 * group), BF),
            shape_of((seq_count, span, LANES), BF),
        ],
        name="prepare",
    )
    block_x, b01, b10, b11 = together([block_x, b01, b10, b11])
    base = [b00, to_blk(b01, 1), to_blk(b10, 2), to_blk(b11, 3)]
    block_xc = to_blk(block_x, 1)
    pairs = group // LANES
    attn_in, qkv, mixed, stats, own0, own1, own2, own3, *powers = run_kernel(
        forward_body,
        sc,
        [mine, block_c, block_x, block_xc, gain_one_row, w_own],
        [
            shape_of((length, width), BF),
            shape_of((length, 3 * group), BF),
            shape_of((length, group), F32),
            shape_of((length, LANES), F32),
            piece,
            piece,
            piece,
            piece,
        ]
        + [shape_of((pairs, 2 * span, (i + 1) * span), BF) for i in range(4)],
        [pltpu.VMEM((4, span, group), BF)],
        name="attention_forward",
    )
    kept0, core_rows, kept2, kept3 = run_kernel(
        pick_body,
        sc,
        [own0, own1, own2, own3, *base],
        [kept_piece, shape_of((span + seat_rows, group), BF), kept_piece, kept_piece],
        name="pick_kept",
    )
    core_rows = to_blk(core_rows, 1)
    late = [kept0, core_rows, to_blk(kept2, 2), to_blk(kept3, 3)]
    own2, own3, *late = together([own2, own3, *late])
    core_rows = late[1]
    a10, a11 = to_blk(own2, 2), to_blk(own3, 3)
    row_box = shape_of((SEAT, 2 * width + LANES), BF)
    after_kept, attn_own, attn_peer, *boxes = run_kernel(
        project_body,
        sc,
        [
            kept0,
            (core_rows, (seat_rows, group), lambda s: (span // seat_rows, 0)) if span % seat_rows == 0 else core_rows[span:],
            *late[2:],
            x_kept,
            tail,
            w_proj,
            gain_two_row,
        ],
        [shape_of((seat_rows, width), F32), kept_piece, kept_piece] + [row_box] * experts,
        name="project",
    )

    order = [0, *reversed(range(1, experts))]
    parts = [to_expert(boxes[j], j) if j else boxes[0] for j in order]
    rows = jnp.concatenate(together([*parts, a10, a11])[:experts], axis=0)
    expert_rows = [rows] + [to_plane(rows, rel) for rel in (1, 2, 3)]
    expert_rows += [to_blk(part, 1) for part in expert_rows]
    hidden_units = w_in.shape[2]
    quad = shape_of((4 * seat_rows, 2 * width), BF)
    half_rows = 4 * seat_rows

    def expert_half(rows, name):
        return run_kernel(
            expert_body,
            sc,
            [*rows, router.T.astype(F32), w_in[0], w_out[0]],
            [
                quad,
                shape_of((half_rows, width), BF),
                shape_of((half_rows, hidden_units), BF),
                shape_of((half_rows, hidden_units), BF),
                shape_of((half_rows, width), BF),
                shape_of((half_rows, LANES), BF),
            ],
            name=name,
        )

    back_own, *own_half = expert_half(expert_rows[:4], "expert_own")
    expert_rows[4], back_own = together([expert_rows[4], back_own])
    back_peer, *peer_half = expert_half(expert_rows[4:], "expert_peer")

    def total_of(parts):
        parts = [part.astype(F32) for part in parts]
        while len(parts) > 1:
            parts = [left + right for left, right in zip(parts[::2], parts[1::2])]
        return parts[0].astype(BF)

    arrived = to_blk(back_peer, 1)
    parts = []
    for rel in range(4):
        at = slice(rel * seat_rows, (rel + 1) * seat_rows)
        part = total_of([back_own[at], arrived[at]])
        parts.append(part if rel == 0 else to_plane(part, rel))
    parts = together(parts)
    cuts = [total_of([part[n * SEAT : (n + 1) * SEAT] for part in parts]) for n in range(experts)]
    cuts = [cuts[order.index(j)] for j in range(experts)]
    back = jnp.concatenate(together([cuts[0]] + [to_expert(cuts[j], j) for j in range(1, experts)]), axis=0)

    extra = -(-(experts + 2) // 16) * 16
    proj_own, proj_peer, router_rows, attn_t = run_kernel(
        projection_grad_body,
        sc,
        [own0, core_rows, a10, a11, g, cols, own_half[0], peer_half[0], own_half[4], peer_half[4], attn_in],
        [shape_of((width, group), BF)] * 2 + [shape_of((extra, width), F32), shape_of((width, length), BF)],
        [pltpu.VMEM((seq_count, span, width), BF)],
        name="projection_grad",
        after=[back_own],
    )
    proj_arrived = to_blk(proj_peer, 1)
    wide_cols = shape_of((width, LANES), F32)
    mid, branch, moe_row, m_own, m_far, m_core = run_kernel(
        return_body,
        sc,
        [back, after_kept, tail, attn_own, attn_peer, gain_two_row, w_proj],
        [
            shape_of((seat_rows, width), F32),
            kept_rows,
            shape_of((1, width), F32),
            kept_piece,
            kept_piece,
            shape_of((seat_rows, 3 * group + width), BF),
        ],
        name="return_rows",
        after=[router_rows, proj_arrived],
    )
    mix_late = [m_own, to_blk(m_core, 1), to_blk(m_own, 2), to_blk(m_far, 3)]

    size = width // 4
    cut = -(-size // (experts * 16)) * 16
    stride = experts * cut

    def scatter_plane(quarters):
        sent = [to_plane(quarters[rel], rel) for rel in (3, 2, 1)]
        return [quarters[0], *sent[::-1]]

    def sum_cuts(parts):
        return [total_of([part[j * cut : (j + 1) * cut] for part in parts]) for j in range(experts)]

    def sum_experts(cuts):
        return total_of(together([cuts[0]] + [to_expert(cuts[j], j) for j in range(1, experts)]))

    def halve_experts(cuts, bits, far):
        return [total_of([near, far[j * cut : (j + 1) * cut]]) for j, near in enumerate(cuts[:bits])]

    def far_cuts(cuts, bits):
        return to_expert(jnp.concatenate(cuts[bits:], axis=0), bits)

    def gather_experts(whole, before=()):
        parts = [whole] + [to_expert(whole, j) for j in range(1, experts)]
        return jnp.concatenate(together([*parts, *before])[:experts], axis=0)

    def gather_plane(column):
        return [column] + [to_plane(column, rel) for rel in (1, 2, 3)]


    tall = shape_of((length, LANES), BF)
    working = [
        pltpu.VMEM((length, LANES), BF),
        pltpu.VMEM((length, LANES), F32),
        pltpu.VMEM((length, LANES), F32),
    ]
    wide_one = group + 3 * LANES
    wide_two = 3 * LANES * (pairs - 1)
    operands = [*base, *mix_late, *powers, qkv, mixed, attn_t, stats, w_own]
    dq, dk, dv, *quarters_one, gain_sum = run_kernel(
        functools.partial(first_backward_body, cut),
        sc,
        [*operands, proj_own, proj_arrived, attn_own, attn_peer, branch],
        [tall, tall, tall] + [shape_of((stride, wide_one), BF)] * 4 + [wide_cols],
        working + [pltpu.VMEM((4 * stride, wide_one), BF)],
        name="attention_backward_one",
    )
    parts_one = scatter_plane(quarters_one)
    *grads, t0, t1, t2, t3 = run_kernel(
        functools.partial(second_backward_body, pairs, cut),
        sc,
        [*operands, gain_sum, moe_row, router_rows],
        [tall] * (3 * (pairs - 1)) + [shape_of((stride + extra, wide_two), BF)] * 4,
        working + [pltpu.VMEM((4 * stride, wide_two), BF)],
        name="attention_backward_two",
    )
    t1, t2, t3, *parts_one = together([t1, t2, t3, *parts_one])
    parts_two = scatter_plane([t0, t1, t2, t3])
    cuts_one, bits = sum_cuts(parts_one), experts // 2
    far = far_cuts(cuts_one, bits)
    part = shape_of((span, width), BF)
    near_piece = shape_of((span // 2, width), BF)
    first_own, sent, upper, lower, near, in_grad, out_grad = run_kernel(
        norm_grad_body,
        sc,
        [dq, dk, dv, *grads, w_own, *own_half[:4], *peer_half[:4]],
        [
            part,
            part,
            near_piece,
            near_piece,
            part,
            shape_of((width, hidden_units), F32),
            shape_of((hidden_units, width), F32),
        ],
        name="norm_one_grad",
        flops=10e9,
    )
    upper, lower = to_blk(upper, 1), to_blk(lower, 1)
    *parts_two, out_grad = together([*parts_two, out_grad])
    upper, lower, *parts_two = together([upper, lower, *parts_two])
    second = to_blk(total_of([near, jnp.concatenate([upper, lower], axis=0)]), 2)
    while bits:
        cuts_one = halve_experts(cuts_one, bits, far)
        bits //= 2
        if bits:
            far = far_cuts(cuts_one, bits)
        if bits == 1:
            far, *_ = together([far, *parts_two])
    whole_one = cuts_one[0]
    column_one = gather_experts(whole_one, [second])
    small = total_of([part[stride:] for part in parts_two])
    whole_two = sum_experts([jnp.concatenate([piece, small], axis=0) for piece in sum_cuts(parts_two)])
    whole_two, small = whole_two[:cut], whole_two[cut:]
    one = gather_plane(column_one)
    sent, small, column_two, *one = together([sent, small, gather_experts(whole_two), *one])
    two = gather_plane(column_two)
    packed = [*one, small, sent]
    packed_rows = sum(part.shape[0] for part in packed)
    (pack,) = run_kernel(pack_body, sc, packed, [shape_of((packed_rows, width), BF)], name="pack")
    output = run_kernel(
        output_body,
        sc,
        [own0, core_rows, a10, a11, x, w_proj, cols, back],
        [shape_of(x.shape, BF)],
        name="output",
        after=[pack],
    )[0]
    pack = to_blk(pack, 1)
    input_grad = run_kernel(
        functools.partial(input_body, packed_rows - span),
        sc,
        [x, g, cols, mid, first_own, pack, second, gain_one_row],
        [shape_of(x.shape, BF)],
        name="input_grad",
    )[0]
    attn_gain, moe_gain, router_grad = run_kernel(
        functools.partial(small_body, experts, 4 * stride),
        sc,
        [small, pack, gain_one_row],
        [shape_of((width,), F32), shape_of((width,), F32), shape_of((experts, width), F32)],
        name="small_grads",
    )

    def grid_kernel(body, steps, arrays, out, block, index, name):
        return pl.pallas_call(
            body,
            grid_spec=pltpu.PrefetchScalarGridSpec(
                num_scalar_prefetch=1,
                grid=(steps,),
                in_specs=[pl.BlockSpec(memory_space=pltpu.VMEM)] * len(arrays),
                out_specs=pl.BlockSpec(block, index),
            ),
            out_shape=out,
            compiler_params=pltpu.CompilerParams(vmem_limit_bytes=16 * 1024 * 1024),
            name=name,
        )(sc, *arrays)

    proj_grad = grid_kernel(
        functools.partial(spread_proj_body, cut),
        6,
        [*one, pack],
        shape_of((width, width), F32),
        (width, LANES),
        lambda i, s: (0, jnp.bitwise_xor(s[2], i // 3) * pairs + i % 3),
        "spread_proj",
    )
    two[3], output, input_grad, proj_grad, attn_gain = together([two[3], output, input_grad, proj_grad, attn_gain])
    peers = [to_blk(two[0], 1), None, None, to_blk(two[3], 1)]
    two[1], two[2], peers[0], peers[3] = together([two[1], two[2], peers[0], peers[3]])
    peers[1], peers[2] = to_blk(two[1], 1), to_blk(two[2], 1)
    qkv_grad = grid_kernel(
        functools.partial(spread_body, cut, group, pairs),
        4,
        [*one, pack, *two, *peers],
        shape_of((width, 3 * width), F32),
        (size, 3 * width),
        lambda i, s: (jnp.bitwise_xor(s[3], i), 0),
        "spread",
    )
    return (
        output,
        input_grad,
        attn_gain,
        qkv_grad,
        proj_grad,
        moe_gain,
        router_grad.T,
        in_grad[None],
        out_grad[None],
    )


def solution(mesh):
    rows, kept = P("batch", "blk", None), P()
    w_in, w_out = P("batch", None, "blk"), P("batch", "blk", None)
    return jax.shard_map(
        functools.partial(local, mesh.shape["blk"], mesh.shape["batch"]),
        mesh=mesh,
        in_specs=(rows, kept, kept, kept, kept, kept, w_in, w_out, P("batch", "blk"), kept, P("batch"), rows),
        out_specs=(rows, rows, kept, kept, kept, kept, kept, w_in, w_out),
        check_vma=False,
    )
```
